256 devices in a mesh: dp: 32 (over y, x, core), replica: 8 (over z).
Axes of the slice: x: 4, y: 4, z: 8, core: 2. Of those that a mesh axis runs over, the one named last changes fastest.
Arguments:
- grads: bfloat16 [1024, 256, 256], P('dp'), may hold values from -6 to 6
- owner: int32 [1024, 1], replicated, may hold values from 0 to 31; in each aligned block of 32 rows (0 to 31, 32 to 63, ...) at most 2 rows name the same one
- left_root: bfloat16 [32, 64, 256, 256], P('dp', None, 'replica'), may hold values from -0.375 to 0.375
- right_root: bfloat16 [32, 64, 256, 256], P('dp'), may hold values from -0.375 to 0.375
- first_moment: float32 [32, 64, 256, 256], P('dp', None, 'replica'), may hold values from -6 to 6
- second_moment: float32 [32, 64, 256, 256], P('dp', None, 'replica'), may hold values from 0.01 to 1
Outputs:
- update: bfloat16 [32, 64, 256, 256], P('dp')
The draws below stay inside these ranges and needn't reach their ends.
Inputs may be any that keep to these rules, and one draw needn't show every extreme that they name: Among the 32 blocks of one flat shard (blocks s * 32 to s * 32 + 31) at most 2 name the same owner; some owner receives exactly 2 from some shard.
All inputs are finite; a program needn't handle non-finite values.
Results may differ from the reference program's by a relative error of at most 0.005.
Values may be sent and summed in bfloat16 or wider, within the bound.
A program may use at most 128 MiB of HBM per device.

```python
import math
import jax
import jax.numpy as jnp
import numpy as np
from jax import lax

ORDER = 256
BPD = 32
SLOT = 2
RS = 64
NB = 1024
N_DP = 32


def shard_levels(key, dims, split, least, high):
    factor_of, own = 1.0, jax.random.fold_in(key, 6)
    for position, parts in split:
        heights = jnp.exp(jax.random.uniform(jax.random.fold_in(own, position), (parts,), jnp.float32, least / len(split), high / len(split)))
        factor_of = factor_of * jnp.repeat(heights, dims[position] // parts).reshape([-1 if axis == position else 1 for axis in range(len(dims))])
    return factor_of


def assign_block(own_key, own, number, rows, amount, top, reach, slope):
    order = jax.random.permutation(own_key, amount)
    crowded, ordinary = load_shares(amount, rows * top, reach, slope, True), load_shares(amount, rows * top, reach, slope, False)
    places = jnp.arange(amount)

    def named(sizes, offset_by):
        used = int((sizes > 0).sum())
        fixed = max(1, used // 4)
        passed = fixed + (places - fixed + offset_by * (used - fixed)) % max(1, amount - fixed)
        return jnp.zeros((amount,), jnp.int32).at[order[jnp.where(places < fixed, places, passed)]].set(jnp.asarray(sizes, jnp.int32))

    sizes = jnp.where(number % 4 == 0, named(crowded, number // 4), named(ordinary, number - number // 4 - 1))
    mixed = jax.random.permutation(jax.random.fold_in(own, 3), amount)
    donor, sink = mixed[0:amount // 2 * 2:2], mixed[1:amount // 2 * 2:2]
    margin = jnp.minimum(sizes[donor] - 1, reach - sizes[sink]) // 2
    margin = jnp.where((donor == order[0]) | (sink == order[0]) | (sizes[sink] == 0), 0, jnp.maximum(margin, 0))
    passed = jax.random.randint(jax.random.fold_in(own, 4), (amount // 2,), 0, 1 << 20) % (margin + 1)
    sizes = sizes.at[donor].add(-passed).at[sink].add(passed)
    items = jnp.searchsorted(jnp.cumsum(sizes), jnp.arange(rows * top), side="right").astype(jnp.int32)
    listing = items.reshape(top, rows).T
    listing = listing[jax.random.permutation(jax.random.fold_in(own, 1), rows)]
    offset_by = jax.random.randint(jax.random.fold_in(own, 2), (rows, 1), 0, top)
    return jnp.take_along_axis(listing, (jnp.arange(top)[None, :] + offset_by) % top, axis=1)


def load_shares(amount, total, limit, lean, full):
    portions = [(1 << 20) // math.isqrt(grade ** lean) + 1 for grade in range(1, amount + 1)]
    largest = limit if full else min(limit, max(-(-total // amount), total * portions[0] // sum(portions)))
    least = 1 if total - largest >= amount - 1 else 0
    holding, spare = [largest] + [least] * (amount - 1), total - largest - least * (amount - 1)
    while spare > 0:
        free = [i for i in range(1, amount) if holding[i] < largest] or [i for i in range(1, amount) if holding[i] < limit]
        mass, remaining = sum([portions[i] for i in free]), spare
        for i in free:
            addition = min(limit - holding[i], max(1, remaining * portions[i] // mass), spare)
            holding[i] = holding[i] + addition
            spare = spare - addition
    return np.array(holding)


def scatter_about(stream_key, extent, spread, limit, pieces=(), kind=jnp.bfloat16):
    loudness = shard_levels(stream_key, extent, pieces, -0.22, 0.18) if pieces else 1.0
    drawn = jax.random.normal(stream_key, extent, jnp.float32) * spread * loudness
    return jnp.minimum(jnp.maximum(drawn, -limit), limit).astype(kind)


def setup_inputs(seed: int = 0) -> dict:
    key_of = jax.random.split(jax.random.key(seed), 7)
    grads = scatter_about(key_of[0], (NB, ORDER, ORDER), 1.0, 6.0, ((0, 32),))
    owner_keys = jax.random.split(jax.random.fold_in(key_of[1], 1), NB // BPD)
    owner_turns = jax.random.permutation(jax.random.fold_in(key_of[1], 3), NB // BPD)
    owner = jax.vmap(lambda own, number: assign_block(jax.random.fold_in(key_of[1], 2), own, number, BPD, N_DP, 1, SLOT, 2))(owner_keys, owner_turns).reshape((NB, 1))
    left_root = scatter_about(key_of[2], (N_DP, RS, ORDER, ORDER), ORDER ** -0.5, 0.375, ((0, 32), (2, 8)))
    right_root = scatter_about(key_of[3], (N_DP, RS, ORDER, ORDER), ORDER ** -0.5, 0.375, ((0, 32),))
    first_moment = scatter_about(key_of[4], (N_DP, RS, ORDER, ORDER), 1.0, 6.0, ((0, 32), (2, 8)), jnp.float32)
    second_moment = jnp.clip(jnp.exp(math.log(1.0) - 4.6051702 * jax.random.uniform(key_of[5], (N_DP, RS, ORDER, ORDER), jnp.float32) ** shard_levels(key_of[5], (N_DP, RS, ORDER, ORDER), ((0, 32), (2, 8)), -0.2, 0.2)), 0.01, 1.0)
    return {"grads": grads, "owner": owner, "left_root": left_root, "right_root": right_root, "first_moment": first_moment, "second_moment": second_moment}


def reference(grads, owner, left_root, right_root, first_moment, second_moment):
    owners = owner[:, 0]
    grouped = owners.reshape(N_DP, BPD)
    equal = (grouped[:, :, None] == grouped[:, None, :]).astype(jnp.int32)
    earlier = (jnp.arange(BPD)[None, :] < jnp.arange(BPD)[:, None]).astype(jnp.int32)
    ranks = lax.optimization_barrier(jnp.sum(equal * earlier[None, :, :], axis=2))
    slots = (jnp.arange(N_DP, dtype=jnp.int32)[:, None] * SLOT + ranks).reshape(-1)
    target = (owners * RS + slots).astype(jnp.int32)
    received = jnp.zeros((N_DP * RS, ORDER, ORDER), jnp.bfloat16).at[target].set(grads).reshape(N_DP, RS, ORDER, ORDER)
    live = jnp.zeros((N_DP * RS,), jnp.float32).at[target].set(1.0).reshape(N_DP, RS)

    def one_owner(items):
        block, lroot, rroot, mone, mtwo, alive = items
        left = jnp.einsum('krc,kcd->krd', lroot.astype(jnp.float32), block.astype(jnp.float32)).astype(jnp.bfloat16)
        precond = jnp.einsum('krc,kcd->krd', left.astype(jnp.float32), rroot.astype(jnp.float32))
        grad32 = block.astype(jnp.float32)
        moment_one = 0.9 * mone + 0.1 * grad32
        moment_two = 0.999 * mtwo + 0.001 * grad32 * grad32
        adam = moment_one / (jnp.sqrt(moment_two) + 1e-08)
        total = float(ORDER * ORDER)
        scale = jnp.sqrt(lax.optimization_barrier(jnp.sum(adam * adam, axis=(1, 2))) / total) / jnp.sqrt(lax.optimization_barrier(jnp.sum(precond * precond, axis=(1, 2))) / total + 1e-06)
        return (precond * (alive * scale)[:, None, None]).astype(jnp.bfloat16)
    return lax.map(one_owner, (received, left_root, right_root, first_moment, second_moment, live))
```

```python
import functools

import jax
import jax.numpy as jnp
from jax import lax
from jax.experimental import pallas as pl
from jax.experimental.pallas import tpu as pltpu
from jax.sharding import PartitionSpec as P

MESH = pl.DeviceIdType.MESH
N_Y, N_X, N_C = 4, 4, 2
N_DP = N_Y * N_X * N_C
N_Z = 8
CHUNK = 8
RING = 4
SIGNS = (1, -1)
LIMIT = 50

START = (0, 12, 16, 40, 48, 60, 64)


def decode(kind, q):
    d, g = (lax.rem(q, 3), q // 3) if kind % 2 == 0 else (3, q)
    first = lax.rem(d + 3, 4)
    dc = lax.rem(g, 2)
    if kind < 2:
        half, second = g // 2, 0
    elif kind < 4:
        half, second = g // 4, 3 - 2 * lax.rem(g // 2, 2)
    else:
        half, second = g // 2, 2
    return half, first, second, dc


def step_kernel(
    owner, grads_hbm, left_hbm, right_hbm, mone_hbm, mtwo_hbm, recv_v, scale_out,
    grads_v, out_v, stage_v, pass_v, relay_v, left_v, right_v, mone_v, mtwo_v,
    adam_v, square_v, tiles_v, idx_v, idx,
    load_sems, left_sems, own_sems, idx_sem, send_sems, recv_sems, ring_send, ring_recv, zsend, zrecv,
):
    me, z = lax.axis_index("dp"), lax.axis_index("replica")
    per_shard, order = grads_hbm.shape[0], grads_hbm.shape[1]
    slots, share = mone_hbm.shape[0], mone_hbm.shape[1]
    total = float(order * order)
    per_ring = slots // RING
    y, x, c = me // (N_X * N_C), (me // N_C) % N_X, me % N_C

    def at(dy, dx, dc):
        return (
            lax.rem(y + dy + N_Y, N_Y) * (N_X * N_C) + lax.rem(x + dx + N_X, N_X) * N_C + lax.rem(c + dc, N_C)
        )

    def along(half, first, second, dc):
        return at(second + half * (first - second), first + half * (second - first), dc)

    def slot_of(kind, pos):
        half, first, second, dc = decode(kind, pos - START[kind])
        return 2 * along(half, first, second, dc) + half

    barrier = pltpu.get_barrier_semaphore()
    near = [(0, 0, 1)] + [(dy, dx, dc) for dy, dx in ((0, 1), (0, -1), (1, 0), (-1, 0)) for dc in range(N_C)]
    for step in near:
        pl.semaphore_signal(barrier, inc=1, device_id=(at(*step), z), device_id_type=MESH)
    for dz in range(1, N_Z):
        pl.semaphore_signal(barrier, inc=1, device_id=(me, lax.rem(z + dz, N_Z)), device_id_type=MESH)

    loads = [
        pltpu.make_async_copy(grads_hbm, grads_v.at[pl.ds(0, per_shard)], load_sems.at[0]),
        pltpu.make_async_copy(mone_hbm, mone_v, load_sems.at[1]),
        pltpu.make_async_copy(mtwo_hbm, mtwo_v, load_sems.at[2]),
        pltpu.make_async_copy(right_hbm, right_v, load_sems.at[3]),
    ]
    loads[0].start()
    for kind in range(6):

        def load_left(pos, carry):
            pltpu.make_async_copy(
                left_hbm.at[slot_of(kind, pos)], left_v.at[z, pos], left_sems.at[pos // per_ring]
            ).start()
            return carry

        lax.fori_loop(START[kind], START[kind + 1], load_left, 0)
    for load in loads[1:]:
        load.start()
    grads_v[per_shard] = jnp.zeros((order, order), jnp.bfloat16)

    row = lax.broadcasted_iota(jnp.int32, (per_shard, 128), 0)
    lane = lax.broadcasted_iota(jnp.int32, (per_shard, 128), 1)
    per_line = 128 // per_shard
    line = owner[:, pl.ds(pl.multiple_of(me // per_line * 128, 128), 128)]
    mine = pltpu.roll(
        jnp.broadcast_to(line, (per_shard, 128)), lax.rem(128 - lax.rem(me, per_line) * per_shard, 128), 1
    )
    names = jnp.sum(jnp.where(row == lane, mine, 0), axis=1, keepdims=True)
    ranks = jnp.sum(jnp.where((names == mine) & (lane < row), 1, 0), axis=1, keepdims=True)
    found = jnp.where(2 * names + ranks == lane, row - per_shard, 0)
    idx_v[...] = per_shard + jnp.sum(found, axis=0, keepdims=True)
    to_scalars = pltpu.make_async_copy(idx_v, idx, idx_sem)
    to_scalars.start()
    to_scalars.wait()
    loads[0].wait()
    pl.semaphore_wait(barrier, len(near) + N_Z - 1)

    def pack(half, first, part, into):
        def one(i, carry):
            p = along(half, first, i // N_C, lax.rem(i, N_C))
            into[i] = grads_v[idx[0, 2 * p + half]]
            return carry

        lax.fori_loop(4 * part, 4 * part + 4, one, 0)

    count = [0]

    def message(src, dst, target):
        n = count[0]
        count[0] += 1
        return pltpu.make_async_remote_copy(
            src_ref=src, dst_ref=dst, send_sem=send_sems.at[n], recv_sem=recv_sems.at[n],
            device_id=(target, z), device_id_type=MESH,
        )

    def place(kind, g):
        n = 1 if kind % 2 else 3
        return recv_v.at[pl.ds(START[kind] + n * g, n)]

    pieces = (pl.ds(0, 3), pl.ds(3, 1))
    via, straight, onward = {}, {}, {}
    far, ahead, inside, passed, own = {}, {}, {}, {}, {}
    for h in range(2):
        for part, sign in enumerate(SIGNS):
            half_part = pl.ds(4 * part, 4)
            via[h, part] = message(out_v.at[h, 2, half_part], pass_v.at[h, part], along(h, sign, 0, 0))
            straight[h, part] = message(out_v.at[h, part], stage_v.at[h, 2 * part], along(h, sign, 0, 0))
            onward[h, part] = message(pass_v.at[h, part], stage_v.at[h, 3, half_part], along(h, sign, 0, 0))
    for h in range(2):
        for m, piece in enumerate(pieces):
            for part, sign in enumerate(SIGNS):
                far[h, m, part] = message(
                    stage_v.at[h, piece, 4 + part], relay_v.at[h, part, piece], along(h, 0, sign, 0)
                )
                for dc in range(N_C):
                    ahead[h, m, part, dc] = message(
                        stage_v.at[h, piece, 2 * (sign % 4) + dc],
                        place(2 + m, (h * 2 + part) * 2 + dc),
                        along(h, 0, sign, dc),
                    )
                passed[h, m, part] = message(
                    relay_v.at[h, part, piece], place(4 + m, h * 2 + part), along(h, 0, sign, part)
                )
            inside[h, m] = message(stage_v.at[h, piece, 1], place(m, h * 2 + 1), at(0, 0, 1))
            own[h, m] = pltpu.make_async_copy(stage_v.at[h, piece, 0], place(m, h * 2), own_sems.at[h, m])

    def ring(part, t, chunk, source):
        piece = left_v.at[source, pl.ds(chunk * per_ring, per_ring)]
        return pltpu.make_async_remote_copy(
            src_ref=piece, dst_ref=piece,
            send_sem=ring_send.at[part, t, chunk], recv_sem=ring_recv.at[part, t, chunk],
            device_id=(me, lax.rem(z + SIGNS[part] + N_Z, N_Z)), device_id_type=MESH,
        )

    def ring_out(part, t, chunk):
        return ring(part, t, chunk, lax.rem(z - SIGNS[part] * t + N_Z, N_Z))

    def ring_in(part, t, chunk):
        return ring(part, t, chunk, lax.rem(z - SIGNS[part] * (t + 1) + N_Z, N_Z))

    def travels(part, t, chunk):
        return t < 3 or chunk % 2 == part

    def pass_on(t, *chunks):
        for chunk in chunks:
            for part in range(2):
                if travels(part, t, chunk):
                    ring_in(part, t, chunk).wait_recv()
                if t < 3 and travels(part, t + 1, chunk):
                    ring_out(part, t + 1, chunk).start()

    rows = pl.ds(pl.multiple_of(z * share, share), share)

    def fold(values):
        values = values[:, :128] + values[:, 128:]
        return jnp.sum(values.reshape(values.shape[0] // 8, 8, 128), axis=0)

    def adam(kind):
        def one(pos, carry):
            k = slot_of(kind, pos)
            grad32 = recv_v[pos, rows, :].astype(jnp.float32)
            moment_one = 0.9 * mone_v[k] + 0.1 * grad32
            moment_two = 0.999 * mtwo_v[k] + 0.001 * grad32 * grad32
            ratio = moment_one / (jnp.sqrt(moment_two) + 1e-08)
            adam_v[k] = fold(ratio * ratio)
            return carry

        lax.fori_loop(START[kind], START[kind + 1], one, 0)

    def multiply(kind, begin, end):
        def some(i, carry):
            places = [begin + 4 * i + j for j in range(4)]
            ks = [slot_of(kind, pos) for pos in places]
            halves = [
                jnp.dot(
                    left_v[:, pos].reshape(order, order), recv_v[pos], preferred_element_type=jnp.float32
                ).astype(jnp.bfloat16)
                for pos in places
            ]
            for pos, k, half in zip(places, ks, halves):
                precond = jnp.dot(half, right_v[k], preferred_element_type=jnp.float32)
                square_v[k] = fold(precond * precond)
                recv_v[pos] = precond.astype(jnp.bfloat16)
            return carry

        lax.fori_loop(0, (end - begin) // 4, some, 0)

    def by_lane(sums):
        by_slot = jnp.sum(jnp.sum(sums, axis=1), axis=1, keepdims=True)
        spread = jnp.broadcast_to(by_slot, (slots, 128))
        return jnp.sum(jnp.where(diagonal, spread, 0.0), axis=0, keepdims=True)

    diagonal = lax.broadcasted_iota(jnp.int32, (slots, 128), 0) == lax.broadcasted_iota(
        jnp.int32, (slots, 128), 1
    )

    for h in range(2):
        for part in range(2):
            pack(h, 2, part, out_v.at[h, 2])
            via[h, part].start()
    for chunk in range(RING):
        first = pl.ds(chunk * per_ring, per_ring)
        pltpu.make_async_copy(left_hbm.at[first], left_v.at[z, first], left_sems.at[chunk]).wait()
        for part in range(2):
            ring_out(part, 0, chunk).start()
    for h in range(2):
        for part, sign in enumerate(SIGNS):
            for half_part in range(2):
                pack(h, sign, half_part, out_v.at[h, part])
            straight[h, part].start()
    for h in range(2):
        for half_part in range(2):
            pack(h, 0, half_part, stage_v.at[h, 1])

    pass_on(0, 0)
    for h in range(2):
        for part in range(2):
            via[h, part].wait_recv()
            onward[h, part].start()
    pass_on(0, 1, 2, 3)
    pass_on(1, 0)
    for load in loads[1:]:
        load.wait()
    for m in range(2):
        for h in range(2):
            for part in range(2):
                (straight if m == 0 else onward)[h, part].wait_recv()
            for part in range(2):
                far[h, m, part].start()
            for part in range(2):
                for dc in range(N_C):
                    ahead[h, m, part, dc].start()
            inside[h, m].start()
            own[h, m].start()
        pass_on(1, *((1, 2) if m == 0 else (3,)))
    for m in range(2):
        for h in range(2):
            own[h, m].wait()
            inside[h, m].wait_recv()
        adam(m)
    pass_on(2, 0)
    for h in range(2):
        for part in range(2):
            far[h, 0, part].wait_recv()
            passed[h, 0, part].start()
    pass_on(2, 1, 2, 3)
    for m in range(2):
        for h in range(2):
            for part in range(2):
                if m == 1:
                    far[h, m, part].wait_recv()
                    passed[h, m, part].start()
                for dc in range(N_C):
                    ahead[h, m, part, dc].wait_recv()
        adam(2 + m)
        if m == 0:
            pass_on(3, 0, 1)
            multiply(0, 0, 12)
            multiply(1, 12, 16)
            multiply(2, 16, 32)
    pass_on(3, 2, 3)
    multiply(2, 32, 40)
    multiply(3, 40, 48)
    for m in range(2):
        for h in range(2):
            for part in range(2):
                passed[h, m, part].wait_recv()
        adam(4 + m)
        if m == 0:
            multiply(4, 48, 60)

    tiles_v[0] = jnp.broadcast_to(by_lane(adam_v[...]), (8, 128))

    def tell(dz):
        return pltpu.make_async_remote_copy(
            src_ref=tiles_v.at[0],
            dst_ref=tiles_v.at[dz],
            send_sem=zsend.at[dz],
            recv_sem=zrecv.at[dz],
            device_id=(me, lax.rem(z + dz, N_Z)),
            device_id_type=MESH,
        )

    for dz in range(1, N_Z):
        tell(dz).start()
    multiply(5, 60, 64)
    sum_pre = by_lane(square_v[...])
    for group in (via, straight, onward, far, ahead, inside, passed):
        for copy in group.values():
            copy.wait_send()
    for t in range(4):
        for chunk in range(RING):
            for part in range(2):
                if travels(part, t, chunk):
                    ring_out(part, t, chunk).wait_send()
    for dz in range(1, N_Z):
        tell(dz).wait()
    sum_adam = jnp.sum(tiles_v[...], axis=0)[:1]
    shard = lax.broadcasted_iota(jnp.int32, (owner.shape[1], 128), 0) // per_shard
    slot = lax.broadcasted_iota(jnp.int32, (owner.shape[1], 128), 1)
    ours = jnp.broadcast_to(jnp.where(owner[...] == me, 1.0, 0.0), (8, owner.shape[1]))
    counts = jnp.dot(
        ours.astype(jnp.bfloat16),
        jnp.where(shard == slot // 2, 1.0, 0.0).astype(jnp.bfloat16),
        preferred_element_type=jnp.float32,
    )[:1]
    rank = lax.rem(slot[:1], 2).astype(jnp.float32)
    live = jnp.where(counts > rank, 1.0, 0.0)
    scale = live * (jnp.sqrt(sum_adam / total) / jnp.sqrt(sum_pre / total + 1e-06))
    by_row = jnp.where(diagonal, jnp.broadcast_to(scale, (slots, 128)), 0.0)
    scale_out[...] = jnp.broadcast_to(jnp.sum(by_row, axis=1, keepdims=True), (slots, 128))


def step(owner, grads, left, right, mone, mtwo):
    per_shard, order, _ = grads.shape
    slots, share, _ = mone.shape
    block = (order, order)
    anywhere = pl.BlockSpec(memory_space=pl.ANY)
    vmem = pl.BlockSpec(memory_space=pltpu.VMEM)
    dma = pltpu.SemaphoreType.DMA
    return pl.pallas_call(
        step_kernel,
        out_shape=(
            pltpu.VMEM((slots, *block), jnp.bfloat16),
            pltpu.VMEM((slots, 128), jnp.float32),
        ),
        in_specs=[vmem] + [anywhere] * 5,
        out_specs=(vmem, vmem),
        scratch_shapes=[
            pltpu.VMEM((per_shard + 1, *block), jnp.bfloat16),
            pltpu.VMEM((2, 3, 8, *block), jnp.bfloat16),
            pltpu.VMEM((2, 4, 8, *block), jnp.bfloat16),
            pltpu.VMEM((2, 2, 4, *block), jnp.bfloat16),
            pltpu.VMEM((2, 2, 4, *block), jnp.bfloat16),
            pltpu.VMEM((N_Z, slots, share, order), jnp.bfloat16),
            pltpu.VMEM((slots, *block), jnp.bfloat16),
            pltpu.VMEM((slots, share, order), jnp.float32),
            pltpu.VMEM((slots, share, order), jnp.float32),
            pltpu.VMEM((slots, 8, 128), jnp.float32),
            pltpu.VMEM((slots, 8, 128), jnp.float32),
            pltpu.VMEM((N_Z, 8, 128), jnp.float32),
            pltpu.VMEM((1, 128), jnp.int32),
            pltpu.SMEM((1, 128), jnp.int32),
            dma((4,)),
            dma((RING,)),
            dma((2, 2)),
            dma,
            dma((48,)),
            dma((48,)),
            dma((2, 4, RING)),
            dma((2, 4, RING)),
            dma((N_Z,)),
            dma((N_Z,)),
        ],
        compiler_params=pltpu.CompilerParams(
            collective_id=0, has_side_effects=True, vmem_limit_bytes=LIMIT * 2**20
        ),
        cost_estimate=pl.CostEstimate(
            flops=4 * slots * order**3, bytes_accessed=4 * 10**8, transcendentals=10**6
        ),
    )(owner, grads, left, right, mone, mtwo)


def place_of(me, slot):
    y, x, c = me // (N_X * N_C), (me // N_C) % N_X, me % N_C
    source, half = slot // 2, lax.rem(slot, 2)
    dy = lax.rem(source // (N_X * N_C) - y + N_Y, N_Y)
    dx = lax.rem(lax.rem(source // N_C, N_X) - x + N_X, N_X)
    dc = lax.rem(source + c, N_C)
    first, second = dx + half * (dy - dx), dy + half * (dx - dy)
    d = lax.rem(first + 1, 4)
    g = half * 2 + dc
    beside = (half * 2 + (3 - second) // 2) * 2 + dc
    near = jnp.where(d == 3, START[1] + g, START[0] + 3 * g + d)
    middle = jnp.where(d == 3, START[3] + beside, START[2] + 3 * beside + d)
    away = jnp.where(d == 3, START[5] + g, START[4] + 3 * g + d)
    return jnp.where(second == 0, near, jnp.where(second == 2, away, middle))


def scale_kernel(x, scale, out):
    me, base = lax.axis_index("dp"), pl.program_id(0) * CHUNK
    for k in range(CHUNK):
        row = scale[k : k + 1, :]
        factor = jnp.concatenate([row, row], axis=1)
        out[k] = (x[place_of(me, base + k)].astype(jnp.float32) * factor).astype(jnp.bfloat16)


def apply_scale(x, scale):
    slots, order, _ = x.shape
    return pl.pallas_call(
        scale_kernel,
        grid=(slots // CHUNK,),
        out_shape=jax.ShapeDtypeStruct(x.shape, jnp.bfloat16),
        in_specs=[pl.BlockSpec(memory_space=pltpu.VMEM), pl.BlockSpec((CHUNK, 128), lambda i: (i, 0))],
        out_specs=pl.BlockSpec((CHUNK, order, order), lambda i: (i, 0, 0)),
        compiler_params=pltpu.CompilerParams(vmem_limit_bytes=24 * 2**20),
    )(x, scale)


def per_device(grads, owner, left_root, right_root, first_moment, second_moment):
    x, scale = step(
        owner.reshape(1, -1), grads, left_root[0], right_root[0], first_moment[0], second_moment[0]
    )
    return apply_scale(x, scale)[None]


def solution(mesh):
    placed = (
        P("dp", None, None),
        P(),
        P("dp", None, "replica", None),
        P("dp", None, None, None),
        P("dp", None, "replica", None),
        P("dp", None, "replica", None),
    )
    return jax.shard_map(
        per_device, mesh=mesh, in_specs=placed, out_specs=P("dp", None, None, None), check_vma=False
    )
```

```python
import functools

import jax
import jax.numpy as jnp
from jax import lax
from jax.experimental import pallas as pl
from jax.experimental.pallas import tpu as pltpu
from jax.sharding import PartitionSpec as P

MESH = pl.DeviceIdType.MESH
N_Y, N_X, N_C = 4, 4, 2
N_DP = N_Y * N_X * N_C
N_Z = 8
GROUP = 4
RING = 4
SIGNS = (1, -1)
LIMIT = 50

NEAR, NEAR_LONG, BESIDE, AWAY_LONG, AWAY, BESIDE_CROSS, BESIDE_LONG = range(7)
START = (0, 12, 16, 28, 32, 44, 56, 64)
PACKED = ((0, 0), (0, 1), (1, 0), (2, 0), (2, 1), (1, 1), (3, 0), (3, 1))
FULL = (pl.ds(0, 3), pl.ds(5, 3))


def decode(kind, q):
    long = kind in (NEAR_LONG, AWAY_LONG, BESIDE_LONG)
    d, g = (3, q) if long else (lax.rem(q, 3), q // 3)
    first, low = lax.rem(d + 3, 4), lax.rem(g, 2)
    if kind in (NEAR, NEAR_LONG):
        return g // 2, first, 0, low
    if kind in (AWAY, AWAY_LONG):
        return g // 2, first, 2, low
    return lax.rem(g // 2, 2), first, 3 - 2 * low, g // 4 if kind == BESIDE_LONG else int(kind == BESIDE_CROSS)


def step_kernel(
    owner, grads_hbm, left_hbm, right_hbm, mone_hbm, mtwo_hbm, recv_v, scale_out,
    grads_v, out_v, stage_v, pass_v, relay_v, left_v, right_v, mone_v, mtwo_v,
    adam_v, square_v, tiles_v, live_v, idx_v, idx,
    load_sems, left_sems, own_sems, idx_sem, send_sems, recv_sems, ring_send, ring_recv, zsend, zrecv,
):
    me, z = lax.axis_index("dp"), lax.axis_index("replica")
    per_shard, order = grads_hbm.shape[0], grads_hbm.shape[1]
    slots, share = mone_hbm.shape[0], mone_hbm.shape[1]
    total = float(order * order)
    per_ring = slots // RING
    y, x, c = me // (N_X * N_C), (me // N_C) % N_X, me % N_C

    def at(dy, dx, dc):
        return (
            lax.rem(y + dy + N_Y, N_Y) * (N_X * N_C) + lax.rem(x + dx + N_X, N_X) * N_C + lax.rem(c + dc, N_C)
        )

    def along(half, first, second, dc):
        return at(second + half * (first - second), first + half * (second - first), dc)

    def slot_of(kind, pos):
        half, first, second, dc = decode(kind, pos - START[kind])
        return 2 * along(half, first, second, dc) + half

    barrier = pltpu.get_barrier_semaphore()
    near = [(0, 0, 1)] + [(dy, dx, dc) for dy, dx in ((0, 1), (0, -1), (1, 0), (-1, 0)) for dc in range(N_C)]
    for step in near:
        pl.semaphore_signal(barrier, inc=1, device_id=(at(*step), z), device_id_type=MESH)
    for dz in range(1, N_Z):
        pl.semaphore_signal(barrier, inc=1, device_id=(me, lax.rem(z + dz, N_Z)), device_id_type=MESH)

    loads = [
        pltpu.make_async_copy(grads_hbm, grads_v.at[pl.ds(0, per_shard)], load_sems.at[0]),
        pltpu.make_async_copy(mone_hbm, mone_v, load_sems.at[1]),
        pltpu.make_async_copy(mtwo_hbm, mtwo_v, load_sems.at[2]),
        pltpu.make_async_copy(right_hbm, right_v, load_sems.at[3]),
    ]
    loads[0].start()
    row = lax.broadcasted_iota(jnp.int32, (per_shard, 128), 0)
    lane = lax.broadcasted_iota(jnp.int32, (per_shard, 128), 1)
    per_line = 128 // per_shard
    line = owner[:, pl.ds(pl.multiple_of(me // per_line * 128, 128), 128)]
    mine = pltpu.roll(
        jnp.broadcast_to(line, (per_shard, 128)), lax.rem(128 - lax.rem(me, per_line) * per_shard, 128), 1
    )
    names = jnp.sum(jnp.where(row == lane, mine, 0), axis=1, keepdims=True)
    ranks = jnp.sum(jnp.where((names == mine) & (lane < row), 1, 0), axis=1, keepdims=True)
    found = jnp.where(2 * names + ranks == lane, row - per_shard, 0)
    idx_v[...] = per_shard + jnp.sum(found, axis=0, keepdims=True)
    to_scalars = pltpu.make_async_copy(idx_v, idx, idx_sem)
    to_scalars.start()
    for kind in range(7):

        def load_left(pos, carry):
            pltpu.make_async_copy(
                left_hbm.at[slot_of(kind, pos)], left_v.at[z, pos], left_sems.at[pos // per_ring]
            ).start()
            return carry

        lax.fori_loop(START[kind], START[kind + 1], load_left, 0)
    for load in loads[1:]:
        load.start()
    grads_v[per_shard] = jnp.zeros((order, order), jnp.bfloat16)
    to_scalars.wait()
    loads[0].wait()
    pl.semaphore_wait(barrier, len(near) + N_Z - 1)

    def pack(half, first, places, into):
        for i in places:
            p = along(half, first, *PACKED[i])
            into[i] = grads_v[idx[0, 2 * p + half]]

    count = [0]

    def message(src, dst, target, plane=z):
        n = count[0]
        count[0] += 1
        return pltpu.make_async_remote_copy(
            src_ref=src, dst_ref=dst, send_sem=send_sems.at[n], recv_sem=recv_sems.at[n],
            device_id=(target, plane), device_id_type=MESH,
        )

    def place(kind, g):
        n = 1 if kind in (NEAR_LONG, AWAY_LONG, BESIDE_LONG) else 3
        return recv_v.at[pl.ds(START[kind] + n * g, n)]

    parity = lax.rem(z, 2)
    half_rows = pl.ds(pl.multiple_of(parity * (order // 2), order // 2), order // 2)
    other_rows = pl.ds(pl.multiple_of((1 - parity) * (order // 2), order // 2), order // 2)
    pieces = (pl.ds(0, 3), pl.ds(3, 1))
    via, straight, onward = {}, {}, {}
    far, ahead, inside, passed, own, swap, swapped = {}, {}, {}, {}, {}, {}, {}
    for h in range(2):
        for part, sign in enumerate(SIGNS):
            there = along(h, sign, 0, 0)
            straight[h, part] = message(out_v.at[h, part], stage_v.at[h, 2 * part], there)
            via[h, 0, part] = message(out_v.at[h, 2, FULL[part]], pass_v.at[h, part, pl.ds(0, 3)], there)
            onward[h, 0, part] = message(pass_v.at[h, part, pl.ds(0, 3)], stage_v.at[h, 3, FULL[part]], there)
            via[h, 1, part] = message(
                out_v.at[h, 2, 3 + part, half_rows], pass_v.at[h, part, 3, half_rows], there
            )
            onward[h, 1, part] = message(
                pass_v.at[h, part, 3, half_rows], stage_v.at[h, 3, 3 + part, half_rows], there
            )
            there = along(h, 0, sign, 0)
            last = along(h, 0, sign, part)
            far[h, 0, part] = message(
                stage_v.at[h, pieces[0], 3 + part], relay_v.at[h, part, pieces[0]], there
            )
            passed[h, 0, part] = message(relay_v.at[h, part, pieces[0]], place(AWAY, h * 2 + part), last)
            far[h, 1, part] = message(
                stage_v.at[h, 3, 3 + part, half_rows], relay_v.at[h, part, 3, half_rows], there
            )
            passed[h, 1, part] = message(
                relay_v.at[h, part, 3, half_rows], recv_v.at[START[AWAY_LONG] + h * 2 + part, half_rows], last
            )
            for m, piece in enumerate(pieces):
                for dc in range(N_C):
                    ahead[h, m, part, dc] = message(
                        stage_v.at[h, piece, PACKED.index((sign % 4, dc))],
                        place((BESIDE, BESIDE_CROSS)[dc], h * 2 + part) if m == 0 else place(BESIDE_LONG, dc * 4 + h * 2 + part),
                        along(h, 0, sign, dc),
                    )
        for m, piece in enumerate(pieces):
            inside[h, m] = message(stage_v.at[h, piece, 1], place((NEAR, NEAR_LONG)[m], h * 2 + 1), at(0, 0, 1))
            own[h, m] = pltpu.make_async_copy(stage_v.at[h, piece, 0], place((NEAR, NEAR_LONG)[m], h * 2), own_sems.at[h, m])
        step = (1 - 2 * parity) * (1 - 2 * h)
        plane = lax.rem(z + step + N_Z, N_Z)
        both = pl.ds(START[AWAY_LONG] + h * 2, 2)
        swap[h] = message(recv_v.at[both, half_rows], recv_v.at[both, half_rows], me, plane)
        swapped[h] = pltpu.make_async_remote_copy(
            src_ref=recv_v.at[both, other_rows], dst_ref=recv_v.at[both, other_rows],
            send_sem=send_sems.at[count[0] - 1], recv_sem=recv_sems.at[count[0] - 1],
            device_id=(me, plane), device_id_type=MESH,
        )

    def ring(part, t, chunk, source):
        piece = left_v.at[source, pl.ds(chunk * per_ring, per_ring)]
        return pltpu.make_async_remote_copy(
            src_ref=piece, dst_ref=piece,
            send_sem=ring_send.at[part, t, chunk], recv_sem=ring_recv.at[part, t, chunk],
            device_id=(me, lax.rem(z + SIGNS[part] + N_Z, N_Z)), device_id_type=MESH,
        )

    def ring_out(part, t, chunk):
        return ring(part, t, chunk, lax.rem(z - SIGNS[part] * t + N_Z, N_Z))

    def ring_in(part, t, chunk):
        return ring(part, t, chunk, lax.rem(z - SIGNS[part] * (t + 1) + N_Z, N_Z))

    def travels(part, t, chunk):
        return t < 3 or chunk % 2 == part

    def pass_on(t, *chunks):
        for chunk in chunks:
            for part in range(2):
                if travels(part, t, chunk):
                    ring_in(part, t, chunk).wait_recv()
                if t < 3 and travels(part, t + 1, chunk):
                    ring_out(part, t + 1, chunk).start()

    def begin(chunk):
        for part in range(2):
            ring_out(part, 0, chunk).start()

    rows = pl.ds(pl.multiple_of(z * share, share), share)

    def fold(values):
        values = values[:, :128] + values[:, 128:]
        return jnp.sum(values.reshape(values.shape[0] // 8, 8, 128), axis=0)

    def adam(kind):
        def some(i, carry):
            for j in range(4):
                pos = START[kind] + 4 * i + j
                k = slot_of(kind, pos)
                grad32 = recv_v[pos, rows, :].astype(jnp.float32)
                moment_one = 0.9 * mone_v[k] + 0.1 * grad32
                moment_two = 0.999 * mtwo_v[k] + 0.001 * grad32 * grad32
                ratio = moment_one / (jnp.sqrt(moment_two) + 1e-08)
                adam_v[k] = fold(ratio * ratio)
            return carry

        lax.fori_loop(0, (START[kind + 1] - START[kind]) // 4, some, 0)

    def multiply(kind):
        def some(i, carry):
            places = [START[kind] + 4 * i + j for j in range(4)]
            ks = [slot_of(kind, pos) for pos in places]
            halves = [
                jnp.dot(
                    left_v[:, pos].reshape(order, order), recv_v[pos], preferred_element_type=jnp.float32
                ).astype(jnp.bfloat16)
                for pos in places
            ]
            for pos, k, half in zip(places, ks, halves):
                precond = jnp.dot(half, right_v[k], preferred_element_type=jnp.float32)
                square_v[k] = fold(precond * precond)
                recv_v[pos] = precond.astype(jnp.bfloat16)
            return carry

        lax.fori_loop(0, (START[kind + 1] - START[kind]) // 4, some, 0)

    def count_live():
        shard = lax.broadcasted_iota(jnp.int32, (owner.shape[1], 128), 0) // per_shard
        slot = lax.broadcasted_iota(jnp.int32, (owner.shape[1], 128), 1)
        ours = jnp.broadcast_to(jnp.where(owner[...] == me, 1.0, 0.0), (8, owner.shape[1]))
        counts = jnp.dot(
            ours.astype(jnp.bfloat16),
            jnp.where(shard == slot // 2, 1.0, 0.0).astype(jnp.bfloat16),
            preferred_element_type=jnp.float32,
        )[:1]
        rank = lax.rem(slot[:1], 2).astype(jnp.float32)
        live_v[...] = jnp.where(counts > rank, 1.0, 0.0)

    def by_lane(sums):
        by_slot = jnp.sum(jnp.sum(sums, axis=1), axis=1, keepdims=True)
        spread = jnp.broadcast_to(by_slot, (slots, 128))
        return jnp.sum(jnp.where(diagonal, spread, 0.0), axis=0, keepdims=True)

    diagonal = lax.broadcasted_iota(jnp.int32, (slots, 128), 0) == lax.broadcasted_iota(
        jnp.int32, (slots, 128), 1
    )

    every = [(h, part) for h in range(2) for part in range(2)]
    for h, part in every:
        pack(h, 2, (3 + part,), out_v.at[h, 2])
        via[h, 1, part].start()
    for h, part in every:
        pack(h, 2, ((0, 1, 2), (5, 6, 7))[part], out_v.at[h, 2])
        via[h, 0, part].start()
    for chunk in range(RING):
        first = pl.ds(chunk * per_ring, per_ring)
        pltpu.make_async_copy(left_hbm.at[first], left_v.at[z, first], left_sems.at[chunk]).wait()
        if chunk < 2:
            begin(chunk)
    for h, part in every:
        pack(h, SIGNS[part], range(8), out_v.at[h, part])
        straight[h, part].start()
    for h, part in every:
        via[h, 1, part].wait_recv()
        onward[h, 1, part].start()
    for h in range(2):
        pack(h, 0, range(8), stage_v.at[h, 1])

    pass_on(0, 0)
    for h, part in every:
        onward[h, 1, part].wait_recv()
        far[h, 1, part].start()
    pass_on(0, 1)
    for h, part in every:
        via[h, 0, part].wait_recv()
        onward[h, 0, part].start()
    for h, part in every:
        far[h, 1, part].wait_recv()
        passed[h, 1, part].start()
    pass_on(1, 0)
    for h in range(2):
        for part in range(2):
            passed[h, 1, part].wait_recv()
        swap[h].start()
    pass_on(1, 1)
    begin(2)
    for load in loads[1:]:
        load.wait()
    count_live()
    pass_on(2, 0)
    for h, part in every:
        straight[h, part].wait_recv()
    for h, part in every:
        far[h, 0, part].start()
    for h in range(2):
        inside[h, 0].start()
        own[h, 0].start()
    pass_on(2, 1)
    begin(3)
    for h, part in every:
        ahead[h, 0, part, 0].start()
    for h in range(2):
        swapped[h].wait_recv()
        swap[h].wait_send()
    adam(AWAY_LONG)
    pass_on(0, 2)
    for h, part in every:
        onward[h, 0, part].wait_recv()
    for h in range(2):
        inside[h, 1].start()
        own[h, 1].start()
    pass_on(3, 0, 1)
    multiply(AWAY_LONG)
    pass_on(0, 3)
    for m in range(2):
        for h in range(2):
            own[h, m].wait()
            inside[h, m].wait_recv()
        adam((NEAR, NEAR_LONG)[m])
    for h, part in every:
        far[h, 0, part].wait_recv()
        passed[h, 0, part].start()
    multiply(NEAR)
    pass_on(1, 2)
    multiply(NEAR_LONG)
    for h, part in every:
        ahead[h, 0, part, 0].wait_recv()
    for h, part in every:
        ahead[h, 0, part, 1].start()
    pass_on(1, 3)
    adam(BESIDE)
    multiply(BESIDE)
    pass_on(2, 2)
    for h, part in every:
        passed[h, 0, part].wait_recv()
    for dc in range(N_C):
        for h, part in every:
            ahead[h, 1, part, dc].start()
    adam(AWAY)
    pass_on(2, 3)
    pass_on(3, 2)
    multiply(AWAY)
    for h, part in every:
        ahead[h, 0, part, 1].wait_recv()
    adam(BESIDE_CROSS)
    pass_on(3, 3)
    multiply(BESIDE_CROSS)
    for dc in range(N_C):
        for h, part in every:
            ahead[h, 1, part, dc].wait_recv()
    adam(BESIDE_LONG)

    tiles_v[0] = jnp.broadcast_to(by_lane(adam_v[...]), (8, 128))

    def tell(dz):
        return pltpu.make_async_remote_copy(
            src_ref=tiles_v.at[0],
            dst_ref=tiles_v.at[dz],
            send_sem=zsend.at[dz],
            recv_sem=zrecv.at[dz],
            device_id=(me, lax.rem(z + dz, N_Z)),
            device_id_type=MESH,
        )

    for dz in range(1, N_Z):
        tell(dz).start()
    multiply(BESIDE_LONG)
    sum_pre = by_lane(square_v[...])
    for group in (via, straight, onward, far, ahead, inside, passed):
        for copy in group.values():
            copy.wait_send()
    for t in range(4):
        for chunk in range(RING):
            for part in range(2):
                if travels(part, t, chunk):
                    ring_out(part, t, chunk).wait_send()
    for dz in range(1, N_Z):
        tell(dz).wait()
    sum_adam = jnp.sum(tiles_v[...], axis=0)[:1]
    scale = live_v[...] * (jnp.sqrt(sum_adam / total) / jnp.sqrt(sum_pre / total + 1e-06))
    by_row = jnp.where(diagonal, jnp.broadcast_to(scale, (slots, 128)), 0.0)
    scale_out[...] = jnp.broadcast_to(jnp.sum(by_row, axis=1, keepdims=True), (slots, 128))


def step(owner, grads, left, right, mone, mtwo):
    per_shard, order, _ = grads.shape
    slots, share, _ = mone.shape
    block = (order, order)
    anywhere = pl.BlockSpec(memory_space=pl.ANY)
    vmem = pl.BlockSpec(memory_space=pltpu.VMEM)
    dma = pltpu.SemaphoreType.DMA
    return pl.pallas_call(
        step_kernel,
        out_shape=(
            pltpu.VMEM((slots, *block), jnp.bfloat16),
            pltpu.VMEM((slots, 128), jnp.float32),
        ),
        in_specs=[vmem] + [anywhere] * 5,
        out_specs=(vmem, vmem),
        scratch_shapes=[
            pltpu.VMEM((per_shard + 1, *block), jnp.bfloat16),
            pltpu.VMEM((2, 3, 8, *block), jnp.bfloat16),
            pltpu.VMEM((2, 4, 8, *block), jnp.bfloat16),
            pltpu.VMEM((2, 2, 4, *block), jnp.bfloat16),
            pltpu.VMEM((2, 2, 4, *block), jnp.bfloat16),
            pltpu.VMEM((N_Z, slots, share, order), jnp.bfloat16),
            pltpu.VMEM((slots, *block), jnp.bfloat16),
            pltpu.VMEM((slots, share, order), jnp.float32),
            pltpu.VMEM((slots, share, order), jnp.float32),
            pltpu.VMEM((slots, 8, 128), jnp.float32),
            pltpu.VMEM((slots, 8, 128), jnp.float32),
            pltpu.VMEM((N_Z, 8, 128), jnp.float32),
            pltpu.VMEM((1, 128), jnp.float32),
            pltpu.VMEM((1, 128), jnp.int32),
            pltpu.SMEM((1, 128), jnp.int32),
            dma((4,)),
            dma((RING,)),
            dma((2, 2)),
            dma,
            dma((58,)),
            dma((58,)),
            dma((2, 4, RING)),
            dma((2, 4, RING)),
            dma((N_Z,)),
            dma((N_Z,)),
        ],
        compiler_params=pltpu.CompilerParams(
            collective_id=0, has_side_effects=True, vmem_limit_bytes=LIMIT * 2**20
        ),
        cost_estimate=pl.CostEstimate(
            flops=4 * slots * order**3, bytes_accessed=4 * 10**8, transcendentals=10**6
        ),
    )(owner, grads, left, right, mone, mtwo)


def place_of(me, slot):
    y, x, c = me // (N_X * N_C), (me // N_C) % N_X, me % N_C
    source, half = slot // 2, lax.rem(slot, 2)
    dy = lax.rem(source // (N_X * N_C) - y + N_Y, N_Y)
    dx = lax.rem(lax.rem(source // N_C, N_X) - x + N_X, N_X)
    dc = lax.rem(source + c, N_C)
    first, second = dx + half * (dy - dx), dy + half * (dx - dy)
    d = lax.rem(first + 1, 4)
    g, beside = half * 2 + dc, half * 2 + (3 - second) // 2
    near = jnp.where(d == 3, START[NEAR_LONG] + g, START[NEAR] + 3 * g + d)
    away = jnp.where(d == 3, START[AWAY_LONG] + g, START[AWAY] + 3 * g + d)
    cross = START[BESIDE] + dc * (START[BESIDE_CROSS] - START[BESIDE])
    middle = jnp.where(d == 3, START[BESIDE_LONG] + dc * 4 + beside, cross + 3 * beside + d)
    return jnp.where(second == 0, near, jnp.where(second == 2, away, middle))


def scale_kernel(x, scale, out, ready, sems):
    me = lax.axis_index("dp")

    def copy(i):
        some = pl.ds(GROUP * i, GROUP)
        return pltpu.make_async_copy(ready.at[some], out.at[some], sems.at[i])

    def one(i, carry):
        for j in range(GROUP):
            k = GROUP * i + j
            row = scale[pl.ds(k, 1), :]
            factor = jnp.concatenate([row, row], axis=1)
            ready[k] = (x[place_of(me, k)].astype(jnp.float32) * factor).astype(jnp.bfloat16)
        copy(i).start()
        return carry

    def settle(i, carry):
        copy(i).wait()
        return carry

    steps = x.shape[0] // GROUP
    lax.fori_loop(0, steps, one, 0)
    lax.fori_loop(0, steps, settle, 0)


def apply_scale(x, scale):
    vmem = pl.BlockSpec(memory_space=pltpu.VMEM)
    return pl.pallas_call(
        scale_kernel,
        out_shape=jax.ShapeDtypeStruct(x.shape, jnp.bfloat16),
        in_specs=[vmem, vmem],
        out_specs=pl.BlockSpec(memory_space=pl.ANY),
        scratch_shapes=[
            pltpu.VMEM(x.shape, jnp.bfloat16),
            pltpu.SemaphoreType.DMA((x.shape[0] // GROUP,)),
        ],
        compiler_params=pltpu.CompilerParams(vmem_limit_bytes=24 * 2**20),
    )(x, scale)


def per_device(grads, owner, left_root, right_root, first_moment, second_moment):
    x, scale = step(
        owner.reshape(1, -1), grads, left_root[0], right_root[0], first_moment[0], second_moment[0]
    )
    return apply_scale(x, scale)[None]


def solution(mesh):
    placed = (
        P("dp", None, None),
        P(),
        P("dp", None, "replica", None),
        P("dp", None, None, None),
        P("dp", None, "replica", None),
        P("dp", None, "replica", None),
    )
    return jax.shard_map(
        per_device, mesh=mesh, in_specs=placed, out_specs=P("dp", None, None, None), check_vma=False
    )
```

```python
import functools

import jax
import jax.numpy as jnp
from jax import lax
from jax.experimental import pallas as pl
from jax.experimental.pallas import tpu as pltpu
from jax.sharding import PartitionSpec as P

MESH = pl.DeviceIdType.MESH
N_Y, N_X, N_C = 4, 4, 2
N_DP = N_Y * N_X * N_C
N_Z = 8
GROUP = 4
RING = 4
SIGNS = (1, -1)
LIMIT = 50

NEAR, NEAR_LONG, BESIDE, AWAY_LONG, AWAY, BESIDE_CROSS, BESIDE_LONG = range(7)
START = (0, 12, 16, 28, 32, 44, 56, 64)
PACKED = ((0, 0), (0, 1), (1, 0), (2, 0), (2, 1), (1, 1), (3, 0), (3, 1))
FULL = (pl.ds(0, 3), pl.ds(5, 3))


def decode(kind, q):
    long = kind in (NEAR_LONG, AWAY_LONG, BESIDE_LONG)
    d, g = (3, q) if long else (lax.rem(q, 3), q // 3)
    first, low = lax.rem(d + 3, 4), lax.rem(g, 2)
    if kind in (NEAR, NEAR_LONG):
        return g // 2, first, 0, low
    if kind in (AWAY, AWAY_LONG):
        return g // 2, first, 2, low
    return lax.rem(g // 2, 2), first, 3 - 2 * low, g // 4 if kind == BESIDE_LONG else int(kind == BESIDE_CROSS)


def step_kernel(
    owner, grads_hbm, left_hbm, right_hbm, mone_hbm, mtwo_hbm, recv_v, scale_out,
    grads_v, out_v, stage_v, pass_v, relay_v, left_v, right_v, mone_v, mtwo_v,
    adam_v, square_v, tiles_v, live_v, idx_v, idx,
    load_sems, left_sems, own_sems, idx_sem, send_sems, recv_sems, ring_send, ring_recv, zsend, zrecv,
):
    me, z = lax.axis_index("dp"), lax.axis_index("replica")
    per_shard, order = grads_hbm.shape[0], grads_hbm.shape[1]
    slots, share = mone_hbm.shape[0], mone_hbm.shape[1]
    total = float(order * order)
    per_ring = slots // RING
    y, x, c = me // (N_X * N_C), (me // N_C) % N_X, me % N_C

    def at(dy, dx, dc):
        return (
            lax.rem(y + dy + N_Y, N_Y) * (N_X * N_C) + lax.rem(x + dx + N_X, N_X) * N_C + lax.rem(c + dc, N_C)
        )

    def along(half, first, second, dc):
        return at(second + half * (first - second), first + half * (second - first), dc)

    def slot_of(kind, pos):
        half, first, second, dc = decode(kind, pos - START[kind])
        return 2 * along(half, first, second, dc) + half

    barrier = pltpu.get_barrier_semaphore()
    near = [(0, 0, 1)] + [(dy, dx, dc) for dy, dx in ((0, 1), (0, -1), (1, 0), (-1, 0)) for dc in range(N_C)]
    for step in near:
        pl.semaphore_signal(barrier, inc=1, device_id=(at(*step), z), device_id_type=MESH)
    for dz in range(1, N_Z):
        pl.semaphore_signal(barrier, inc=1, device_id=(me, lax.rem(z + dz, N_Z)), device_id_type=MESH)

    loads = [
        pltpu.make_async_copy(grads_hbm, grads_v.at[pl.ds(0, per_shard)], load_sems.at[0]),
        pltpu.make_async_copy(mone_hbm, mone_v, load_sems.at[1]),
        pltpu.make_async_copy(mtwo_hbm, mtwo_v, load_sems.at[2]),
        pltpu.make_async_copy(right_hbm, right_v, load_sems.at[3]),
    ]
    loads[0].start()
    row = lax.broadcasted_iota(jnp.int32, (per_shard, 128), 0)
    lane = lax.broadcasted_iota(jnp.int32, (per_shard, 128), 1)
    per_line = 128 // per_shard
    line = owner[:, pl.ds(pl.multiple_of(me // per_line * 128, 128), 128)]
    mine = pltpu.roll(
        jnp.broadcast_to(line, (per_shard, 128)), lax.rem(128 - lax.rem(me, per_line) * per_shard, 128), 1
    )
    names = jnp.sum(jnp.where(row == lane, mine, 0), axis=1, keepdims=True)
    ranks = jnp.sum(jnp.where((names == mine) & (lane < row), 1, 0), axis=1, keepdims=True)
    found = jnp.where(2 * names + ranks == lane, row - per_shard, 0)
    idx_v[...] = per_shard + jnp.sum(found, axis=0, keepdims=True)
    to_scalars = pltpu.make_async_copy(idx_v, idx, idx_sem)
    to_scalars.start()
    for kind in range(7):

        def load_left(pos, carry):
            pltpu.make_async_copy(
                left_hbm.at[slot_of(kind, pos)], left_v.at[z, pos], left_sems.at[pos // per_ring]
            ).start()
            return carry

        lax.fori_loop(START[kind], START[kind + 1], load_left, 0)
    for load in loads[1:]:
        load.start()
    grads_v[per_shard] = jnp.zeros((order, order), jnp.bfloat16)
    to_scalars.wait()
    loads[0].wait()
    pl.semaphore_wait(barrier, len(near) + N_Z - 1)

    def pack(half, first, places, into):
        for i in places:
            p = along(half, first, *PACKED[i])
            into[i] = grads_v[idx[0, 2 * p + half]]

    count = [0]

    def message(src, dst, target, plane=z):
        n = count[0]
        count[0] += 1
        return pltpu.make_async_remote_copy(
            src_ref=src, dst_ref=dst, send_sem=send_sems.at[n], recv_sem=recv_sems.at[n],
            device_id=(target, plane), device_id_type=MESH,
        )

    def place(kind, g):
        n = 1 if kind in (NEAR_LONG, AWAY_LONG, BESIDE_LONG) else 3
        return recv_v.at[pl.ds(START[kind] + n * g, n)]

    parity = lax.rem(z, 2)
    half_rows = pl.ds(pl.multiple_of(parity * (order // 2), order // 2), order // 2)
    other_rows = pl.ds(pl.multiple_of((1 - parity) * (order // 2), order // 2), order // 2)
    pieces = (pl.ds(0, 3), pl.ds(3, 1))
    via, straight, onward = {}, {}, {}
    far, ahead, inside, passed, own, swap, swapped = {}, {}, {}, {}, {}, {}, {}
    for h in range(2):
        for part, sign in enumerate(SIGNS):
            there = along(h, sign, 0, 0)
            straight[h, part] = message(out_v.at[h, part], stage_v.at[h, 2 * part], there)
            via[h, 0, part] = message(out_v.at[h, 2, FULL[part]], pass_v.at[h, part, pl.ds(0, 3)], there)
            onward[h, 0, part] = message(pass_v.at[h, part, pl.ds(0, 3)], stage_v.at[h, 3, FULL[part]], there)
            via[h, 1, part] = message(
                out_v.at[h, 2, 3 + part, half_rows], pass_v.at[h, part, 3, half_rows], there
            )
            onward[h, 1, part] = message(
                pass_v.at[h, part, 3, half_rows], stage_v.at[h, 3, 3 + part, half_rows], there
            )
            there = along(h, 0, sign, 0)
            last = along(h, 0, sign, part)
            far[h, 0, part] = message(
                stage_v.at[h, pieces[0], 3 + part], relay_v.at[h, part, pieces[0]], there
            )
            passed[h, 0, part] = message(relay_v.at[h, part, pieces[0]], place(AWAY, h * 2 + part), last)
            far[h, 1, part] = message(
                stage_v.at[h, 3, 3 + part, half_rows], relay_v.at[h, part, 3, half_rows], there
            )
            passed[h, 1, part] = message(
                relay_v.at[h, part, 3, half_rows], recv_v.at[START[AWAY_LONG] + h * 2 + part, half_rows], last
            )
            for m, piece in enumerate(pieces):
                for dc in range(N_C):
                    ahead[h, m, part, dc] = message(
                        stage_v.at[h, piece, PACKED.index((sign % 4, dc))],
                        place((BESIDE, BESIDE_CROSS)[dc], h * 2 + part) if m == 0 else place(BESIDE_LONG, dc * 4 + h * 2 + part),
                        along(h, 0, sign, dc),
                    )
        for m, piece in enumerate(pieces):
            inside[h, m] = message(stage_v.at[h, piece, 1], place((NEAR, NEAR_LONG)[m], h * 2 + 1), at(0, 0, 1))
            own[h, m] = pltpu.make_async_copy(stage_v.at[h, piece, 0], place((NEAR, NEAR_LONG)[m], h * 2), own_sems.at[h, m])
        step = (1 - 2 * parity) * (1 - 2 * h)
        plane = lax.rem(z + step + N_Z, N_Z)
        both = pl.ds(START[AWAY_LONG] + h * 2, 2)
        swap[h] = message(recv_v.at[both, half_rows], recv_v.at[both, half_rows], me, plane)
        swapped[h] = pltpu.make_async_remote_copy(
            src_ref=recv_v.at[both, other_rows], dst_ref=recv_v.at[both, other_rows],
            send_sem=send_sems.at[count[0] - 1], recv_sem=recv_sems.at[count[0] - 1],
            device_id=(me, plane), device_id_type=MESH,
        )

    def ring(part, t, chunk, source):
        piece = left_v.at[source, pl.ds(chunk * per_ring, per_ring)]
        return pltpu.make_async_remote_copy(
            src_ref=piece, dst_ref=piece,
            send_sem=ring_send.at[part, t, chunk], recv_sem=ring_recv.at[part, t, chunk],
            device_id=(me, lax.rem(z + SIGNS[part] + N_Z, N_Z)), device_id_type=MESH,
        )

    def ring_out(part, t, chunk):
        return ring(part, t, chunk, lax.rem(z - SIGNS[part] * t + N_Z, N_Z))

    def ring_in(part, t, chunk):
        return ring(part, t, chunk, lax.rem(z - SIGNS[part] * (t + 1) + N_Z, N_Z))

    def travels(part, t, chunk):
        return t < 3 or chunk % 2 == part

    def pass_on(t, *chunks):
        for chunk in chunks:
            for part in range(2):
                if travels(part, t, chunk):
                    ring_in(part, t, chunk).wait_recv()
                if t < 3 and travels(part, t + 1, chunk):
                    ring_out(part, t + 1, chunk).start()

    def begin(chunk):
        for part in range(2):
            ring_out(part, 0, chunk).start()

    rows = pl.ds(pl.multiple_of(z * share, share), share)

    def fold(values):
        values = values[:, :128] + values[:, 128:]
        return jnp.sum(values.reshape(values.shape[0] // 8, 8, 128), axis=0)

    def in_fours(kind, some):
        def one(i, carry):
            places = [START[kind] + 4 * i + j for j in range(4)]
            some(places, [slot_of(kind, pos) for pos in places])
            return carry

        lax.fori_loop(0, (START[kind + 1] - START[kind]) // 4, one, 0)

    def absorb(kind):
        def some(places, ks):
            for pos, k in zip(places, ks):
                grad32 = recv_v[pos, rows, :].astype(jnp.float32)
                moment_one = 0.9 * mone_v[k] + 0.1 * grad32
                moment_two = 0.999 * mtwo_v[k] + 0.001 * grad32 * grad32
                ratio = moment_one / (jnp.sqrt(moment_two) + 1e-08)
                adam_v[k] = fold(ratio * ratio)
            for pos, k in zip(places, ks):
                product = jnp.dot(recv_v[pos], right_v[k], preferred_element_type=jnp.float32)
                recv_v[pos] = product.astype(jnp.bfloat16)

        in_fours(kind, some)

    def finish(kind):
        def some(places, ks):
            for pos, k in zip(places, ks):
                precond = jnp.dot(
                    left_v[:, pos].reshape(order, order), recv_v[pos], preferred_element_type=jnp.float32
                )
                square_v[k] = fold(precond * precond)
                recv_v[pos] = precond.astype(jnp.bfloat16)

        in_fours(kind, some)

    def count_live():
        shard = lax.broadcasted_iota(jnp.int32, (owner.shape[1], 128), 0) // per_shard
        slot = lax.broadcasted_iota(jnp.int32, (owner.shape[1], 128), 1)
        ours = jnp.broadcast_to(jnp.where(owner[...] == me, 1.0, 0.0), (8, owner.shape[1]))
        counts = jnp.dot(
            ours.astype(jnp.bfloat16),
            jnp.where(shard == slot // 2, 1.0, 0.0).astype(jnp.bfloat16),
            preferred_element_type=jnp.float32,
        )[:1]
        rank = lax.rem(slot[:1], 2).astype(jnp.float32)
        live_v[...] = jnp.where(counts > rank, 1.0, 0.0)

    def by_lane(sums):
        by_slot = jnp.sum(jnp.sum(sums, axis=1), axis=1, keepdims=True)
        spread = jnp.broadcast_to(by_slot, (slots, 128))
        return jnp.sum(jnp.where(diagonal, spread, 0.0), axis=0, keepdims=True)

    diagonal = lax.broadcasted_iota(jnp.int32, (slots, 128), 0) == lax.broadcasted_iota(
        jnp.int32, (slots, 128), 1
    )

    every = [(h, part) for h in range(2) for part in range(2)]
    for h, part in every:
        pack(h, 2, (3 + part,), out_v.at[h, 2])
        via[h, 1, part].start()
    for h, part in every:
        pack(h, 2, ((0, 1, 2), (5, 6, 7))[part], out_v.at[h, 2])
        via[h, 0, part].start()
    for chunk in range(RING):
        first = pl.ds(chunk * per_ring, per_ring)
        pltpu.make_async_copy(left_hbm.at[first], left_v.at[z, first], left_sems.at[chunk]).wait()
        begin(chunk)
    for h, part in every:
        pack(h, SIGNS[part], range(8), out_v.at[h, part])
        straight[h, part].start()
    for h, part in every:
        via[h, 1, part].wait_recv()
        onward[h, 1, part].start()
    for h in range(2):
        pack(h, 0, range(8), stage_v.at[h, 1])

    for h, part in every:
        via[h, 0, part].wait_recv()
        onward[h, 0, part].start()
    for h, part in every:
        onward[h, 1, part].wait_recv()
        far[h, 1, part].start()
    count_live()
    pass_on(0, 0, 1, 2, 3)
    for h, part in every:
        far[h, 1, part].wait_recv()
        passed[h, 1, part].start()
    for h, part in every:
        straight[h, part].wait_recv()
    for h, part in every:
        far[h, 0, part].start()
    for h, part in every:
        ahead[h, 0, part, 0].start()
    for h in range(2):
        inside[h, 0].start()
        own[h, 0].start()
    for h in range(2):
        for part in range(2):
            passed[h, 1, part].wait_recv()
        swap[h].start()
    pass_on(1, 0, 1, 2, 3)
    for h, part in every:
        onward[h, 0, part].wait_recv()
    for h in range(2):
        inside[h, 1].start()
        own[h, 1].start()
    for load in loads[1:]:
        load.wait()
    for m in range(2):
        for h in range(2):
            own[h, m].wait()
            inside[h, m].wait_recv()
    absorb(NEAR)
    for h, part in every:
        far[h, 0, part].wait_recv()
        passed[h, 0, part].start()
    for h, part in every:
        ahead[h, 0, part, 0].wait_recv()
    for h, part in every:
        ahead[h, 0, part, 1].start()
    for h in range(2):
        swapped[h].wait_recv()
        swap[h].wait_send()
    absorb(NEAR_LONG)
    absorb(AWAY_LONG)
    absorb(BESIDE)
    pass_on(2, 0, 1, 2, 3)
    for h, part in every:
        passed[h, 0, part].wait_recv()
    for dc in range(N_C):
        for h, part in every:
            ahead[h, 1, part, dc].start()
    absorb(AWAY)
    for h, part in every:
        ahead[h, 0, part, 1].wait_recv()
    absorb(BESIDE_CROSS)
    pass_on(3, 0, 1)
    for kind in (NEAR, NEAR_LONG, BESIDE, AWAY_LONG):
        finish(kind)
    for dc in range(N_C):
        for h, part in every:
            ahead[h, 1, part, dc].wait_recv()
    absorb(BESIDE_LONG)

    tiles_v[0] = jnp.broadcast_to(by_lane(adam_v[...]), (8, 128))

    def tell(dz):
        return pltpu.make_async_remote_copy(
            src_ref=tiles_v.at[0],
            dst_ref=tiles_v.at[dz],
            send_sem=zsend.at[dz],
            recv_sem=zrecv.at[dz],
            device_id=(me, lax.rem(z + dz, N_Z)),
            device_id_type=MESH,
        )

    for dz in range(1, N_Z):
        tell(dz).start()
    pass_on(3, 2, 3)
    for kind in (AWAY, BESIDE_CROSS, BESIDE_LONG):
        finish(kind)
    sum_pre = by_lane(square_v[...])
    for group in (via, straight, onward, far, ahead, inside, passed):
        for copy in group.values():
            copy.wait_send()
    for t in range(4):
        for chunk in range(RING):
            for part in range(2):
                if travels(part, t, chunk):
                    ring_out(part, t, chunk).wait_send()
    for dz in range(1, N_Z):
        tell(dz).wait()
    sum_adam = jnp.sum(tiles_v[...], axis=0)[:1]
    scale = live_v[...] * (jnp.sqrt(sum_adam / total) / jnp.sqrt(sum_pre / total + 1e-06))
    by_row = jnp.where(diagonal, jnp.broadcast_to(scale, (slots, 128)), 0.0)
    scale_out[...] = jnp.broadcast_to(jnp.sum(by_row, axis=1, keepdims=True), (slots, 128))


def step(owner, grads, left, right, mone, mtwo):
    per_shard, order, _ = grads.shape
    slots, share, _ = mone.shape
    block = (order, order)
    anywhere = pl.BlockSpec(memory_space=pl.ANY)
    vmem = pl.BlockSpec(memory_space=pltpu.VMEM)
    dma = pltpu.SemaphoreType.DMA
    return pl.pallas_call(
        step_kernel,
        out_shape=(
            pltpu.VMEM((slots, *block), jnp.bfloat16),
            pltpu.VMEM((slots, 128), jnp.float32),
        ),
        in_specs=[vmem] + [anywhere] * 5,
        out_specs=(vmem, vmem),
        scratch_shapes=[
            pltpu.VMEM((per_shard + 1, *block), jnp.bfloat16),
            pltpu.VMEM((2, 3, 8, *block), jnp.bfloat16),
            pltpu.VMEM((2, 4, 8, *block), jnp.bfloat16),
            pltpu.VMEM((2, 2, 4, *block), jnp.bfloat16),
            pltpu.VMEM((2, 2, 4, *block), jnp.bfloat16),
            pltpu.VMEM((N_Z, slots, share, order), jnp.bfloat16),
            pltpu.VMEM((slots, *block), jnp.bfloat16),
            pltpu.VMEM((slots, share, order), jnp.float32),
            pltpu.VMEM((slots, share, order), jnp.float32),
            pltpu.VMEM((slots, 8, 128), jnp.float32),
            pltpu.VMEM((slots, 8, 128), jnp.float32),
            pltpu.VMEM((N_Z, 8, 128), jnp.float32),
            pltpu.VMEM((1, 128), jnp.float32),
            pltpu.VMEM((1, 128), jnp.int32),
            pltpu.SMEM((1, 128), jnp.int32),
            dma((4,)),
            dma((RING,)),
            dma((2, 2)),
            dma,
            dma((58,)),
            dma((58,)),
            dma((2, 4, RING)),
            dma((2, 4, RING)),
            dma((N_Z,)),
            dma((N_Z,)),
        ],
        compiler_params=pltpu.CompilerParams(
            collective_id=0, has_side_effects=True, vmem_limit_bytes=LIMIT * 2**20
        ),
        cost_estimate=pl.CostEstimate(
            flops=4 * slots * order**3, bytes_accessed=4 * 10**8, transcendentals=10**6
        ),
    )(owner, grads, left, right, mone, mtwo)


def place_of(me, slot):
    y, x, c = me // (N_X * N_C), (me // N_C) % N_X, me % N_C
    source, half = slot // 2, lax.rem(slot, 2)
    dy = lax.rem(source // (N_X * N_C) - y + N_Y, N_Y)
    dx = lax.rem(lax.rem(source // N_C, N_X) - x + N_X, N_X)
    dc = lax.rem(source + c, N_C)
    first, second = dx + half * (dy - dx), dy + half * (dx - dy)
    d = lax.rem(first + 1, 4)
    g, beside = half * 2 + dc, half * 2 + (3 - second) // 2
    near = jnp.where(d == 3, START[NEAR_LONG] + g, START[NEAR] + 3 * g + d)
    away = jnp.where(d == 3, START[AWAY_LONG] + g, START[AWAY] + 3 * g + d)
    cross = START[BESIDE] + dc * (START[BESIDE_CROSS] - START[BESIDE])
    middle = jnp.where(d == 3, START[BESIDE_LONG] + dc * 4 + beside, cross + 3 * beside + d)
    return jnp.where(second == 0, near, jnp.where(second == 2, away, middle))


def scale_kernel(x, scale, out, ready, sems):
    me = lax.axis_index("dp")

    def copy(i):
        some = pl.ds(GROUP * i, GROUP)
        return pltpu.make_async_copy(ready.at[some], out.at[some], sems.at[i])

    def one(i, carry):
        for j in range(GROUP):
            k = GROUP * i + j
            row = scale[pl.ds(k, 1), :]
            factor = jnp.concatenate([row, row], axis=1)
            ready[k] = (x[place_of(me, k)].astype(jnp.float32) * factor).astype(jnp.bfloat16)
        copy(i).start()
        return carry

    def settle(i, carry):
        copy(i).wait()
        return carry

    steps = x.shape[0] // GROUP
    lax.fori_loop(0, steps, one, 0)
    lax.fori_loop(0, steps, settle, 0)


def apply_scale(x, scale):
    vmem = pl.BlockSpec(memory_space=pltpu.VMEM)
    return pl.pallas_call(
        scale_kernel,
        out_shape=jax.ShapeDtypeStruct(x.shape, jnp.bfloat16),
        in_specs=[vmem, vmem],
        out_specs=pl.BlockSpec(memory_space=pl.ANY),
        scratch_shapes=[
            pltpu.VMEM(x.shape, jnp.bfloat16),
            pltpu.SemaphoreType.DMA((x.shape[0] // GROUP,)),
        ],
        compiler_params=pltpu.CompilerParams(vmem_limit_bytes=24 * 2**20),
    )(x, scale)


def per_device(grads, owner, left_root, right_root, first_moment, second_moment):
    x, scale = step(
        owner.reshape(1, -1), grads, left_root[0], right_root[0], first_moment[0], second_moment[0]
    )
    return apply_scale(x, scale)[None]


def solution(mesh):
    placed = (
        P("dp", None, None),
        P(),
        P("dp", None, "replica", None),
        P("dp", None, None, None),
        P("dp", None, "replica", None),
        P("dp", None, "replica", None),
    )
    return jax.shard_map(
        per_device, mesh=mesh, in_specs=placed, out_specs=P("dp", None, None, None), check_vma=False
    )
```

```python
import functools

import jax
import jax.numpy as jnp
from jax import lax
from jax.experimental import pallas as pl
from jax.experimental.pallas import tpu as pltpu
from jax.sharding import PartitionSpec as P

MESH = pl.DeviceIdType.MESH
N_Y, N_X, N_C = 4, 4, 2
N_DP = N_Y * N_X * N_C
N_Z = 8
GROUP = 4
RING = 4
SIGNS = (1, -1)
LIMIT = 50

NEAR, NEAR_LONG, BESIDE, AWAY_LONG, AWAY, BESIDE_CROSS, BESIDE_LONG = range(7)
START = (0, 12, 16, 28, 32, 44, 56, 64)
PACKED = ((0, 0), (0, 1), (1, 0), (2, 0), (2, 1), (1, 1), (3, 0), (3, 1))
FULL = (pl.ds(0, 3), pl.ds(5, 3))


def decode(kind, q):
    long = kind in (NEAR_LONG, AWAY_LONG, BESIDE_LONG)
    d, g = (3, q) if long else (lax.rem(q, 3), q // 3)
    first, low = lax.rem(d + 3, 4), lax.rem(g, 2)
    if kind in (NEAR, NEAR_LONG):
        return g // 2, first, 0, low
    if kind in (AWAY, AWAY_LONG):
        return g // 2, first, 2, low
    return lax.rem(g // 2, 2), first, 3 - 2 * low, g // 4 if kind == BESIDE_LONG else int(kind == BESIDE_CROSS)


def step_kernel(
    owner, grads_hbm, left_hbm, right_hbm, mone_hbm, mtwo_hbm, recv_v, scale_out,
    grads_v, out_v, stage_v, pass_v, relay_v, left_v, right_v, mone_v, mtwo_v,
    adam_v, square_v, tiles_v, live_v, idx_v, idx,
    load_sems, left_sems, own_sems, idx_sem, send_sems, recv_sems, ring_send, ring_recv, zsend, zrecv,
):
    me, z = lax.axis_index("dp"), lax.axis_index("replica")
    per_shard, order = grads_hbm.shape[0], grads_hbm.shape[1]
    slots, share = mone_hbm.shape[0], mone_hbm.shape[1]
    total = float(order * order)
    per_ring = slots // RING
    y, x, c = me // (N_X * N_C), (me // N_C) % N_X, me % N_C

    def at(dy, dx, dc):
        return (
            lax.rem(y + dy + N_Y, N_Y) * (N_X * N_C) + lax.rem(x + dx + N_X, N_X) * N_C + lax.rem(c + dc, N_C)
        )

    def along(half, first, second, dc):
        return at(second + half * (first - second), first + half * (second - first), dc)

    def slot_of(kind, pos):
        half, first, second, dc = decode(kind, pos - START[kind])
        return 2 * along(half, first, second, dc) + half

    barrier = pltpu.get_barrier_semaphore()
    near = [(0, 0, 1)] + [(dy, dx, dc) for dy, dx in ((0, 1), (0, -1), (1, 0), (-1, 0)) for dc in range(N_C)]
    for step in near:
        pl.semaphore_signal(barrier, inc=1, device_id=(at(*step), z), device_id_type=MESH)
    for dz in range(1, N_Z):
        pl.semaphore_signal(barrier, inc=1, device_id=(me, lax.rem(z + dz, N_Z)), device_id_type=MESH)

    loads = [
        pltpu.make_async_copy(grads_hbm, grads_v.at[pl.ds(0, per_shard)], load_sems.at[0]),
        pltpu.make_async_copy(mone_hbm, mone_v, load_sems.at[1]),
        pltpu.make_async_copy(mtwo_hbm, mtwo_v, load_sems.at[2]),
        pltpu.make_async_copy(right_hbm, right_v, load_sems.at[3]),
    ]
    loads[0].start()
    row = lax.broadcasted_iota(jnp.int32, (per_shard, 128), 0)
    lane = lax.broadcasted_iota(jnp.int32, (per_shard, 128), 1)
    per_line = 128 // per_shard
    line = owner[:, pl.ds(pl.multiple_of(me // per_line * 128, 128), 128)]
    mine = pltpu.roll(
        jnp.broadcast_to(line, (per_shard, 128)), lax.rem(128 - lax.rem(me, per_line) * per_shard, 128), 1
    )
    names = jnp.sum(jnp.where(row == lane, mine, 0), axis=1, keepdims=True)
    ranks = jnp.sum(jnp.where((names == mine) & (lane < row), 1, 0), axis=1, keepdims=True)
    found = jnp.where(2 * names + ranks == lane, row - per_shard, 0)
    idx_v[...] = per_shard + jnp.sum(found, axis=0, keepdims=True)
    to_scalars = pltpu.make_async_copy(idx_v, idx, idx_sem)
    to_scalars.start()
    for kind in range(7):

        def load_left(pos, carry):
            pltpu.make_async_copy(
                left_hbm.at[slot_of(kind, pos)], left_v.at[z, pos], left_sems.at[pos // per_ring]
            ).start()
            return carry

        lax.fori_loop(START[kind], START[kind + 1], load_left, 0)
    for load in loads[1:]:
        load.start()
    grads_v[per_shard] = jnp.zeros((order, order), jnp.bfloat16)
    to_scalars.wait()
    loads[0].wait()
    pl.semaphore_wait(barrier, len(near) + N_Z - 1)

    def pack(half, first, places, into):
        for i in places:
            p = along(half, first, *PACKED[i])
            into[i] = grads_v[idx[0, 2 * p + half]]

    count = [0]

    def message(src, dst, target, plane=z):
        n = count[0]
        count[0] += 1
        return pltpu.make_async_remote_copy(
            src_ref=src, dst_ref=dst, send_sem=send_sems.at[n], recv_sem=recv_sems.at[n],
            device_id=(target, plane), device_id_type=MESH,
        )

    def place(kind, g):
        n = 1 if kind in (NEAR_LONG, AWAY_LONG, BESIDE_LONG) else 3
        return recv_v.at[pl.ds(START[kind] + n * g, n)]

    parity = lax.rem(z, 2)
    half_rows = pl.ds(pl.multiple_of(parity * (order // 2), order // 2), order // 2)
    other_rows = pl.ds(pl.multiple_of((1 - parity) * (order // 2), order // 2), order // 2)
    pieces = (pl.ds(0, 3), pl.ds(3, 1))
    via, straight, onward = {}, {}, {}
    far, ahead, inside, passed, own, swap, swapped = {}, {}, {}, {}, {}, {}, {}
    for h in range(2):
        for part, sign in enumerate(SIGNS):
            there = along(h, sign, 0, 0)
            for b, some in enumerate((*FULL, pl.ds(3, 2))):
                straight[h, b, part] = message(out_v.at[h, part, some], stage_v.at[h, 2 * part, some], there)
            via[h, 0, part] = message(out_v.at[h, 2, FULL[part]], pass_v.at[h, part, pl.ds(0, 3)], there)
            onward[h, 0, part] = message(pass_v.at[h, part, pl.ds(0, 3)], stage_v.at[h, 3, FULL[part]], there)
            via[h, 1, part] = message(
                out_v.at[h, 2, 3 + part, half_rows], pass_v.at[h, part, 3, half_rows], there
            )
            onward[h, 1, part] = message(
                pass_v.at[h, part, 3, half_rows], stage_v.at[h, 3, 3 + part, half_rows], there
            )
            there = along(h, 0, sign, 0)
            last = along(h, 0, sign, part)
            far[h, 0, part] = message(
                stage_v.at[h, pieces[0], 3 + part], relay_v.at[h, part, pieces[0]], there
            )
            passed[h, 0, part] = message(relay_v.at[h, part, pieces[0]], place(AWAY, h * 2 + part), last)
            far[h, 1, part] = message(
                stage_v.at[h, 3, 3 + part, half_rows], relay_v.at[h, part, 3, half_rows], there
            )
            passed[h, 1, part] = message(
                relay_v.at[h, part, 3, half_rows], recv_v.at[START[AWAY_LONG] + h * 2 + part, half_rows], last
            )
            for m, piece in enumerate(pieces):
                for dc in range(N_C):
                    ahead[h, m, part, dc] = message(
                        stage_v.at[h, piece, PACKED.index((sign % 4, dc))],
                        place((BESIDE, BESIDE_CROSS)[dc], h * 2 + part) if m == 0 else place(BESIDE_LONG, dc * 4 + h * 2 + part),
                        along(h, 0, sign, dc),
                    )
        for m, piece in enumerate(pieces):
            inside[h, m] = message(stage_v.at[h, piece, 1], place((NEAR, NEAR_LONG)[m], h * 2 + 1), at(0, 0, 1))
            own[h, m] = pltpu.make_async_copy(stage_v.at[h, piece, 0], place((NEAR, NEAR_LONG)[m], h * 2), own_sems.at[h, m])
        step = (1 - 2 * parity) * (1 - 2 * h)
        plane = lax.rem(z + step + N_Z, N_Z)
        both = pl.ds(START[AWAY_LONG] + h * 2, 2)
        swap[h] = message(recv_v.at[both, half_rows], recv_v.at[both, half_rows], me, plane)
        swapped[h] = pltpu.make_async_remote_copy(
            src_ref=recv_v.at[both, other_rows], dst_ref=recv_v.at[both, other_rows],
            send_sem=send_sems.at[count[0] - 1], recv_sem=recv_sems.at[count[0] - 1],
            device_id=(me, plane), device_id_type=MESH,
        )

    def ring(part, t, chunk, source):
        piece = left_v.at[source, pl.ds(chunk * per_ring, per_ring)]
        return pltpu.make_async_remote_copy(
            src_ref=piece, dst_ref=piece,
            send_sem=ring_send.at[part, t, chunk], recv_sem=ring_recv.at[part, t, chunk],
            device_id=(me, lax.rem(z + SIGNS[part] + N_Z, N_Z)), device_id_type=MESH,
        )

    def ring_out(part, t, chunk):
        return ring(part, t, chunk, lax.rem(z - SIGNS[part] * t + N_Z, N_Z))

    def ring_in(part, t, chunk):
        return ring(part, t, chunk, lax.rem(z - SIGNS[part] * (t + 1) + N_Z, N_Z))

    def travels(part, t, chunk):
        return t < 3 or chunk % 2 == part

    def pass_on(t, *chunks):
        for chunk in chunks:
            for part in range(2):
                if travels(part, t, chunk):
                    ring_in(part, t, chunk).wait_recv()
                if t < 3 and travels(part, t + 1, chunk):
                    ring_out(part, t + 1, chunk).start()

    def begin(chunk):
        for part in range(2):
            ring_out(part, 0, chunk).start()

    rows = pl.ds(pl.multiple_of(z * share, share), share)

    def fold(values):
        values = values[:, :128] + values[:, 128:]
        return jnp.sum(values.reshape(values.shape[0] // 8, 8, 128), axis=0)

    def in_fours(kind, some):
        def one(i, carry):
            places = [START[kind] + 4 * i + j for j in range(4)]
            some(places, [slot_of(kind, pos) for pos in places])
            return carry

        lax.fori_loop(0, (START[kind + 1] - START[kind]) // 4, one, 0)

    def absorb(kind):
        def some(places, ks):
            for pos, k in zip(places, ks):
                grad32 = recv_v[pos, rows, :].astype(jnp.float32)
                moment_one = 0.9 * mone_v[k] + 0.1 * grad32
                moment_two = 0.999 * mtwo_v[k] + 0.001 * grad32 * grad32
                ratio = moment_one / (jnp.sqrt(moment_two) + 1e-08)
                adam_v[k] = fold(ratio * ratio)
            for pos, k in zip(places, ks):
                product = jnp.dot(recv_v[pos], right_v[k], preferred_element_type=jnp.float32)
                recv_v[pos] = product.astype(jnp.bfloat16)

        in_fours(kind, some)

    def finish(kind):
        def some(places, ks):
            for pos, k in zip(places, ks):
                precond = jnp.dot(
                    left_v[:, pos].reshape(order, order), recv_v[pos], preferred_element_type=jnp.float32
                )
                square_v[k] = fold(precond * precond)
                recv_v[pos] = precond.astype(jnp.bfloat16)

        in_fours(kind, some)

    def count_live():
        shard = lax.broadcasted_iota(jnp.int32, (owner.shape[1], 128), 0) // per_shard
        slot = lax.broadcasted_iota(jnp.int32, (owner.shape[1], 128), 1)
        ours = jnp.broadcast_to(jnp.where(owner[...] == me, 1.0, 0.0), (8, owner.shape[1]))
        counts = jnp.dot(
            ours.astype(jnp.bfloat16),
            jnp.where(shard == slot // 2, 1.0, 0.0).astype(jnp.bfloat16),
            preferred_element_type=jnp.float32,
        )[:1]
        rank = lax.rem(slot[:1], 2).astype(jnp.float32)
        live_v[...] = jnp.where(counts > rank, 1.0, 0.0)

    def by_lane(sums):
        by_slot = jnp.sum(jnp.sum(sums, axis=1), axis=1, keepdims=True)
        spread = jnp.broadcast_to(by_slot, (slots, 128))
        return jnp.sum(jnp.where(diagonal, spread, 0.0), axis=0, keepdims=True)

    diagonal = lax.broadcasted_iota(jnp.int32, (slots, 128), 0) == lax.broadcasted_iota(
        jnp.int32, (slots, 128), 1
    )

    every = [(h, part) for h in range(2) for part in range(2)]
    thirds = ((0, 1, 2), (5, 6, 7), (3, 4))

    def ready(chunk):
        first = pl.ds(chunk * per_ring, per_ring)
        pltpu.make_async_copy(left_hbm.at[first], left_v.at[z, first], left_sems.at[chunk]).wait()
        begin(chunk)

    for h, part in every:
        pack(h, 2, (3 + part,), out_v.at[h, 2])
        via[h, 1, part].start()
    for h, part in every:
        pack(h, SIGNS[part], thirds[2], out_v.at[h, part])
        straight[h, 2, part].start()
    for h, part in every:
        pack(h, 2, thirds[part], out_v.at[h, 2])
        via[h, 0, part].start()
    ready(0)
    ready(1)
    for h in range(2):
        pack(h, 0, thirds[2], stage_v.at[h, 1])
    for h, part in every:
        via[h, 1, part].wait_recv()
        onward[h, 1, part].start()
    for h, part in every:
        for b in range(2):
            pack(h, SIGNS[part], thirds[b], out_v.at[h, part])
            straight[h, b, part].start()
    ready(2)
    ready(3)
    for h in range(2):
        for b in range(2):
            pack(h, 0, thirds[b], stage_v.at[h, 1])
    count_live()

    for h, part in every:
        straight[h, 2, part].wait_recv()
    for h, part in every:
        far[h, 0, part].start()
    for h, part in every:
        onward[h, 1, part].wait_recv()
        far[h, 1, part].start()
    for h, part in every:
        via[h, 0, part].wait_recv()
        onward[h, 0, part].start()
    pass_on(0, 0, 1)
    for h, part in every:
        far[h, 1, part].wait_recv()
        passed[h, 1, part].start()
    pass_on(0, 2, 3)
    for h in range(2):
        for part in range(2):
            passed[h, 1, part].wait_recv()
        swap[h].start()
    for h, part in every:
        far[h, 0, part].wait_recv()
        passed[h, 0, part].start()
    for h, part in every:
        for b in range(2):
            straight[h, b, part].wait_recv()
    for h, part in every:
        ahead[h, 0, part, 0].start()
    for h in range(2):
        inside[h, 0].start()
        own[h, 0].start()
    pass_on(1, 0, 1)
    for h, part in every:
        onward[h, 0, part].wait_recv()
    for h in range(2):
        inside[h, 1].start()
        own[h, 1].start()
    for load in loads[1:]:
        load.wait()
    for m in range(2):
        for h in range(2):
            own[h, m].wait()
            inside[h, m].wait_recv()
    absorb(NEAR)
    for h, part in every:
        ahead[h, 0, part, 1].start()
    pass_on(1, 2, 3)
    absorb(NEAR_LONG)
    for h in range(2):
        swapped[h].wait_recv()
        swap[h].wait_send()
    absorb(AWAY_LONG)
    for h, part in every:
        ahead[h, 0, part, 0].wait_recv()
    for dc in range(N_C):
        for h, part in every:
            ahead[h, 1, part, dc].start()
    absorb(BESIDE)
    pass_on(2, 0, 1)
    for h, part in every:
        passed[h, 0, part].wait_recv()
    absorb(AWAY)
    pass_on(2, 2, 3)
    for h, part in every:
        ahead[h, 0, part, 1].wait_recv()
    absorb(BESIDE_CROSS)
    for dc in range(N_C):
        for h, part in every:
            ahead[h, 1, part, dc].wait_recv()
    absorb(BESIDE_LONG)

    tiles_v[0] = jnp.broadcast_to(by_lane(adam_v[...]), (8, 128))

    def tell(dz):
        return pltpu.make_async_remote_copy(
            src_ref=tiles_v.at[0],
            dst_ref=tiles_v.at[dz],
            send_sem=zsend.at[dz],
            recv_sem=zrecv.at[dz],
            device_id=(me, lax.rem(z + dz, N_Z)),
            device_id_type=MESH,
        )

    for dz in range(1, N_Z):
        tell(dz).start()
    pass_on(3, 0, 1)
    for kind in (NEAR, NEAR_LONG, BESIDE, AWAY_LONG):
        finish(kind)
    pass_on(3, 2)
    finish(AWAY)
    pass_on(3, 3)
    for kind in (BESIDE_CROSS, BESIDE_LONG):
        finish(kind)
    sum_pre = by_lane(square_v[...])
    for group in (via, straight, onward, far, ahead, inside, passed):
        for copy in group.values():
            copy.wait_send()
    for t in range(4):
        for chunk in range(RING):
            for part in range(2):
                if travels(part, t, chunk):
                    ring_out(part, t, chunk).wait_send()
    for dz in range(1, N_Z):
        tell(dz).wait()
    sum_adam = jnp.sum(tiles_v[...], axis=0)[:1]
    scale = live_v[...] * (jnp.sqrt(sum_adam / total) / jnp.sqrt(sum_pre / total + 1e-06))
    by_row = jnp.where(diagonal, jnp.broadcast_to(scale, (slots, 128)), 0.0)
    scale_out[...] = jnp.broadcast_to(jnp.sum(by_row, axis=1, keepdims=True), (slots, 128))


def step(owner, grads, left, right, mone, mtwo):
    per_shard, order, _ = grads.shape
    slots, share, _ = mone.shape
    block = (order, order)
    anywhere = pl.BlockSpec(memory_space=pl.ANY)
    vmem = pl.BlockSpec(memory_space=pltpu.VMEM)
    dma = pltpu.SemaphoreType.DMA
    return pl.pallas_call(
        step_kernel,
        out_shape=(
            pltpu.VMEM((slots, *block), jnp.bfloat16),
            pltpu.VMEM((slots, 128), jnp.float32),
        ),
        in_specs=[vmem] + [anywhere] * 5,
        out_specs=(vmem, vmem),
        scratch_shapes=[
            pltpu.VMEM((per_shard + 1, *block), jnp.bfloat16),
            pltpu.VMEM((2, 3, 8, *block), jnp.bfloat16),
            pltpu.VMEM((2, 4, 8, *block), jnp.bfloat16),
            pltpu.VMEM((2, 2, 4, *block), jnp.bfloat16),
            pltpu.VMEM((2, 2, 4, *block), jnp.bfloat16),
            pltpu.VMEM((N_Z, slots, share, order), jnp.bfloat16),
            pltpu.VMEM((slots, *block), jnp.bfloat16),
            pltpu.VMEM((slots, share, order), jnp.float32),
            pltpu.VMEM((slots, share, order), jnp.float32),
            pltpu.VMEM((slots, 8, 128), jnp.float32),
            pltpu.VMEM((slots, 8, 128), jnp.float32),
            pltpu.VMEM((N_Z, 8, 128), jnp.float32),
            pltpu.VMEM((1, 128), jnp.float32),
            pltpu.VMEM((1, 128), jnp.int32),
            pltpu.SMEM((1, 128), jnp.int32),
            dma((4,)),
            dma((RING,)),
            dma((2, 2)),
            dma,
            dma((66,)),
            dma((66,)),
            dma((2, 4, RING)),
            dma((2, 4, RING)),
            dma((N_Z,)),
            dma((N_Z,)),
        ],
        compiler_params=pltpu.CompilerParams(
            collective_id=0, has_side_effects=True, vmem_limit_bytes=LIMIT * 2**20
        ),
        cost_estimate=pl.CostEstimate(
            flops=4 * slots * order**3, bytes_accessed=4 * 10**8, transcendentals=10**6
        ),
    )(owner, grads, left, right, mone, mtwo)


def place_of(me, slot):
    y, x, c = me // (N_X * N_C), (me // N_C) % N_X, me % N_C
    source, half = slot // 2, lax.rem(slot, 2)
    dy = lax.rem(source // (N_X * N_C) - y + N_Y, N_Y)
    dx = lax.rem(lax.rem(source // N_C, N_X) - x + N_X, N_X)
    dc = lax.rem(source + c, N_C)
    first, second = dx + half * (dy - dx), dy + half * (dx - dy)
    d = lax.rem(first + 1, 4)
    g, beside = half * 2 + dc, half * 2 + (3 - second) // 2
    near = jnp.where(d == 3, START[NEAR_LONG] + g, START[NEAR] + 3 * g + d)
    away = jnp.where(d == 3, START[AWAY_LONG] + g, START[AWAY] + 3 * g + d)
    cross = START[BESIDE] + dc * (START[BESIDE_CROSS] - START[BESIDE])
    middle = jnp.where(d == 3, START[BESIDE_LONG] + dc * 4 + beside, cross + 3 * beside + d)
    return jnp.where(second == 0, near, jnp.where(second == 2, away, middle))


def scale_kernel(x, scale, out, ready, sems):
    me = lax.axis_index("dp")

    def copy(i):
        some = pl.ds(GROUP * i, GROUP)
        return pltpu.make_async_copy(ready.at[some], out.at[some], sems.at[i])

    def one(i, carry):
        for j in range(GROUP):
            k = GROUP * i + j
            row = scale[pl.ds(k, 1), :]
            factor = jnp.concatenate([row, row], axis=1)
            ready[k] = (x[place_of(me, k)].astype(jnp.float32) * factor).astype(jnp.bfloat16)
        copy(i).start()
        return carry

    def settle(i, carry):
        copy(i).wait()
        return carry

    steps = x.shape[0] // GROUP
    lax.fori_loop(0, steps, one, 0)
    lax.fori_loop(0, steps, settle, 0)


def apply_scale(x, scale):
    vmem = pl.BlockSpec(memory_space=pltpu.VMEM)
    return pl.pallas_call(
        scale_kernel,
        out_shape=jax.ShapeDtypeStruct(x.shape, jnp.bfloat16),
        in_specs=[vmem, vmem],
        out_specs=pl.BlockSpec(memory_space=pl.ANY),
        scratch_shapes=[
            pltpu.VMEM(x.shape, jnp.bfloat16),
            pltpu.SemaphoreType.DMA((x.shape[0] // GROUP,)),
        ],
        compiler_params=pltpu.CompilerParams(vmem_limit_bytes=24 * 2**20),
    )(x, scale)


def per_device(grads, owner, left_root, right_root, first_moment, second_moment):
    x, scale = step(
        owner.reshape(1, -1), grads, left_root[0], right_root[0], first_moment[0], second_moment[0]
    )
    return apply_scale(x, scale)[None]


def solution(mesh):
    placed = (
        P("dp", None, None),
        P(),
        P("dp", None, "replica", None),
        P("dp", None, None, None),
        P("dp", None, "replica", None),
        P("dp", None, "replica", None),
    )
    return jax.shard_map(
        per_device, mesh=mesh, in_specs=placed, out_specs=P("dp", None, None, None), check_vma=False
    )
```

```python
import functools

import jax
import jax.numpy as jnp
from jax import lax
from jax.experimental import pallas as pl
from jax.experimental.pallas import tpu as pltpu
from jax.sharding import PartitionSpec as P

MESH = pl.DeviceIdType.MESH
N_Y, N_X, N_C = 4, 4, 2
N_DP = N_Y * N_X * N_C
N_Z = 8
GROUP = 4
RING = 4
SIGNS = (1, -1)
LIMIT = 50

NEAR, NEAR_LONG, BESIDE, AWAY_LONG, AWAY, BESIDE_CROSS, BESIDE_LONG = range(7)
START = (0, 12, 16, 28, 32, 44, 56, 64)
PACKED = ((0, 0), (0, 1), (1, 0), (2, 0), (2, 1), (1, 1), (3, 0), (3, 1))
FULL = (pl.ds(0, 3), pl.ds(5, 3))


def decode(kind, q):
    long = kind in (NEAR_LONG, AWAY_LONG, BESIDE_LONG)
    d, g = (3, q) if long else (lax.rem(q, 3), q // 3)
    first, low = lax.rem(d + 3, 4), lax.rem(g, 2)
    if kind in (NEAR, NEAR_LONG):
        return g // 2, first, 0, low
    if kind in (AWAY, AWAY_LONG):
        return g // 2, first, 2, low
    return lax.rem(g // 2, 2), first, 3 - 2 * low, g // 4 if kind == BESIDE_LONG else int(kind == BESIDE_CROSS)


def step_kernel(
    owner, grads_hbm, left_hbm, right_hbm, mone_hbm, mtwo_hbm, recv_v, scale_out,
    grads_v, out_v, stage_v, pass_v, relay_v, left_v, right_v, mone_v, mtwo_v,
    adam_v, square_v, tiles_v, live_v, idx_v, idx,
    load_sems, left_sems, own_sems, idx_sem, send_sems, recv_sems, ring_send, ring_recv, zsend, zrecv,
):
    me, z = lax.axis_index("dp"), lax.axis_index("replica")
    per_shard, order = grads_hbm.shape[0], grads_hbm.shape[1]
    slots, share = mone_hbm.shape[0], mone_hbm.shape[1]
    total = float(order * order)
    per_ring = slots // RING
    y, x, c = me // (N_X * N_C), (me // N_C) % N_X, me % N_C

    def at(dy, dx, dc):
        return (
            lax.rem(y + dy + N_Y, N_Y) * (N_X * N_C) + lax.rem(x + dx + N_X, N_X) * N_C + lax.rem(c + dc, N_C)
        )

    def along(half, first, second, dc):
        return at(second + half * (first - second), first + half * (second - first), dc)

    def slot_of(kind, pos):
        half, first, second, dc = decode(kind, pos - START[kind])
        return 2 * along(half, first, second, dc) + half

    barrier = pltpu.get_barrier_semaphore()
    near = [(0, 0, 1)] + [(dy, dx, dc) for dy, dx in ((0, 1), (0, -1), (1, 0), (-1, 0)) for dc in range(N_C)]
    for step in near:
        pl.semaphore_signal(barrier, inc=1, device_id=(at(*step), z), device_id_type=MESH)
    for dz in range(1, N_Z):
        pl.semaphore_signal(barrier, inc=1, device_id=(me, lax.rem(z + dz, N_Z)), device_id_type=MESH)

    loads = [
        pltpu.make_async_copy(grads_hbm, grads_v.at[pl.ds(0, per_shard)], load_sems.at[0]),
        pltpu.make_async_copy(mone_hbm, mone_v, load_sems.at[1]),
        pltpu.make_async_copy(mtwo_hbm, mtwo_v, load_sems.at[2]),
        pltpu.make_async_copy(right_hbm, right_v, load_sems.at[3]),
    ]
    loads[0].start()
    row = lax.broadcasted_iota(jnp.int32, (per_shard, 128), 0)
    lane = lax.broadcasted_iota(jnp.int32, (per_shard, 128), 1)
    per_line = 128 // per_shard
    line = owner[:, pl.ds(pl.multiple_of(me // per_line * 128, 128), 128)]
    mine = pltpu.roll(
        jnp.broadcast_to(line, (per_shard, 128)), lax.rem(128 - lax.rem(me, per_line) * per_shard, 128), 1
    )
    names = jnp.sum(jnp.where(row == lane, mine, 0), axis=1, keepdims=True)
    ranks = jnp.sum(jnp.where((names == mine) & (lane < row), 1, 0), axis=1, keepdims=True)
    found = jnp.where(2 * names + ranks == lane, row - per_shard, 0)
    idx_v[...] = per_shard + jnp.sum(found, axis=0, keepdims=True)
    to_scalars = pltpu.make_async_copy(idx_v, idx, idx_sem)
    to_scalars.start()
    for kind in range(7):

        def load_left(pos, carry):
            pltpu.make_async_copy(
                left_hbm.at[slot_of(kind, pos)], left_v.at[z, pos], left_sems.at[pos // per_ring]
            ).start()
            return carry

        lax.fori_loop(START[kind], START[kind + 1], load_left, 0)
    for load in loads[1:]:
        load.start()
    grads_v[per_shard] = jnp.zeros((order, order), jnp.bfloat16)
    to_scalars.wait()
    loads[0].wait()
    pl.semaphore_wait(barrier, len(near) + N_Z - 1)

    def pack(half, first, places, into):
        for i in places:
            p = along(half, first, *PACKED[i])
            into[i] = grads_v[idx[0, 2 * p + half]]

    count = [0]

    def message(src, dst, target, plane=z):
        n = count[0]
        count[0] += 1
        return pltpu.make_async_remote_copy(
            src_ref=src, dst_ref=dst, send_sem=send_sems.at[n], recv_sem=recv_sems.at[n],
            device_id=(target, plane), device_id_type=MESH,
        )

    def place(kind, g):
        n = 1 if kind in (NEAR_LONG, AWAY_LONG, BESIDE_LONG) else 3
        return recv_v.at[pl.ds(START[kind] + n * g, n)]

    parity = lax.rem(z, 2)
    half_rows = pl.ds(pl.multiple_of(parity * (order // 2), order // 2), order // 2)
    other_rows = pl.ds(pl.multiple_of((1 - parity) * (order // 2), order // 2), order // 2)
    pieces = (pl.ds(0, 3), pl.ds(3, 1))
    via, straight, onward = {}, {}, {}
    far, ahead, inside, passed, own, swap, swapped = {}, {}, {}, {}, {}, {}, {}
    for h in range(2):
        for part, sign in enumerate(SIGNS):
            there = along(h, sign, 0, 0)
            for b, some in enumerate((*FULL, pl.ds(3, 2))):
                straight[h, b, part] = message(out_v.at[h, part, some], stage_v.at[h, 2 * part, some], there)
            via[h, 0, part] = message(out_v.at[h, 2, FULL[part]], pass_v.at[h, part, pl.ds(0, 3)], there)
            onward[h, 0, part] = message(pass_v.at[h, part, pl.ds(0, 3)], stage_v.at[h, 3, FULL[part]], there)
            via[h, 1, part] = message(
                out_v.at[h, 2, 3 + part, half_rows], pass_v.at[h, part, 3, half_rows], there
            )
            onward[h, 1, part] = message(
                pass_v.at[h, part, 3, half_rows], stage_v.at[h, 3, 3 + part, half_rows], there
            )
            there = along(h, 0, sign, 0)
            last = along(h, 0, sign, part)
            far[h, 0, part] = message(
                stage_v.at[h, pieces[0], 3 + part], relay_v.at[h, part, pieces[0]], there
            )
            passed[h, 0, part] = message(relay_v.at[h, part, pieces[0]], place(AWAY, h * 2 + part), last)
            far[h, 1, part] = message(
                stage_v.at[h, 3, 3 + part, half_rows], relay_v.at[h, part, 3, half_rows], there
            )
            passed[h, 1, part] = message(
                relay_v.at[h, part, 3, half_rows], recv_v.at[START[AWAY_LONG] + h * 2 + part, half_rows], last
            )
            for m, piece in enumerate(pieces):
                for dc in range(N_C):
                    ahead[h, m, part, dc] = message(
                        stage_v.at[h, piece, PACKED.index((sign % 4, dc))],
                        place((BESIDE, BESIDE_CROSS)[dc], h * 2 + part) if m == 0 else place(BESIDE_LONG, dc * 4 + h * 2 + part),
                        along(h, 0, sign, dc),
                    )
        for m, piece in enumerate(pieces):
            inside[h, m] = message(stage_v.at[h, piece, 1], place((NEAR, NEAR_LONG)[m], h * 2 + 1), at(0, 0, 1))
            own[h, m] = pltpu.make_async_copy(stage_v.at[h, piece, 0], place((NEAR, NEAR_LONG)[m], h * 2), own_sems.at[h, m])
        step = (1 - 2 * parity) * (1 - 2 * h)
        plane = lax.rem(z + step + N_Z, N_Z)
        both = pl.ds(START[AWAY_LONG] + h * 2, 2)
        swap[h] = message(recv_v.at[both, half_rows], recv_v.at[both, half_rows], me, plane)
        swapped[h] = pltpu.make_async_remote_copy(
            src_ref=recv_v.at[both, other_rows], dst_ref=recv_v.at[both, other_rows],
            send_sem=send_sems.at[count[0] - 1], recv_sem=recv_sems.at[count[0] - 1],
            device_id=(me, plane), device_id_type=MESH,
        )

    def ring(part, t, chunk, source):
        piece = left_v.at[source, pl.ds(chunk * per_ring, per_ring)]
        return pltpu.make_async_remote_copy(
            src_ref=piece, dst_ref=piece,
            send_sem=ring_send.at[part, t, chunk], recv_sem=ring_recv.at[part, t, chunk],
            device_id=(me, lax.rem(z + SIGNS[part] + N_Z, N_Z)), device_id_type=MESH,
        )

    def ring_out(part, t, chunk):
        return ring(part, t, chunk, lax.rem(z - SIGNS[part] * t + N_Z, N_Z))

    def ring_in(part, t, chunk):
        return ring(part, t, chunk, lax.rem(z - SIGNS[part] * (t + 1) + N_Z, N_Z))

    def travels(part, t, chunk):
        return t < 3 or chunk % 2 == part

    def pass_on(t, *chunks):
        for chunk in chunks:
            for part in range(2):
                if travels(part, t, chunk):
                    ring_in(part, t, chunk).wait_recv()
                if t < 3 and travels(part, t + 1, chunk):
                    ring_out(part, t + 1, chunk).start()

    def begin(chunk):
        for part in range(2):
            ring_out(part, 0, chunk).start()

    rows = pl.ds(pl.multiple_of(z * share, share), share)

    def fold(values):
        values = values[:, :128] + values[:, 128:]
        return jnp.sum(values.reshape(values.shape[0] // 8, 8, 128), axis=0)

    def in_fours(kind, some, only=None):
        def one(i, carry):
            places = [START[kind] + 4 * i + j for j in range(4)]
            some(places, [slot_of(kind, pos) for pos in places])
            return carry

        if only is None:
            lax.fori_loop(0, (START[kind + 1] - START[kind]) // 4, one, 0)
        else:
            one(only, 0)

    def absorb(kind, only=None):
        def some(places, ks):
            for pos, k in zip(places, ks):
                grad32 = recv_v[pos, rows, :].astype(jnp.float32)
                moment_one = 0.9 * mone_v[k] + 0.1 * grad32
                moment_two = 0.999 * mtwo_v[k] + 0.001 * grad32 * grad32
                ratio = moment_one / (jnp.sqrt(moment_two) + 1e-08)
                adam_v[k] = fold(ratio * ratio)
            for pos, k in zip(places, ks):
                product = jnp.dot(recv_v[pos], right_v[k], preferred_element_type=jnp.float32)
                recv_v[pos] = product.astype(jnp.bfloat16)

        in_fours(kind, some, only)

    def finish(kind):
        def some(places, ks):
            for pos, k in zip(places, ks):
                precond = jnp.dot(
                    left_v[:, pos].reshape(order, order), recv_v[pos], preferred_element_type=jnp.float32
                )
                square_v[k] = fold(precond * precond)
                recv_v[pos] = precond.astype(jnp.bfloat16)

        in_fours(kind, some)

    def count_live():
        shard = lax.broadcasted_iota(jnp.int32, (owner.shape[1], 128), 0) // per_shard
        slot = lax.broadcasted_iota(jnp.int32, (owner.shape[1], 128), 1)
        ours = jnp.broadcast_to(jnp.where(owner[...] == me, 1.0, 0.0), (8, owner.shape[1]))
        counts = jnp.dot(
            ours.astype(jnp.bfloat16),
            jnp.where(shard == slot // 2, 1.0, 0.0).astype(jnp.bfloat16),
            preferred_element_type=jnp.float32,
        )[:1]
        rank = lax.rem(slot[:1], 2).astype(jnp.float32)
        live_v[...] = jnp.where(counts > rank, 1.0, 0.0)

    def by_lane(sums):
        by_slot = jnp.sum(jnp.sum(sums, axis=1), axis=1, keepdims=True)
        spread = jnp.broadcast_to(by_slot, (slots, 128))
        return jnp.sum(jnp.where(diagonal, spread, 0.0), axis=0, keepdims=True)

    diagonal = lax.broadcasted_iota(jnp.int32, (slots, 128), 0) == lax.broadcasted_iota(
        jnp.int32, (slots, 128), 1
    )

    every = [(h, part) for h in range(2) for part in range(2)]
    thirds = ((0, 1, 2), (5, 6, 7), (3, 4))

    def ready(chunk):
        first = pl.ds(chunk * per_ring, per_ring)
        pltpu.make_async_copy(left_hbm.at[first], left_v.at[z, first], left_sems.at[chunk]).wait()
        begin(chunk)

    for chunk in range(RING):
        ready(chunk)
    for h, part in every:
        pack(h, 2, (3 + part,), out_v.at[h, 2])
        via[h, 1, part].start()
    for h, part in every:
        pack(h, 2, thirds[part], out_v.at[h, 2])
        via[h, 0, part].start()
    for h, part in every:
        pack(h, SIGNS[part], thirds[2], out_v.at[h, part])
        straight[h, 2, part].start()
    for h, part in every:
        via[h, 1, part].wait_recv()
        onward[h, 1, part].start()
    for b in range(2):
        for h, part in every:
            pack(h, SIGNS[part], thirds[b], out_v.at[h, part])
            straight[h, b, part].start()
    for h in range(2):
        pack(h, 0, range(8), stage_v.at[h, 1])
    count_live()

    pass_on(0, 0)
    for h, part in every:
        via[h, 0, part].wait_recv()
        onward[h, 0, part].start()
    pass_on(0, 1)
    for h, part in every:
        onward[h, 1, part].wait_recv()
        far[h, 1, part].start()
    for h, part in every:
        straight[h, 2, part].wait_recv()
    for h, part in every:
        far[h, 0, part].start()
    pass_on(0, 2, 3)
    pass_on(1, 0)
    for h, part in every:
        for b in range(2):
            straight[h, b, part].wait_recv()
    for h, part in every:
        ahead[h, 0, part, 0].start()
    for h in range(2):
        inside[h, 0].start()
        own[h, 0].start()
    pass_on(1, 1, 2)
    for h, part in every:
        onward[h, 0, part].wait_recv()
    for h in range(2):
        inside[h, 1].start()
        own[h, 1].start()
    for h, part in every:
        far[h, 1, part].wait_recv()
        passed[h, 1, part].start()
    for load in loads[1:]:
        load.wait()
    for m in range(2):
        for h in range(2):
            own[h, m].wait()
            inside[h, m].wait_recv()
    absorb(NEAR)
    absorb(NEAR_LONG)
    pass_on(1, 3)
    for h, part in every:
        far[h, 0, part].wait_recv()
        passed[h, 0, part].start()
    for h, part in every:
        ahead[h, 0, part, 1].start()
    for dc in range(N_C):
        for h, part in every:
            ahead[h, 1, part, dc].start()
    pass_on(2, 0, 1)
    for h, part in every:
        ahead[h, 0, part, 0].wait_recv()
    for h in range(2):
        for part in range(2):
            passed[h, 1, part].wait_recv()
        swap[h].start()
    absorb(BESIDE)
    pass_on(2, 2, 3)
    for h, part in every:
        passed[h, 0, part].wait_recv()
    absorb(AWAY)
    pass_on(3, 0, 1)
    for kind in (NEAR, NEAR_LONG, BESIDE):
        finish(kind)
    for h in range(2):
        swapped[h].wait_recv()
        swap[h].wait_send()
    absorb(AWAY_LONG)
    finish(AWAY_LONG)
    for h, part in every:
        ahead[h, 0, part, 1].wait_recv()
    absorb(BESIDE_CROSS)
    pass_on(3, 2)
    finish(AWAY)
    pass_on(3, 3)
    for dc in range(N_C):
        for h, part in every:
            ahead[h, 1, part, dc].wait_recv()
        absorb(BESIDE_LONG, dc)

    tiles_v[0] = jnp.broadcast_to(by_lane(adam_v[...]), (8, 128))

    def tell(dz):
        return pltpu.make_async_remote_copy(
            src_ref=tiles_v.at[0],
            dst_ref=tiles_v.at[dz],
            send_sem=zsend.at[dz],
            recv_sem=zrecv.at[dz],
            device_id=(me, lax.rem(z + dz, N_Z)),
            device_id_type=MESH,
        )

    for dz in range(1, N_Z):
        tell(dz).start()
    finish(BESIDE_CROSS)
    finish(BESIDE_LONG)
    sum_pre = by_lane(square_v[...])
    for group in (via, straight, onward, far, ahead, inside, passed):
        for copy in group.values():
            copy.wait_send()
    for t in range(4):
        for chunk in range(RING):
            for part in range(2):
                if travels(part, t, chunk):
                    ring_out(part, t, chunk).wait_send()
    for dz in range(1, N_Z):
        tell(dz).wait()
    sum_adam = jnp.sum(tiles_v[...], axis=0)[:1]
    scale = live_v[...] * (jnp.sqrt(sum_adam / total) / jnp.sqrt(sum_pre / total + 1e-06))
    by_row = jnp.where(diagonal, jnp.broadcast_to(scale, (slots, 128)), 0.0)
    scale_out[...] = jnp.broadcast_to(jnp.sum(by_row, axis=1, keepdims=True), (slots, 128))


def step(owner, grads, left, right, mone, mtwo):
    per_shard, order, _ = grads.shape
    slots, share, _ = mone.shape
    block = (order, order)
    anywhere = pl.BlockSpec(memory_space=pl.ANY)
    vmem = pl.BlockSpec(memory_space=pltpu.VMEM)
    dma = pltpu.SemaphoreType.DMA
    return pl.pallas_call(
        step_kernel,
        out_shape=(
            pltpu.VMEM((slots, *block), jnp.bfloat16),
            pltpu.VMEM((slots, 128), jnp.float32),
        ),
        in_specs=[vmem] + [anywhere] * 5,
        out_specs=(vmem, vmem),
        scratch_shapes=[
            pltpu.VMEM((per_shard + 1, *block), jnp.bfloat16),
            pltpu.VMEM((2, 3, 8, *block), jnp.bfloat16),
            pltpu.VMEM((2, 4, 8, *block), jnp.bfloat16),
            pltpu.VMEM((2, 2, 4, *block), jnp.bfloat16),
            pltpu.VMEM((2, 2, 4, *block), jnp.bfloat16),
            pltpu.VMEM((N_Z, slots, share, order), jnp.bfloat16),
            pltpu.VMEM((slots, *block), jnp.bfloat16),
            pltpu.VMEM((slots, share, order), jnp.float32),
            pltpu.VMEM((slots, share, order), jnp.float32),
            pltpu.VMEM((slots, 8, 128), jnp.float32),
            pltpu.VMEM((slots, 8, 128), jnp.float32),
            pltpu.VMEM((N_Z, 8, 128), jnp.float32),
            pltpu.VMEM((1, 128), jnp.float32),
            pltpu.VMEM((1, 128), jnp.int32),
            pltpu.SMEM((1, 128), jnp.int32),
            dma((4,)),
            dma((RING,)),
            dma((2, 2)),
            dma,
            dma((66,)),
            dma((66,)),
            dma((2, 4, RING)),
            dma((2, 4, RING)),
            dma((N_Z,)),
            dma((N_Z,)),
        ],
        compiler_params=pltpu.CompilerParams(
            collective_id=0, has_side_effects=True, vmem_limit_bytes=LIMIT * 2**20
        ),
        cost_estimate=pl.CostEstimate(
            flops=4 * slots * order**3, bytes_accessed=4 * 10**8, transcendentals=10**6
        ),
    )(owner, grads, left, right, mone, mtwo)


def place_of(me, slot):
    y, x, c = me // (N_X * N_C), (me // N_C) % N_X, me % N_C
    source, half = slot // 2, lax.rem(slot, 2)
    dy = lax.rem(source // (N_X * N_C) - y + N_Y, N_Y)
    dx = lax.rem(lax.rem(source // N_C, N_X) - x + N_X, N_X)
    dc = lax.rem(source + c, N_C)
    first, second = dx + half * (dy - dx), dy + half * (dx - dy)
    d = lax.rem(first + 1, 4)
    g, beside = half * 2 + dc, half * 2 + (3 - second) // 2
    near = jnp.where(d == 3, START[NEAR_LONG] + g, START[NEAR] + 3 * g + d)
    away = jnp.where(d == 3, START[AWAY_LONG] + g, START[AWAY] + 3 * g + d)
    cross = START[BESIDE] + dc * (START[BESIDE_CROSS] - START[BESIDE])
    middle = jnp.where(d == 3, START[BESIDE_LONG] + dc * 4 + beside, cross + 3 * beside + d)
    return jnp.where(second == 0, near, jnp.where(second == 2, away, middle))


def scale_kernel(x, scale, out, ready, sems):
    me = lax.axis_index("dp")

    def copy(i):
        some = pl.ds(GROUP * i, GROUP)
        return pltpu.make_async_copy(ready.at[some], out.at[some], sems.at[i])

    def one(i, carry):
        for j in range(GROUP):
            k = GROUP * i + j
            row = scale[pl.ds(k, 1), :]
            factor = jnp.concatenate([row, row], axis=1)
            ready[k] = (x[place_of(me, k)].astype(jnp.float32) * factor).astype(jnp.bfloat16)
        copy(i).start()
        return carry

    def settle(i, carry):
        copy(i).wait()
        return carry

    steps = x.shape[0] // GROUP
    lax.fori_loop(0, steps, one, 0)
    lax.fori_loop(0, steps, settle, 0)


def apply_scale(x, scale):
    vmem = pl.BlockSpec(memory_space=pltpu.VMEM)
    return pl.pallas_call(
        scale_kernel,
        out_shape=jax.ShapeDtypeStruct(x.shape, jnp.bfloat16),
        in_specs=[vmem, vmem],
        out_specs=pl.BlockSpec(memory_space=pl.ANY),
        scratch_shapes=[
            pltpu.VMEM(x.shape, jnp.bfloat16),
            pltpu.SemaphoreType.DMA((x.shape[0] // GROUP,)),
        ],
        compiler_params=pltpu.CompilerParams(vmem_limit_bytes=24 * 2**20),
    )(x, scale)


def per_device(grads, owner, left_root, right_root, first_moment, second_moment):
    x, scale = step(
        owner.reshape(1, -1), grads, left_root[0], right_root[0], first_moment[0], second_moment[0]
    )
    return apply_scale(x, scale)[None]


def solution(mesh):
    placed = (
        P("dp", None, None),
        P(),
        P("dp", None, "replica", None),
        P("dp", None, None, None),
        P("dp", None, "replica", None),
        P("dp", None, "replica", None),
    )
    return jax.shard_map(
        per_device, mesh=mesh, in_specs=placed, out_specs=P("dp", None, None, None), check_vma=False
    )
```

```python
import functools

import jax
import jax.numpy as jnp
from jax import lax
from jax.experimental import pallas as pl
from jax.experimental.pallas import tpu as pltpu
from jax.sharding import PartitionSpec as P

MESH = pl.DeviceIdType.MESH
N_Y, N_X, N_C = 4, 4, 2
N_DP = N_Y * N_X * N_C
N_Z = 8
GROUP = 4
RING = 4
SIGNS = (1, -1)
LIMIT = 50

NEAR, NEAR_LONG, BESIDE, AWAY_LONG, AWAY, BESIDE_CROSS, BESIDE_LONG = range(7)
START = (0, 12, 16, 28, 32, 44, 56, 64)
PACKED = ((0, 0), (0, 1), (1, 0), (2, 0), (2, 1), (1, 1), (3, 0), (3, 1))
FULL = (pl.ds(0, 3), pl.ds(5, 3))


def decode(kind, q):
    long = kind in (NEAR_LONG, AWAY_LONG, BESIDE_LONG)
    d, g = (3, q) if long else (lax.rem(q, 3), q // 3)
    first, low = lax.rem(d + 3, 4), lax.rem(g, 2)
    if kind in (NEAR, NEAR_LONG):
        return g // 2, first, 0, low
    if kind in (AWAY, AWAY_LONG):
        return g // 2, first, 2, low
    return lax.rem(g // 2, 2), first, 3 - 2 * low, g // 4 if kind == BESIDE_LONG else int(kind == BESIDE_CROSS)


def step_kernel(
    owner, grads_hbm, left_hbm, right_hbm, mone_hbm, mtwo_hbm, recv_v, scale_out,
    grads_v, out_v, stage_v, pass_v, relay_v, left_v, right_v, mone_v, mtwo_v,
    adam_v, square_v, tiles_v, strip_v, live_v, idx_v, idx,
    load_sems, left_sems, own_sems, idx_sem, send_sems, recv_sems, ring_send, ring_recv, zsend, zrecv,
):
    me, z = lax.axis_index("dp"), lax.axis_index("replica")
    per_shard, order = grads_hbm.shape[0], grads_hbm.shape[1]
    slots, share = mone_hbm.shape[0], mone_hbm.shape[1]
    total = float(order * order)
    per_ring = slots // RING
    y, x, c = me // (N_X * N_C), (me // N_C) % N_X, me % N_C

    def at(dy, dx, dc):
        return (
            lax.rem(y + dy + N_Y, N_Y) * (N_X * N_C) + lax.rem(x + dx + N_X, N_X) * N_C + lax.rem(c + dc, N_C)
        )

    def along(half, first, second, dc):
        return at(second + half * (first - second), first + half * (second - first), dc)

    def slot_of(kind, pos):
        half, first, second, dc = decode(kind, pos - START[kind])
        return 2 * along(half, first, second, dc) + half

    quarter = per_shard // 4
    grad_loads = [
        pltpu.make_async_copy(grads_hbm.at[some], grads_v.at[some], load_sems.at[i])
        for i, some in enumerate(pl.ds(quarter * i, quarter) for i in range(4))
    ]
    loads = [
        pltpu.make_async_copy(mone_hbm, mone_v, load_sems.at[4]),
        pltpu.make_async_copy(mtwo_hbm, mtwo_v, load_sems.at[5]),
        pltpu.make_async_copy(right_hbm, right_v, load_sems.at[6]),
    ]
    for load in grad_loads:
        load.start()

    barrier = pltpu.get_barrier_semaphore()
    near = [(0, 0, 1)] + [(dy, dx, dc) for dy, dx in ((0, 1), (0, -1), (1, 0), (-1, 0)) for dc in range(N_C)]
    for step in near:
        pl.semaphore_signal(barrier, inc=1, device_id=(at(*step), z), device_id_type=MESH)
    for dz in range(1, N_Z):
        pl.semaphore_signal(barrier, inc=1, device_id=(me, lax.rem(z + dz, N_Z)), device_id_type=MESH)

    row = lax.broadcasted_iota(jnp.int32, (per_shard, 128), 0)
    lane = lax.broadcasted_iota(jnp.int32, (per_shard, 128), 1)
    per_line = 128 // per_shard
    line = owner[:, pl.ds(pl.multiple_of(me // per_line * 128, 128), 128)]
    mine = pltpu.roll(
        jnp.broadcast_to(line, (per_shard, 128)), lax.rem(128 - lax.rem(me, per_line) * per_shard, 128), 1
    )
    names = jnp.sum(jnp.where(row == lane, mine, 0), axis=1, keepdims=True)
    ranks = jnp.sum(jnp.where((names == mine) & (lane < row), 1, 0), axis=1, keepdims=True)
    found = jnp.where(2 * names + ranks == lane, row - per_shard, 0)
    idx_v[...] = per_shard + jnp.sum(found, axis=0, keepdims=True)
    to_scalars = pltpu.make_async_copy(idx_v, idx, idx_sem)
    to_scalars.start()
    for kind in range(7):

        def load_left(pos, carry):
            pltpu.make_async_copy(
                left_hbm.at[slot_of(kind, pos)], left_v.at[z, pos], left_sems.at[pos // per_ring]
            ).start()
            return carry

        lax.fori_loop(START[kind], START[kind + 1], load_left, 0)
    grads_v[per_shard] = jnp.zeros((order, order), jnp.bfloat16)
    pl.semaphore_wait(barrier, len(near) + N_Z - 1)

    def pack(half, first, places, into):
        for i in places:
            p = along(half, first, *PACKED[i])
            into[i] = grads_v[idx[0, 2 * p + half]]

    count = [0]

    def message(src, dst, target, plane=z):
        n = count[0]
        count[0] += 1
        return pltpu.make_async_remote_copy(
            src_ref=src, dst_ref=dst, send_sem=send_sems.at[n], recv_sem=recv_sems.at[n],
            device_id=(target, plane), device_id_type=MESH,
        )

    def place(kind, g):
        n = 1 if kind in (NEAR_LONG, AWAY_LONG, BESIDE_LONG) else 3
        return recv_v.at[pl.ds(START[kind] + n * g, n)]

    parity = lax.rem(z, 2)
    half_rows = pl.ds(pl.multiple_of(parity * (order // 2), order // 2), order // 2)
    other_rows = pl.ds(pl.multiple_of((1 - parity) * (order // 2), order // 2), order // 2)
    pieces = (pl.ds(0, 3), pl.ds(3, 1))
    via, straight, onward = {}, {}, {}
    far, ahead, inside, passed, own, swap, swapped, strip = {}, {}, {}, {}, {}, {}, {}, {}
    rows = pl.ds(pl.multiple_of(z * share, share), share)
    for h in range(2):
        for part, sign in enumerate(SIGNS):
            there = along(h, sign, 0, 0)
            for b, some in enumerate((*FULL, pl.ds(3, 2))):
                straight[h, b, part] = message(out_v.at[h, part, some], stage_v.at[h, 2 * part, some], there)
            via[h, 0, part] = message(out_v.at[h, 2, FULL[part]], pass_v.at[h, part, pl.ds(0, 3)], there)
            onward[h, 0, part] = message(pass_v.at[h, part, pl.ds(0, 3)], stage_v.at[h, 3, FULL[part]], there)
            via[h, 1, part] = message(
                out_v.at[h, 2, 3 + part, half_rows], pass_v.at[h, part, 3, half_rows], there
            )
            onward[h, 1, part] = message(
                pass_v.at[h, part, 3, half_rows], stage_v.at[h, 3, 3 + part, half_rows], there
            )
            there = along(h, 0, sign, 0)
            last = along(h, 0, sign, part)
            far[h, 0, part] = message(
                stage_v.at[h, pieces[0], 3 + part], relay_v.at[h, part, pieces[0]], there
            )
            passed[h, 0, part] = message(relay_v.at[h, part, pieces[0]], place(AWAY, h * 2 + part), last)
            far[h, 1, part] = message(
                stage_v.at[h, 3, 3 + part, half_rows], relay_v.at[h, part, 3, half_rows], there
            )
            passed[h, 1, part] = message(
                relay_v.at[h, part, 3, half_rows], recv_v.at[START[AWAY_LONG] + h * 2 + part, half_rows], last
            )
            for dc in range(N_C):
                strip[h, part, dc] = message(
                    stage_v.at[h, 3, PACKED.index((sign % 4, dc)), rows],
                    strip_v.at[dc * 4 + h * 2 + part],
                    along(h, 0, sign, dc),
                )
            for m, piece in enumerate(pieces):
                for dc in range(N_C):
                    ahead[h, m, part, dc] = message(
                        stage_v.at[h, piece, PACKED.index((sign % 4, dc))],
                        place((BESIDE, BESIDE_CROSS)[dc], h * 2 + part) if m == 0 else place(BESIDE_LONG, dc * 4 + h * 2 + part),
                        along(h, 0, sign, dc),
                    )
        for m, piece in enumerate(pieces):
            inside[h, m] = message(stage_v.at[h, piece, 1], place((NEAR, NEAR_LONG)[m], h * 2 + 1), at(0, 0, 1))
            own[h, m] = pltpu.make_async_copy(stage_v.at[h, piece, 0], place((NEAR, NEAR_LONG)[m], h * 2), own_sems.at[h, m])
        step = (1 - 2 * parity) * (1 - 2 * h)
        plane = lax.rem(z + step + N_Z, N_Z)
        both = pl.ds(START[AWAY_LONG] + h * 2, 2)
        swap[h] = message(recv_v.at[both, half_rows], recv_v.at[both, half_rows], me, plane)
        swapped[h] = pltpu.make_async_remote_copy(
            src_ref=recv_v.at[both, other_rows], dst_ref=recv_v.at[both, other_rows],
            send_sem=send_sems.at[count[0] - 1], recv_sem=recv_sems.at[count[0] - 1],
            device_id=(me, plane), device_id_type=MESH,
        )

    def ring(part, t, chunk, source):
        piece = left_v.at[source, pl.ds(chunk * per_ring, per_ring)]
        return pltpu.make_async_remote_copy(
            src_ref=piece, dst_ref=piece,
            send_sem=ring_send.at[part, t, chunk], recv_sem=ring_recv.at[part, t, chunk],
            device_id=(me, lax.rem(z + SIGNS[part] + N_Z, N_Z)), device_id_type=MESH,
        )

    def ring_out(part, t, chunk):
        return ring(part, t, chunk, lax.rem(z - SIGNS[part] * t + N_Z, N_Z))

    def ring_in(part, t, chunk):
        return ring(part, t, chunk, lax.rem(z - SIGNS[part] * (t + 1) + N_Z, N_Z))

    def travels(part, t, chunk):
        return t < 3 or chunk % 2 == part

    def pass_on(t, *chunks):
        for chunk in chunks:
            for part in range(2):
                if travels(part, t, chunk):
                    ring_in(part, t, chunk).wait_recv()
                if t < 3 and travels(part, t + 1, chunk):
                    ring_out(part, t + 1, chunk).start()

    def begin(chunk):
        for part in range(2):
            ring_out(part, 0, chunk).start()

    def fold(values):
        values = values[:, :128] + values[:, 128:]
        return jnp.sum(values.reshape(values.shape[0] // 8, 8, 128), axis=0)

    def in_fours(kind, some, only=None):
        def one(i, carry):
            places = [START[kind] + 4 * i + j for j in range(4)]
            some(places, [slot_of(kind, pos) for pos in places])
            return carry

        if only is None:
            lax.fori_loop(0, (START[kind + 1] - START[kind]) // 4, one, 0)
        else:
            one(only, 0)

    def square_ratio(grad, k):
        grad32 = grad.astype(jnp.float32)
        moment_one = 0.9 * mone_v[k] + 0.1 * grad32
        moment_two = 0.999 * mtwo_v[k] + 0.001 * grad32 * grad32
        ratio = moment_one / (jnp.sqrt(moment_two) + 1e-08)
        adam_v[k] = fold(ratio * ratio)

    def absorb(kind, only=None):
        def some(places, ks):
            if kind != BESIDE_LONG:
                for pos, k in zip(places, ks):
                    square_ratio(recv_v[pos, rows, :], k)
            for pos, k in zip(places, ks):
                product = jnp.dot(recv_v[pos], right_v[k], preferred_element_type=jnp.float32)
                recv_v[pos] = product.astype(jnp.bfloat16)

        in_fours(kind, some, only)

    def adam_of_strips():
        def some(places, ks):
            for pos, k in zip(places, ks):
                square_ratio(strip_v[pos - START[BESIDE_LONG]], k)

        in_fours(BESIDE_LONG, some)

    def finish(kind, only=None):
        def some(places, ks):
            for pos, k in zip(places, ks):
                precond = jnp.dot(
                    left_v[:, pos].reshape(order, order), recv_v[pos], preferred_element_type=jnp.float32
                )
                square_v[k] = fold(precond * precond)
                recv_v[pos] = precond.astype(jnp.bfloat16)

        in_fours(kind, some, only)

    def count_live():
        shard = lax.broadcasted_iota(jnp.int32, (owner.shape[1], 128), 0) // per_shard
        slot = lax.broadcasted_iota(jnp.int32, (owner.shape[1], 128), 1)
        ours = jnp.broadcast_to(jnp.where(owner[...] == me, 1.0, 0.0), (8, owner.shape[1]))
        counts = jnp.dot(
            ours.astype(jnp.bfloat16),
            jnp.where(shard == slot // 2, 1.0, 0.0).astype(jnp.bfloat16),
            preferred_element_type=jnp.float32,
        )[:1]
        rank = lax.rem(slot[:1], 2).astype(jnp.float32)
        live_v[...] = jnp.where(counts > rank, 1.0, 0.0)

    def by_lane(sums):
        by_slot = jnp.sum(jnp.sum(sums, axis=1), axis=1, keepdims=True)
        spread = jnp.broadcast_to(by_slot, (slots, 128))
        return jnp.sum(jnp.where(diagonal, spread, 0.0), axis=0, keepdims=True)

    diagonal = lax.broadcasted_iota(jnp.int32, (slots, 128), 0) == lax.broadcasted_iota(
        jnp.int32, (slots, 128), 1
    )

    every = [(h, part) for h in range(2) for part in range(2)]
    thirds = ((0, 1, 2), (5, 6, 7), (3, 4))

    def ready(chunk):
        first = pl.ds(chunk * per_ring, per_ring)
        pltpu.make_async_copy(left_hbm.at[first], left_v.at[z, first], left_sems.at[chunk]).wait()
        begin(chunk)

    for chunk in range(RING):
        ready(chunk)
    to_scalars.wait()
    for load in grad_loads:
        load.wait()
    for load in loads:
        load.start()
    for h, part in every:
        pack(h, 2, (3 + part,), out_v.at[h, 2])
        via[h, 1, part].start()
    for h, part in every:
        pack(h, 2, thirds[part], out_v.at[h, 2])
        via[h, 0, part].start()
    for h, part in every:
        pack(h, SIGNS[part], thirds[2], out_v.at[h, part])
        straight[h, 2, part].start()
    for h, part in every:
        via[h, 1, part].wait_recv()
        onward[h, 1, part].start()
    for b in range(2):
        for h, part in every:
            pack(h, SIGNS[part], thirds[b], out_v.at[h, part])
            straight[h, b, part].start()
    for h in range(2):
        pack(h, 0, range(8), stage_v.at[h, 1])
    count_live()

    pass_on(0, 0)
    for h, part in every:
        via[h, 0, part].wait_recv()
        onward[h, 0, part].start()
    pass_on(0, 1)
    for h, part in every:
        onward[h, 1, part].wait_recv()
        far[h, 1, part].start()
    for h, part in every:
        straight[h, 2, part].wait_recv()
    for h, part in every:
        far[h, 0, part].start()
    pass_on(0, 2, 3)
    pass_on(1, 0)
    for h, part in every:
        for b in range(2):
            straight[h, b, part].wait_recv()
    for h, part in every:
        ahead[h, 0, part, 0].start()
    for h in range(2):
        inside[h, 0].start()
        own[h, 0].start()
    pass_on(1, 1, 2)
    for h, part in every:
        onward[h, 0, part].wait_recv()
    for h in range(2):
        inside[h, 1].start()
        own[h, 1].start()
    for h, part in every:
        far[h, 1, part].wait_recv()
        passed[h, 1, part].start()
    for load in loads:
        load.wait()
    for m in range(2):
        for h in range(2):
            own[h, m].wait()
            inside[h, m].wait_recv()
    absorb(NEAR)
    absorb(NEAR_LONG)
    pass_on(1, 3)
    for h, part in every:
        far[h, 0, part].wait_recv()
        passed[h, 0, part].start()
    for h, part in every:
        ahead[h, 0, part, 1].start()
    for dc in range(N_C):
        for h, part in every:
            strip[h, part, dc].start()
    for dc in range(N_C):
        for h, part in every:
            ahead[h, 1, part, dc].start()
    pass_on(2, 0, 1)
    for h, part in every:
        ahead[h, 0, part, 0].wait_recv()
    for h in range(2):
        for part in range(2):
            passed[h, 1, part].wait_recv()
        swap[h].start()
    absorb(BESIDE)
    pass_on(2, 2, 3)
    for h, part in every:
        passed[h, 0, part].wait_recv()
    absorb(AWAY)
    pass_on(3, 0, 1)
    for kind in (NEAR, NEAR_LONG, BESIDE):
        finish(kind)
    for h in range(2):
        swapped[h].wait_recv()
        swap[h].wait_send()
    absorb(AWAY_LONG)
    finish(AWAY_LONG)
    for h, part in every:
        ahead[h, 0, part, 1].wait_recv()
    absorb(BESIDE_CROSS)
    for dc in range(N_C):
        for h, part in every:
            strip[h, part, dc].wait_recv()
    adam_of_strips()

    tiles_v[0] = jnp.broadcast_to(by_lane(adam_v[...]), (8, 128))

    def tell(dz):
        return pltpu.make_async_remote_copy(
            src_ref=tiles_v.at[0],
            dst_ref=tiles_v.at[dz],
            send_sem=zsend.at[dz],
            recv_sem=zrecv.at[dz],
            device_id=(me, lax.rem(z + dz, N_Z)),
            device_id_type=MESH,
        )

    for dz in range(1, N_Z):
        tell(dz).start()
    pass_on(3, 2)
    finish(AWAY)
    pass_on(3, 3)
    finish(BESIDE_CROSS)
    for dc in range(N_C):
        for h, part in every:
            ahead[h, 1, part, dc].wait_recv()
        absorb(BESIDE_LONG, dc)
        finish(BESIDE_LONG, dc)
    sum_pre = by_lane(square_v[...])
    for group in (via, straight, onward, far, ahead, inside, passed, strip):
        for copy in group.values():
            copy.wait_send()
    for t in range(4):
        for chunk in range(RING):
            for part in range(2):
                if travels(part, t, chunk):
                    ring_out(part, t, chunk).wait_send()
    for dz in range(1, N_Z):
        tell(dz).wait()
    sum_adam = jnp.sum(tiles_v[...], axis=0)[:1]
    scale = live_v[...] * (jnp.sqrt(sum_adam / total) / jnp.sqrt(sum_pre / total + 1e-06))
    by_row = jnp.where(diagonal, jnp.broadcast_to(scale, (slots, 128)), 0.0)
    scale_out[...] = jnp.broadcast_to(jnp.sum(by_row, axis=1, keepdims=True), (slots, 128))


def step(owner, grads, left, right, mone, mtwo):
    per_shard, order, _ = grads.shape
    slots, share, _ = mone.shape
    block = (order, order)
    anywhere = pl.BlockSpec(memory_space=pl.ANY)
    vmem = pl.BlockSpec(memory_space=pltpu.VMEM)
    dma = pltpu.SemaphoreType.DMA
    return pl.pallas_call(
        step_kernel,
        out_shape=(
            pltpu.VMEM((slots, *block), jnp.bfloat16),
            pltpu.VMEM((slots, 128), jnp.float32),
        ),
        in_specs=[vmem] + [anywhere] * 5,
        out_specs=(vmem, vmem),
        scratch_shapes=[
            pltpu.VMEM((per_shard + 1, *block), jnp.bfloat16),
            pltpu.VMEM((2, 3, 8, *block), jnp.bfloat16),
            pltpu.VMEM((2, 4, 8, *block), jnp.bfloat16),
            pltpu.VMEM((2, 2, 4, *block), jnp.bfloat16),
            pltpu.VMEM((2, 2, 4, *block), jnp.bfloat16),
            pltpu.VMEM((N_Z, slots, share, order), jnp.bfloat16),
            pltpu.VMEM((slots, *block), jnp.bfloat16),
            pltpu.VMEM((slots, share, order), jnp.float32),
            pltpu.VMEM((slots, share, order), jnp.float32),
            pltpu.VMEM((slots, 8, 128), jnp.float32),
            pltpu.VMEM((slots, 8, 128), jnp.float32),
            pltpu.VMEM((N_Z, 8, 128), jnp.float32),
            pltpu.VMEM((8, share, order), jnp.bfloat16),
            pltpu.VMEM((1, 128), jnp.float32),
            pltpu.VMEM((1, 128), jnp.int32),
            pltpu.SMEM((1, 128), jnp.int32),
            dma((7,)),
            dma((RING,)),
            dma((2, 2)),
            dma,
            dma((74,)),
            dma((74,)),
            dma((2, 4, RING)),
            dma((2, 4, RING)),
            dma((N_Z,)),
            dma((N_Z,)),
        ],
        compiler_params=pltpu.CompilerParams(
            collective_id=0, has_side_effects=True, vmem_limit_bytes=LIMIT * 2**20
        ),
        cost_estimate=pl.CostEstimate(
            flops=4 * slots * order**3, bytes_accessed=4 * 10**8, transcendentals=10**6
        ),
    )(owner, grads, left, right, mone, mtwo)


def place_of(me, slot):
    y, x, c = me // (N_X * N_C), (me // N_C) % N_X, me % N_C
    source, half = slot // 2, lax.rem(slot, 2)
    dy = lax.rem(source // (N_X * N_C) - y + N_Y, N_Y)
    dx = lax.rem(lax.rem(source // N_C, N_X) - x + N_X, N_X)
    dc = lax.rem(source + c, N_C)
    first, second = dx + half * (dy - dx), dy + half * (dx - dy)
    d = lax.rem(first + 1, 4)
    g, beside = half * 2 + dc, half * 2 + (3 - second) // 2
    near = jnp.where(d == 3, START[NEAR_LONG] + g, START[NEAR] + 3 * g + d)
    away = jnp.where(d == 3, START[AWAY_LONG] + g, START[AWAY] + 3 * g + d)
    cross = START[BESIDE] + dc * (START[BESIDE_CROSS] - START[BESIDE])
    middle = jnp.where(d == 3, START[BESIDE_LONG] + dc * 4 + beside, cross + 3 * beside + d)
    return jnp.where(second == 0, near, jnp.where(second == 2, away, middle))


def scale_kernel(x, scale, out, ready, sems):
    me = lax.axis_index("dp")

    def copy(i):
        some = pl.ds(GROUP * i, GROUP)
        return pltpu.make_async_copy(ready.at[some], out.at[some], sems.at[i])

    def one(i, carry):
        for j in range(GROUP):
            k = GROUP * i + j
            row = scale[pl.ds(k, 1), :]
            factor = jnp.concatenate([row, row], axis=1)
            ready[k] = (x[place_of(me, k)].astype(jnp.float32) * factor).astype(jnp.bfloat16)
        copy(i).start()
        return carry

    def settle(i, carry):
        copy(i).wait()
        return carry

    steps = x.shape[0] // GROUP
    lax.fori_loop(0, steps, one, 0)
    lax.fori_loop(0, steps, settle, 0)


def apply_scale(x, scale):
    vmem = pl.BlockSpec(memory_space=pltpu.VMEM)
    return pl.pallas_call(
        scale_kernel,
        out_shape=jax.ShapeDtypeStruct(x.shape, jnp.bfloat16),
        in_specs=[vmem, vmem],
        out_specs=pl.BlockSpec(memory_space=pl.ANY),
        scratch_shapes=[
            pltpu.VMEM(x.shape, jnp.bfloat16),
            pltpu.SemaphoreType.DMA((x.shape[0] // GROUP,)),
        ],
        compiler_params=pltpu.CompilerParams(vmem_limit_bytes=24 * 2**20),
    )(x, scale)


def per_device(grads, owner, left_root, right_root, first_moment, second_moment):
    x, scale = step(
        owner.reshape(1, -1), grads, left_root[0], right_root[0], first_moment[0], second_moment[0]
    )
    return apply_scale(x, scale)[None]


def solution(mesh):
    placed = (
        P("dp", None, None),
        P(),
        P("dp", None, "replica", None),
        P("dp", None, None, None),
        P("dp", None, "replica", None),
        P("dp", None, "replica", None),
    )
    return jax.shard_map(
        per_device, mesh=mesh, in_specs=placed, out_specs=P("dp", None, None, None), check_vma=False
    )
```

```python
import functools

import jax
import jax.numpy as jnp
from jax import lax
from jax.experimental import pallas as pl
from jax.experimental.pallas import tpu as pltpu
from jax.sharding import PartitionSpec as P

MESH = pl.DeviceIdType.MESH
N_Y, N_X, N_C = 4, 4, 2
N_DP = N_Y * N_X * N_C
N_Z = 8
RING = 4
SIGNS = (1, -1)
LIMIT = 48

NEAR, NEAR_LONG, BESIDE, AWAY_LONG, AWAY, BESIDE_CROSS, BESIDE_LONG = range(7)
START = (0, 12, 16, 28, 32, 44, 56, 64)
PACKED = ((0, 0), (0, 1), (1, 0), (2, 0), (2, 1), (1, 1), (3, 0), (3, 1))
FULL = (pl.ds(0, 3), pl.ds(5, 3))


def decode(kind, q):
    long = kind in (NEAR_LONG, AWAY_LONG, BESIDE_LONG)
    d, g = (3, q) if long else (lax.rem(q, 3), q // 3)
    first, low = lax.rem(d + 3, 4), lax.rem(g, 2)
    if kind in (NEAR, NEAR_LONG):
        return g // 2, first, 0, low
    if kind in (AWAY, AWAY_LONG):
        return g // 2, first, 2, low
    return lax.rem(g // 2, 2), first, 3 - 2 * low, g // 4 if kind == BESIDE_LONG else int(kind == BESIDE_CROSS)


def slot_at(me, kind, pos):
    y, x, c = me // (N_X * N_C), (me // N_C) % N_X, me % N_C
    half, first, second, dc = decode(kind, pos - START[kind])
    dy, dx = second + half * (first - second), first + half * (second - first)
    source = lax.rem(y + dy, N_Y) * (N_X * N_C) + lax.rem(x + dx, N_X) * N_C + lax.rem(c + dc, N_C)
    return 2 * source + half


def step_kernel(
    owner, grads_hbm, left_hbm, right_hbm, mone_hbm, mtwo_hbm, recv_v, left_late, right_late, scale_out,
    grads_v, out_v, stage_v, pass_v, relay_v, left_v, right_v, mone_v, mtwo_v,
    adam_v, square_v, tiles_v, strip_v, live_v, idx_v, idx,
    load_sems, left_sems, own_sems, late_sems, idx_sem, send_sems, recv_sems, ring_send, ring_recv, zsend, zrecv,
):
    me, z = lax.axis_index("dp"), lax.axis_index("replica")
    per_shard, order = grads_hbm.shape[0], grads_hbm.shape[1]
    slots, share = mone_hbm.shape[0], mone_hbm.shape[1]
    total = float(order * order)
    per_ring = slots // RING
    y, x, c = me // (N_X * N_C), (me // N_C) % N_X, me % N_C

    def at(dy, dx, dc):
        return (
            lax.rem(y + dy + N_Y, N_Y) * (N_X * N_C) + lax.rem(x + dx + N_X, N_X) * N_C + lax.rem(c + dc, N_C)
        )

    def along(half, first, second, dc):
        return at(second + half * (first - second), first + half * (second - first), dc)

    def slot_of(kind, pos):
        return slot_at(me, kind, pos)

    quarter = per_shard // 4
    grad_loads = [
        pltpu.make_async_copy(grads_hbm.at[some], grads_v.at[some], load_sems.at[i])
        for i, some in enumerate(pl.ds(quarter * i, quarter) for i in range(4))
    ]
    loads = [
        pltpu.make_async_copy(mone_hbm, mone_v, load_sems.at[4]),
        pltpu.make_async_copy(mtwo_hbm, mtwo_v, load_sems.at[5]),
        pltpu.make_async_copy(right_hbm, right_v, load_sems.at[6]),
    ]
    for load in grad_loads:
        load.start()

    barrier = pltpu.get_barrier_semaphore()
    near = [(0, 0, 1)] + [(dy, dx, dc) for dy, dx in ((0, 1), (0, -1), (1, 0), (-1, 0)) for dc in range(N_C)]
    for step in near:
        pl.semaphore_signal(barrier, inc=1, device_id=(at(*step), z), device_id_type=MESH)
    for dz in range(1, N_Z):
        pl.semaphore_signal(barrier, inc=1, device_id=(me, lax.rem(z + dz, N_Z)), device_id_type=MESH)

    row = lax.broadcasted_iota(jnp.int32, (per_shard, 128), 0)
    lane = lax.broadcasted_iota(jnp.int32, (per_shard, 128), 1)
    per_line = 128 // per_shard
    line = owner[:, pl.ds(pl.multiple_of(me // per_line * 128, 128), 128)]
    mine = pltpu.roll(
        jnp.broadcast_to(line, (per_shard, 128)), lax.rem(128 - lax.rem(me, per_line) * per_shard, 128), 1
    )
    names = jnp.sum(jnp.where(row == lane, mine, 0), axis=1, keepdims=True)
    ranks = jnp.sum(jnp.where((names == mine) & (lane < row), 1, 0), axis=1, keepdims=True)
    found = jnp.where(2 * names + ranks == lane, row - per_shard, 0)
    idx_v[...] = per_shard + jnp.sum(found, axis=0, keepdims=True)
    to_scalars = pltpu.make_async_copy(idx_v, idx, idx_sem)
    to_scalars.start()
    for kind in range(7):

        def load_left(pos, carry):
            pltpu.make_async_copy(
                left_hbm.at[slot_of(kind, pos)], left_v.at[z, pos], left_sems.at[pos // per_ring]
            ).start()
            return carry

        lax.fori_loop(START[kind], START[kind + 1], load_left, 0)
    grads_v[per_shard] = jnp.zeros((order, order), jnp.bfloat16)
    pl.semaphore_wait(barrier, len(near) + N_Z - 1)

    def pack(half, first, places, into):
        for i in places:
            p = along(half, first, *PACKED[i])
            into[i] = grads_v[idx[0, 2 * p + half]]

    count = [0]

    def message(src, dst, target, plane=z):
        n = count[0]
        count[0] += 1
        return pltpu.make_async_remote_copy(
            src_ref=src, dst_ref=dst, send_sem=send_sems.at[n], recv_sem=recv_sems.at[n],
            device_id=(target, plane), device_id_type=MESH,
        )

    def place(kind, g):
        n = 1 if kind in (NEAR_LONG, AWAY_LONG, BESIDE_LONG) else 3
        return recv_v.at[pl.ds(START[kind] + n * g, n)]

    parity = lax.rem(z, 2)
    half_rows = pl.ds(pl.multiple_of(parity * (order // 2), order // 2), order // 2)
    other_rows = pl.ds(pl.multiple_of((1 - parity) * (order // 2), order // 2), order // 2)
    pieces = (pl.ds(0, 3), pl.ds(3, 1))
    via, straight, onward = {}, {}, {}
    far, ahead, inside, passed, own, swap, swapped, strip = {}, {}, {}, {}, {}, {}, {}, {}
    rows = pl.ds(pl.multiple_of(z * share, share), share)
    for h in range(2):
        for part, sign in enumerate(SIGNS):
            there = along(h, sign, 0, 0)
            for b, some in enumerate((*FULL, pl.ds(3, 2))):
                straight[h, b, part] = message(out_v.at[h, part, some], stage_v.at[h, 2 * part, some], there)
            via[h, 0, part] = message(out_v.at[h, 2, FULL[part]], pass_v.at[h, part, pl.ds(0, 3)], there)
            onward[h, 0, part] = message(pass_v.at[h, part, pl.ds(0, 3)], stage_v.at[h, 3, FULL[part]], there)
            via[h, 1, part] = message(
                out_v.at[h, 2, 3 + part, half_rows], pass_v.at[h, part, 3, half_rows], there
            )
            onward[h, 1, part] = message(
                pass_v.at[h, part, 3, half_rows], stage_v.at[h, 3, 3 + part, half_rows], there
            )
            there = along(h, 0, sign, 0)
            last = along(h, 0, sign, part)
            far[h, 0, part] = message(
                stage_v.at[h, pieces[0], 3 + part], relay_v.at[h, part, pieces[0]], there
            )
            passed[h, 0, part] = message(relay_v.at[h, part, pieces[0]], place(AWAY, h * 2 + part), last)
            far[h, 1, part] = message(
                stage_v.at[h, 3, 3 + part, half_rows], relay_v.at[h, part, 3, half_rows], there
            )
            passed[h, 1, part] = message(
                relay_v.at[h, part, 3, half_rows], recv_v.at[START[AWAY_LONG] + h * 2 + part, half_rows], last
            )
            for dc in range(N_C):
                strip[h, part, dc] = message(
                    stage_v.at[h, 3, PACKED.index((sign % 4, dc)), rows],
                    strip_v.at[dc * 4 + h * 2 + part],
                    along(h, 0, sign, dc),
                )
            for m, piece in enumerate(pieces):
                for dc in range(N_C):
                    ahead[h, m, part, dc] = message(
                        stage_v.at[h, piece, PACKED.index((sign % 4, dc))],
                        place((BESIDE, BESIDE_CROSS)[dc], h * 2 + part) if m == 0 else place(BESIDE_LONG, dc * 4 + h * 2 + part),
                        along(h, 0, sign, dc),
                    )
        for m, piece in enumerate(pieces):
            inside[h, m] = message(stage_v.at[h, piece, 1], place((NEAR, NEAR_LONG)[m], h * 2 + 1), at(0, 0, 1))
            own[h, m] = pltpu.make_async_copy(stage_v.at[h, piece, 0], place((NEAR, NEAR_LONG)[m], h * 2), own_sems.at[h, m])
        step = (1 - 2 * parity) * (1 - 2 * h)
        plane = lax.rem(z + step + N_Z, N_Z)
        both = pl.ds(START[AWAY_LONG] + h * 2, 2)
        swap[h] = message(recv_v.at[both, half_rows], recv_v.at[both, half_rows], me, plane)
        swapped[h] = pltpu.make_async_remote_copy(
            src_ref=recv_v.at[both, other_rows], dst_ref=recv_v.at[both, other_rows],
            send_sem=send_sems.at[count[0] - 1], recv_sem=recv_sems.at[count[0] - 1],
            device_id=(me, plane), device_id_type=MESH,
        )

    def ring(part, t, chunk, source):
        piece = left_v.at[source, pl.ds(chunk * per_ring, per_ring)]
        return pltpu.make_async_remote_copy(
            src_ref=piece, dst_ref=piece,
            send_sem=ring_send.at[part, t, chunk], recv_sem=ring_recv.at[part, t, chunk],
            device_id=(me, lax.rem(z + SIGNS[part] + N_Z, N_Z)), device_id_type=MESH,
        )

    def ring_out(part, t, chunk):
        return ring(part, t, chunk, lax.rem(z - SIGNS[part] * t + N_Z, N_Z))

    def ring_in(part, t, chunk):
        return ring(part, t, chunk, lax.rem(z - SIGNS[part] * (t + 1) + N_Z, N_Z))

    def travels(part, t, chunk):
        return t < 3 or chunk % 2 == part

    def pass_on(t, *chunks):
        for chunk in chunks:
            for part in range(2):
                if travels(part, t, chunk):
                    ring_in(part, t, chunk).wait_recv()
                if t < 3 and travels(part, t + 1, chunk):
                    ring_out(part, t + 1, chunk).start()

    def begin(chunk):
        for part in range(2):
            ring_out(part, 0, chunk).start()

    def fold(values):
        values = values[:, :128] + values[:, 128:]
        return jnp.sum(values.reshape(values.shape[0] // 8, 8, 128), axis=0)

    def in_fours(kind, some):
        def one(i, carry):
            places = [START[kind] + 4 * i + j for j in range(4)]
            some(places, [slot_of(kind, pos) for pos in places])
            return carry

        lax.fori_loop(0, (START[kind + 1] - START[kind]) // 4, one, 0)

    def square_ratio(grad, k):
        grad32 = grad.astype(jnp.float32)
        moment_one = 0.9 * mone_v[k] + 0.1 * grad32
        moment_two = 0.999 * mtwo_v[k] + 0.001 * grad32 * grad32
        ratio = moment_one / (jnp.sqrt(moment_two) + 1e-08)
        adam_v[k] = fold(ratio * ratio)

    def absorb(kind):
        def some(places, ks):
            for pos, k in zip(places, ks):
                square_ratio(recv_v[pos, rows, :], k)
            for pos, k in zip(places, ks):
                product = jnp.dot(recv_v[pos], right_v[k], preferred_element_type=jnp.float32)
                recv_v[pos] = product.astype(jnp.bfloat16)

        in_fours(kind, some)

    def adam_of_strips():
        def some(places, ks):
            for pos, k in zip(places, ks):
                square_ratio(strip_v[pos - START[BESIDE_LONG]], k)
                square_v[k] = jnp.zeros((8, 128), jnp.float32)

        in_fours(BESIDE_LONG, some)

    def finish(kind):
        def some(places, ks):
            for pos, k in zip(places, ks):
                precond = jnp.dot(
                    left_v[:, pos].reshape(order, order), recv_v[pos], preferred_element_type=jnp.float32
                )
                square_v[k] = fold(precond * precond)
                recv_v[pos] = precond.astype(jnp.bfloat16)

        in_fours(kind, some)

    def count_live():
        shard = lax.broadcasted_iota(jnp.int32, (owner.shape[1], 128), 0) // per_shard
        slot = lax.broadcasted_iota(jnp.int32, (owner.shape[1], 128), 1)
        ours = jnp.broadcast_to(jnp.where(owner[...] == me, 1.0, 0.0), (8, owner.shape[1]))
        counts = jnp.dot(
            ours.astype(jnp.bfloat16),
            jnp.where(shard == slot // 2, 1.0, 0.0).astype(jnp.bfloat16),
            preferred_element_type=jnp.float32,
        )[:1]
        rank = lax.rem(slot[:1], 2).astype(jnp.float32)
        live_v[...] = jnp.where(counts > rank, 1.0, 0.0)

    def by_lane(sums):
        by_slot = jnp.sum(jnp.sum(sums, axis=1), axis=1, keepdims=True)
        spread = jnp.broadcast_to(by_slot, (slots, 128))
        return jnp.sum(jnp.where(diagonal, spread, 0.0), axis=0, keepdims=True)

    diagonal = lax.broadcasted_iota(jnp.int32, (slots, 128), 0) == lax.broadcasted_iota(
        jnp.int32, (slots, 128), 1
    )

    every = [(h, part) for h in range(2) for part in range(2)]
    thirds = ((0, 1, 2), (5, 6, 7), (3, 4))

    def ready(chunk):
        first = pl.ds(chunk * per_ring, per_ring)
        pltpu.make_async_copy(left_hbm.at[first], left_v.at[z, first], left_sems.at[chunk]).wait()
        begin(chunk)

    for chunk in range(RING):
        ready(chunk)
    to_scalars.wait()
    for load in grad_loads:
        load.wait()
    for load in loads:
        load.start()
    for h, part in every:
        pack(h, 2, (3 + part,), out_v.at[h, 2])
        via[h, 1, part].start()
    for h, part in every:
        pack(h, 2, thirds[part], out_v.at[h, 2])
        via[h, 0, part].start()
    for h, part in every:
        pack(h, SIGNS[part], thirds[2], out_v.at[h, part])
        straight[h, 2, part].start()
    for h, part in every:
        via[h, 1, part].wait_recv()
        onward[h, 1, part].start()
    for b in range(2):
        for h, part in every:
            pack(h, SIGNS[part], thirds[b], out_v.at[h, part])
            straight[h, b, part].start()
    for h in range(2):
        pack(h, 0, range(8), stage_v.at[h, 1])
    count_live()

    pass_on(0, 0)
    for h, part in every:
        via[h, 0, part].wait_recv()
        onward[h, 0, part].start()
    pass_on(0, 1)
    for h, part in every:
        onward[h, 1, part].wait_recv()
        far[h, 1, part].start()
    for h, part in every:
        straight[h, 2, part].wait_recv()
    for h, part in every:
        far[h, 0, part].start()
    pass_on(0, 2, 3)
    pass_on(1, 0)
    for h, part in every:
        for b in range(2):
            straight[h, b, part].wait_recv()
    for h, part in every:
        ahead[h, 0, part, 0].start()
    for h in range(2):
        inside[h, 0].start()
        own[h, 0].start()
    pass_on(1, 1, 2)
    for h, part in every:
        onward[h, 0, part].wait_recv()
    for h in range(2):
        inside[h, 1].start()
        own[h, 1].start()
    for h, part in every:
        far[h, 1, part].wait_recv()
        passed[h, 1, part].start()
    for load in loads:
        load.wait()
    first_late = START[BESIDE_LONG]
    to_late = [
        pltpu.make_async_copy(right_v.at[slot_of(BESIDE_LONG, first_late + i)], right_late.at[i], late_sems.at[i])
        for i in range(slots - first_late)
    ]
    for copy in to_late:
        copy.start()
    for m in range(2):
        for h in range(2):
            own[h, m].wait()
            inside[h, m].wait_recv()
    absorb(NEAR)
    absorb(NEAR_LONG)
    pass_on(1, 3)
    for h, part in every:
        far[h, 0, part].wait_recv()
        passed[h, 0, part].start()
    for h, part in every:
        ahead[h, 0, part, 1].start()
    for dc in range(N_C):
        for h, part in every:
            strip[h, part, dc].start()
    for dc in range(N_C):
        for h, part in every:
            ahead[h, 1, part, dc].start()
    pass_on(2, 0, 1)
    for h, part in every:
        ahead[h, 0, part, 0].wait_recv()
    for h in range(2):
        for part in range(2):
            passed[h, 1, part].wait_recv()
        swap[h].start()
    absorb(BESIDE)
    pass_on(2, 2, 3)
    for h, part in every:
        passed[h, 0, part].wait_recv()
    absorb(AWAY)
    pass_on(3, 0, 1)
    for kind in (NEAR, NEAR_LONG, BESIDE):
        finish(kind)
    for h in range(2):
        swapped[h].wait_recv()
        swap[h].wait_send()
    absorb(AWAY_LONG)
    finish(AWAY_LONG)
    for h, part in every:
        ahead[h, 0, part, 1].wait_recv()
    absorb(BESIDE_CROSS)
    for dc in range(N_C):
        for h, part in every:
            strip[h, part, dc].wait_recv()
    adam_of_strips()

    tiles_v[0] = jnp.broadcast_to(by_lane(adam_v[...]), (8, 128))

    def tell(dz):
        return pltpu.make_async_remote_copy(
            src_ref=tiles_v.at[0],
            dst_ref=tiles_v.at[dz],
            send_sem=zsend.at[dz],
            recv_sem=zrecv.at[dz],
            device_id=(me, lax.rem(z + dz, N_Z)),
            device_id_type=MESH,
        )

    for dz in range(1, N_Z):
        tell(dz).start()
    pass_on(3, 2)
    finish(AWAY)
    pass_on(3, 3)
    to_late.append(
        pltpu.make_async_copy(
            left_v.at[:, pl.ds(first_late, slots - first_late)], left_late, late_sems.at[slots - first_late]
        )
    )
    to_late[-1].start()
    finish(BESIDE_CROSS)
    sum_pre = by_lane(square_v[...])
    for dz in range(1, N_Z):
        tell(dz).wait()
    sum_adam = jnp.sum(tiles_v[...], axis=0)[:1]
    lane = lax.broadcasted_iota(jnp.int32, (1, 128), 1)
    dy = lax.rem(lane // (2 * N_X * N_C) - y + 2 * N_Y, N_Y)
    dx = lax.rem(lax.rem(lane // (2 * N_C), N_X) - x + N_X, N_X)
    odd = lax.rem(lane, 2) == 1
    later = (jnp.where(odd, dy, dx) == 2) & (lax.rem(jnp.where(odd, dx, dy), 2) == 1)
    norm = live_v[...] * jnp.sqrt(sum_adam / total)
    scale = jnp.where(later, norm, norm / jnp.sqrt(sum_pre / total + 1e-06))
    by_row = jnp.where(diagonal, jnp.broadcast_to(scale, (slots, 128)), 0.0)
    scale_out[...] = jnp.broadcast_to(jnp.sum(by_row, axis=1, keepdims=True), (slots, 128))
    for copy in to_late:
        copy.wait()
    for dc in range(N_C):
        for h, part in every:
            ahead[h, 1, part, dc].wait_recv()
    for group in (via, straight, onward, far, ahead, inside, passed, strip):
        for copy in group.values():
            copy.wait_send()
    for t in range(4):
        for chunk in range(RING):
            for part in range(2):
                if travels(part, t, chunk):
                    ring_out(part, t, chunk).wait_send()


def step(owner, grads, left, right, mone, mtwo):
    per_shard, order, _ = grads.shape
    slots, share, _ = mone.shape
    block = (order, order)
    late = slots - START[BESIDE_LONG]
    anywhere = pl.BlockSpec(memory_space=pl.ANY)
    vmem = pl.BlockSpec(memory_space=pltpu.VMEM)
    dma = pltpu.SemaphoreType.DMA
    return pl.pallas_call(
        step_kernel,
        out_shape=(
            pltpu.VMEM((slots, *block), jnp.bfloat16),
            pltpu.VMEM((N_Z, late, share, order), jnp.bfloat16),
            pltpu.VMEM((late, *block), jnp.bfloat16),
            pltpu.VMEM((slots, 128), jnp.float32),
        ),
        in_specs=[vmem] + [anywhere] * 5,
        out_specs=(vmem, vmem, vmem, vmem),
        scratch_shapes=[
            pltpu.VMEM((per_shard + 1, *block), jnp.bfloat16),
            pltpu.VMEM((2, 3, 8, *block), jnp.bfloat16),
            pltpu.VMEM((2, 4, 8, *block), jnp.bfloat16),
            pltpu.VMEM((2, 2, 4, *block), jnp.bfloat16),
            pltpu.VMEM((2, 2, 4, *block), jnp.bfloat16),
            pltpu.VMEM((N_Z, slots, share, order), jnp.bfloat16),
            pltpu.VMEM((slots, *block), jnp.bfloat16),
            pltpu.VMEM((slots, share, order), jnp.float32),
            pltpu.VMEM((slots, share, order), jnp.float32),
            pltpu.VMEM((slots, 8, 128), jnp.float32),
            pltpu.VMEM((slots, 8, 128), jnp.float32),
            pltpu.VMEM((N_Z, 8, 128), jnp.float32),
            pltpu.VMEM((8, share, order), jnp.bfloat16),
            pltpu.VMEM((1, 128), jnp.float32),
            pltpu.VMEM((1, 128), jnp.int32),
            pltpu.SMEM((1, 128), jnp.int32),
            dma((7,)),
            dma((RING,)),
            dma((2, 2)),
            dma((late + 1,)),
            dma,
            dma((74,)),
            dma((74,)),
            dma((2, 4, RING)),
            dma((2, 4, RING)),
            dma((N_Z,)),
            dma((N_Z,)),
        ],
        compiler_params=pltpu.CompilerParams(
            collective_id=0, has_side_effects=True, vmem_limit_bytes=LIMIT * 2**20
        ),
        cost_estimate=pl.CostEstimate(
            flops=4 * slots * order**3, bytes_accessed=4 * 10**8, transcendentals=10**6
        ),
    )(owner, grads, left, right, mone, mtwo)


def scale_kernel(x, left, right, scale, out, ready, sems):
    me = lax.axis_index("dp")
    order = x.shape[1]
    last = START[BESIDE_LONG]

    def copy(kind, pos):
        return pltpu.make_async_copy(ready.at[pos], out.at[slot_at(me, kind, pos)], sems.at[pos])

    def row(kind, pos):
        return scale[pl.ds(slot_at(me, kind, pos), 1), :]

    def in_fours(kind, some):
        def one(i, carry):
            places = [START[kind] + 4 * i + j for j in range(4)]
            some(places)
            for pos in places:
                copy(kind, pos).start()
            return carry

        lax.fori_loop(0, (START[kind + 1] - START[kind]) // 4, one, 0)

    def store(pos, values, factor):
        ready[pos] = (values * jnp.concatenate([factor, factor], axis=1)).astype(jnp.bfloat16)

    for kind in range(BESIDE_LONG):

        def scaled(places):
            for pos in places:
                store(pos, x[pos].astype(jnp.float32), row(kind, pos))

        in_fours(kind, scaled)

    def whole(places):
        halves = [
            jnp.dot(
                left[:, pos - last].reshape(order, order), x[pos], preferred_element_type=jnp.float32
            ).astype(jnp.bfloat16)
            for pos in places
        ]
        preconds = [
            jnp.dot(half, right[pos - last], preferred_element_type=jnp.float32)
            for pos, half in zip(places, halves)
        ]
        for pos, precond in zip(places, preconds):
            mean = jnp.sum(precond * precond, axis=(0, 1), keepdims=True) / float(order * order) + 1e-06
            store(pos, precond, row(BESIDE_LONG, pos) / jnp.sqrt(mean))

    in_fours(BESIDE_LONG, whole)
    for kind in range(BESIDE_LONG + 1):

        def settle(pos, carry):
            copy(kind, pos).wait()
            return carry

        lax.fori_loop(START[kind], START[kind + 1], settle, 0)


def apply_scale(x, left, right, scale):
    vmem, anywhere = pl.BlockSpec(memory_space=pltpu.VMEM), pl.BlockSpec(memory_space=pl.ANY)
    return pl.pallas_call(
        scale_kernel,
        out_shape=jax.ShapeDtypeStruct(x.shape, jnp.bfloat16),
        in_specs=[vmem] * 4,
        out_specs=anywhere,
        scratch_shapes=[
            pltpu.VMEM(x.shape, jnp.bfloat16),
            pltpu.SemaphoreType.DMA((x.shape[0],)),
        ],
        compiler_params=pltpu.CompilerParams(vmem_limit_bytes=24 * 2**20),
    )(x, left, right, scale)


def per_device(grads, owner, left_root, right_root, first_moment, second_moment):
    x, left, right, scale = step(
        owner.reshape(1, -1), grads, left_root[0], right_root[0], first_moment[0], second_moment[0]
    )
    return apply_scale(x, left, right, scale)[None]


def solution(mesh):
    placed = (
        P("dp", None, None),
        P(),
        P("dp", None, "replica", None),
        P("dp", None, None, None),
        P("dp", None, "replica", None),
        P("dp", None, "replica", None),
    )
    return jax.shard_map(
        per_device, mesh=mesh, in_specs=placed, out_specs=P("dp", None, None, None), check_vma=False
    )
```

```python
import functools

import jax
import jax.numpy as jnp
from jax import lax
from jax.experimental import pallas as pl
from jax.experimental.pallas import tpu as pltpu
from jax.sharding import PartitionSpec as P

MESH = pl.DeviceIdType.MESH
N_Y, N_X, N_C = 4, 4, 2
N_DP = N_Y * N_X * N_C
N_Z = 8
RING = 4
SIGNS = (1, -1)
LIMIT = 48

NEAR, NEAR_LONG, BESIDE, AWAY_LONG, AWAY, BESIDE_CROSS, BESIDE_LONG = range(7)
START = (0, 12, 16, 28, 32, 44, 56, 64)
PACKED = ((0, 0), (0, 1), (1, 0), (2, 0), (2, 1), (1, 1), (3, 0), (3, 1))
FULL = (pl.ds(0, 3), pl.ds(5, 3))


def decode(kind, q):
    long = kind in (NEAR_LONG, AWAY_LONG, BESIDE_LONG)
    d, g = (3, q) if long else (lax.rem(q, 3), q // 3)
    first, low = lax.rem(d + 3, 4), lax.rem(g, 2)
    if kind in (NEAR, NEAR_LONG):
        return g // 2, first, 0, low
    if kind in (AWAY, AWAY_LONG):
        return g // 2, first, 2, low
    return lax.rem(g // 2, 2), first, 3 - 2 * low, g // 4 if kind == BESIDE_LONG else int(kind == BESIDE_CROSS)


def slot_at(me, kind, pos):
    y, x, c = me // (N_X * N_C), (me // N_C) % N_X, me % N_C
    half, first, second, dc = decode(kind, pos - START[kind])
    dy, dx = second + half * (first - second), first + half * (second - first)
    source = lax.rem(y + dy, N_Y) * (N_X * N_C) + lax.rem(x + dx, N_X) * N_C + lax.rem(c + dc, N_C)
    return 2 * source + half


def step_kernel(
    owner, grads_hbm, left_hbm, right_hbm, mone_hbm, mtwo_hbm, recv_v, left_late, right_late, scale_out,
    grads_v, out_v, stage_v, pass_v, relay_v, left_v, right_v, mone_v, mtwo_v,
    adam_v, square_v, tiles_v, strip_v, live_v, idx_v, idx,
    load_sems, left_sems, own_sems, late_sems, idx_sem, send_sems, recv_sems, ring_send, ring_recv, zsend, zrecv,
):
    me, z = lax.axis_index("dp"), lax.axis_index("replica")
    per_shard, order = grads_hbm.shape[0], grads_hbm.shape[1]
    slots, share = mone_hbm.shape[0], mone_hbm.shape[1]
    total = float(order * order)
    per_ring = slots // RING
    y, x, c = me // (N_X * N_C), (me // N_C) % N_X, me % N_C

    def at(dy, dx, dc):
        return (
            lax.rem(y + dy + N_Y, N_Y) * (N_X * N_C) + lax.rem(x + dx + N_X, N_X) * N_C + lax.rem(c + dc, N_C)
        )

    def along(half, first, second, dc):
        return at(second + half * (first - second), first + half * (second - first), dc)

    def slot_of(kind, pos):
        return slot_at(me, kind, pos)

    quarter = per_shard // 4
    grad_loads = [
        pltpu.make_async_copy(grads_hbm.at[some], grads_v.at[some], load_sems.at[i])
        for i, some in enumerate(pl.ds(quarter * i, quarter) for i in range(4))
    ]
    loads = [
        pltpu.make_async_copy(mone_hbm, mone_v, load_sems.at[4]),
        pltpu.make_async_copy(mtwo_hbm, mtwo_v, load_sems.at[5]),
        pltpu.make_async_copy(right_hbm, right_v, load_sems.at[6]),
    ]
    for load in grad_loads:
        load.start()

    barrier = pltpu.get_barrier_semaphore()
    near = [(0, 0, 1)] + [(dy, dx, dc) for dy, dx in ((0, 1), (0, -1), (1, 0), (-1, 0)) for dc in range(N_C)]
    for step in near:
        pl.semaphore_signal(barrier, inc=1, device_id=(at(*step), z), device_id_type=MESH)
    for dz in range(1, N_Z):
        pl.semaphore_signal(barrier, inc=1, device_id=(me, lax.rem(z + dz, N_Z)), device_id_type=MESH)

    row = lax.broadcasted_iota(jnp.int32, (per_shard, 128), 0)
    lane = lax.broadcasted_iota(jnp.int32, (per_shard, 128), 1)
    per_line = 128 // per_shard
    line = owner[:, pl.ds(pl.multiple_of(me // per_line * 128, 128), 128)]
    mine = pltpu.roll(
        jnp.broadcast_to(line, (per_shard, 128)), lax.rem(128 - lax.rem(me, per_line) * per_shard, 128), 1
    )
    names = jnp.sum(jnp.where(row == lane, mine, 0), axis=1, keepdims=True)
    ranks = jnp.sum(jnp.where((names == mine) & (lane < row), 1, 0), axis=1, keepdims=True)
    found = jnp.where(2 * names + ranks == lane, row - per_shard, 0)
    idx_v[...] = per_shard + jnp.sum(found, axis=0, keepdims=True)
    to_scalars = pltpu.make_async_copy(idx_v, idx, idx_sem)
    to_scalars.start()
    for kind in range(7):

        def load_left(pos, carry):
            pltpu.make_async_copy(
                left_hbm.at[slot_of(kind, pos)], left_v.at[z, pos], left_sems.at[pos // per_ring]
            ).start()
            return carry

        lax.fori_loop(START[kind], START[kind + 1], load_left, 0)
    grads_v[per_shard] = jnp.zeros((order, order), jnp.bfloat16)
    pl.semaphore_wait(barrier, len(near) + N_Z - 1)

    def pack(half, first, places, into):
        for i in places:
            p = along(half, first, *PACKED[i])
            into[i] = grads_v[idx[0, 2 * p + half]]

    count = [0]

    def message(src, dst, target, plane=z):
        n = count[0]
        count[0] += 1
        return pltpu.make_async_remote_copy(
            src_ref=src, dst_ref=dst, send_sem=send_sems.at[n], recv_sem=recv_sems.at[n],
            device_id=(target, plane), device_id_type=MESH,
        )

    def place(kind, g):
        n = 1 if kind in (NEAR_LONG, AWAY_LONG, BESIDE_LONG) else 3
        return recv_v.at[pl.ds(START[kind] + n * g, n)]

    parity = lax.rem(z, 2)
    half_rows = pl.ds(pl.multiple_of(parity * (order // 2), order // 2), order // 2)
    other_rows = pl.ds(pl.multiple_of((1 - parity) * (order // 2), order // 2), order // 2)
    pieces = (pl.ds(0, 3), pl.ds(3, 1))
    via, straight, onward = {}, {}, {}
    far, ahead, inside, passed, own, swap, swapped, strip = {}, {}, {}, {}, {}, {}, {}, {}
    rows = pl.ds(pl.multiple_of(z * share, share), share)
    for h in range(2):
        for part, sign in enumerate(SIGNS):
            there = along(h, sign, 0, 0)
            for b, some in enumerate((*FULL, pl.ds(3, 2))):
                straight[h, b, part] = message(out_v.at[h, part, some], stage_v.at[h, 2 * part, some], there)
            via[h, 0, part] = message(out_v.at[h, 2, FULL[part]], pass_v.at[h, part, pl.ds(0, 3)], there)
            onward[h, 0, part] = message(pass_v.at[h, part, pl.ds(0, 3)], stage_v.at[h, 3, FULL[part]], there)
            via[h, 1, part] = message(
                out_v.at[h, 2, 3 + part, half_rows], pass_v.at[h, part, 3, half_rows], there
            )
            onward[h, 1, part] = message(
                pass_v.at[h, part, 3, half_rows], stage_v.at[h, 3, 3 + part, half_rows], there
            )
            there = along(h, 0, sign, 0)
            last = along(h, 0, sign, part)
            far[h, 0, part] = message(
                stage_v.at[h, pieces[0], 3 + part], relay_v.at[h, part, pieces[0]], there
            )
            passed[h, 0, part] = message(relay_v.at[h, part, pieces[0]], place(AWAY, h * 2 + part), last)
            far[h, 1, part] = message(
                stage_v.at[h, 3, 3 + part, half_rows], relay_v.at[h, part, 3, half_rows], there
            )
            passed[h, 1, part] = message(
                relay_v.at[h, part, 3, half_rows], recv_v.at[START[AWAY_LONG] + h * 2 + part, half_rows], last
            )
            for dc in range(N_C):
                strip[h, part, dc] = message(
                    stage_v.at[h, 3, PACKED.index((sign % 4, dc)), rows],
                    strip_v.at[dc * 4 + h * 2 + part],
                    along(h, 0, sign, dc),
                )
            for m, piece in enumerate(pieces):
                for dc in range(N_C):
                    ahead[h, m, part, dc] = message(
                        stage_v.at[h, piece, PACKED.index((sign % 4, dc))],
                        place((BESIDE, BESIDE_CROSS)[dc], h * 2 + part) if m == 0 else place(BESIDE_LONG, dc * 4 + h * 2 + part),
                        along(h, 0, sign, dc),
                    )
        for m, piece in enumerate(pieces):
            inside[h, m] = message(stage_v.at[h, piece, 1], place((NEAR, NEAR_LONG)[m], h * 2 + 1), at(0, 0, 1))
            own[h, m] = pltpu.make_async_copy(stage_v.at[h, piece, 0], place((NEAR, NEAR_LONG)[m], h * 2), own_sems.at[h, m])
        step = (1 - 2 * parity) * (1 - 2 * h)
        plane = lax.rem(z + step + N_Z, N_Z)
        both = pl.ds(START[AWAY_LONG] + h * 2, 2)
        swap[h] = message(recv_v.at[both, half_rows], recv_v.at[both, half_rows], me, plane)
        swapped[h] = pltpu.make_async_remote_copy(
            src_ref=recv_v.at[both, other_rows], dst_ref=recv_v.at[both, other_rows],
            send_sem=send_sems.at[count[0] - 1], recv_sem=recv_sems.at[count[0] - 1],
            device_id=(me, plane), device_id_type=MESH,
        )

    def ring(part, t, chunk, source):
        piece = left_v.at[source, pl.ds(chunk * per_ring, per_ring)]
        return pltpu.make_async_remote_copy(
            src_ref=piece, dst_ref=piece,
            send_sem=ring_send.at[part, t, chunk], recv_sem=ring_recv.at[part, t, chunk],
            device_id=(me, lax.rem(z + SIGNS[part] + N_Z, N_Z)), device_id_type=MESH,
        )

    def ring_out(part, t, chunk):
        return ring(part, t, chunk, lax.rem(z - SIGNS[part] * t + N_Z, N_Z))

    def ring_in(part, t, chunk):
        return ring(part, t, chunk, lax.rem(z - SIGNS[part] * (t + 1) + N_Z, N_Z))

    def travels(part, t, chunk):
        return t < 3 or chunk % 2 == part

    def pass_on(t, *chunks):
        for chunk in chunks:
            for part in range(2):
                if travels(part, t, chunk):
                    ring_in(part, t, chunk).wait_recv()
                if t < 3 and travels(part, t + 1, chunk):
                    ring_out(part, t + 1, chunk).start()

    def begin(chunk):
        for part in range(2):
            ring_out(part, 0, chunk).start()

    def fold(values):
        values = values[:, :128] + values[:, 128:]
        return jnp.sum(values.reshape(values.shape[0] // 8, 8, 128), axis=0)

    def in_fours(kind, some):
        def one(i, carry):
            places = [START[kind] + 4 * i + j for j in range(4)]
            some(places, [slot_of(kind, pos) for pos in places])
            return carry

        lax.fori_loop(0, (START[kind + 1] - START[kind]) // 4, one, 0)

    def square_ratio(grad, k):
        grad32 = grad.astype(jnp.float32)
        moment_one = 0.9 * mone_v[k] + 0.1 * grad32
        moment_two = 0.999 * mtwo_v[k] + 0.001 * grad32 * grad32
        ratio = moment_one / (jnp.sqrt(moment_two) + 1e-08)
        adam_v[k] = fold(ratio * ratio)

    def absorb(kind, adam=True, product=True):
        def some(places, ks):
            for pos, k in zip(places, ks) if adam else ():
                square_ratio(recv_v[pos, rows, :], k)
            for pos, k in zip(places, ks) if product else ():
                right = jnp.dot(recv_v[pos], right_v[k], preferred_element_type=jnp.float32)
                recv_v[pos] = right.astype(jnp.bfloat16)

        in_fours(kind, some)

    def adam_of_strips():
        def some(places, ks):
            for pos, k in zip(places, ks):
                square_ratio(strip_v[pos - START[BESIDE_LONG]], k)
                square_v[k] = jnp.zeros((8, 128), jnp.float32)

        in_fours(BESIDE_LONG, some)

    def finish(kind):
        def some(places, ks):
            for pos, k in zip(places, ks):
                precond = jnp.dot(
                    left_v[:, pos].reshape(order, order), recv_v[pos], preferred_element_type=jnp.float32
                )
                square_v[k] = fold(precond * precond)
                recv_v[pos] = precond.astype(jnp.bfloat16)

        in_fours(kind, some)

    def count_live():
        shard = lax.broadcasted_iota(jnp.int32, (owner.shape[1], 128), 0) // per_shard
        slot = lax.broadcasted_iota(jnp.int32, (owner.shape[1], 128), 1)
        ours = jnp.broadcast_to(jnp.where(owner[...] == me, 1.0, 0.0), (8, owner.shape[1]))
        counts = jnp.dot(
            ours.astype(jnp.bfloat16),
            jnp.where(shard == slot // 2, 1.0, 0.0).astype(jnp.bfloat16),
            preferred_element_type=jnp.float32,
        )[:1]
        rank = lax.rem(slot[:1], 2).astype(jnp.float32)
        live_v[...] = jnp.where(counts > rank, 1.0, 0.0)

    def by_lane(sums):
        by_slot = jnp.sum(jnp.sum(sums, axis=1), axis=1, keepdims=True)
        spread = jnp.broadcast_to(by_slot, (slots, 128))
        return jnp.sum(jnp.where(diagonal, spread, 0.0), axis=0, keepdims=True)

    diagonal = lax.broadcasted_iota(jnp.int32, (slots, 128), 0) == lax.broadcasted_iota(
        jnp.int32, (slots, 128), 1
    )

    every = [(h, part) for h in range(2) for part in range(2)]
    thirds = ((0, 1, 2), (5, 6, 7), (3, 4))

    def ready(chunk):
        first = pl.ds(chunk * per_ring, per_ring)
        pltpu.make_async_copy(left_hbm.at[first], left_v.at[z, first], left_sems.at[chunk]).wait()
        begin(chunk)

    for chunk in range(RING):
        ready(chunk)
    to_scalars.wait()
    for load in grad_loads:
        load.wait()
    for load in loads:
        load.start()
    for h, part in every:
        pack(h, 2, (3 + part,), out_v.at[h, 2])
        via[h, 1, part].start()
    for h, part in every:
        pack(h, 2, thirds[part], out_v.at[h, 2])
        via[h, 0, part].start()
    for h, part in every:
        pack(h, SIGNS[part], thirds[2], out_v.at[h, part])
        straight[h, 2, part].start()
    for h, part in every:
        via[h, 1, part].wait_recv()
        onward[h, 1, part].start()
    for b in range(2):
        for h, part in every:
            pack(h, SIGNS[part], thirds[b], out_v.at[h, part])
            straight[h, b, part].start()
    for h in range(2):
        pack(h, 0, range(8), stage_v.at[h, 1])
    count_live()

    pass_on(0, 0)
    for h, part in every:
        via[h, 0, part].wait_recv()
        onward[h, 0, part].start()
    pass_on(0, 1)
    for h, part in every:
        onward[h, 1, part].wait_recv()
        far[h, 1, part].start()
    for h, part in every:
        straight[h, 2, part].wait_recv()
    for h, part in every:
        far[h, 0, part].start()
    pass_on(0, 2, 3)
    pass_on(1, 0)
    for h, part in every:
        for b in range(2):
            straight[h, b, part].wait_recv()
    for h, part in every:
        ahead[h, 0, part, 0].start()
    for h in range(2):
        inside[h, 0].start()
        own[h, 0].start()
    pass_on(1, 1, 2)
    for h, part in every:
        onward[h, 0, part].wait_recv()
    for dc in range(N_C):
        for h, part in every:
            strip[h, part, dc].start()
    for h in range(2):
        inside[h, 1].start()
        own[h, 1].start()
    for h, part in every:
        far[h, 1, part].wait_recv()
        passed[h, 1, part].start()
    for load in loads:
        load.wait()
    first_late = START[BESIDE_LONG]
    to_late = [
        pltpu.make_async_copy(right_v.at[slot_of(BESIDE_LONG, first_late + i)], right_late.at[i], late_sems.at[i])
        for i in range(slots - first_late)
    ]
    for copy in to_late:
        copy.start()
    for m in range(2):
        for h in range(2):
            own[h, m].wait()
            inside[h, m].wait_recv()
    absorb(NEAR)
    absorb(NEAR_LONG)
    pass_on(1, 3)
    for h, part in every:
        far[h, 0, part].wait_recv()
        passed[h, 0, part].start()
    for h, part in every:
        ahead[h, 0, part, 1].start()
    for dc in range(N_C):
        for h, part in every:
            ahead[h, 1, part, dc].start()
    pass_on(2, 0, 1)
    for h, part in every:
        ahead[h, 0, part, 0].wait_recv()
    for h in range(2):
        for part in range(2):
            passed[h, 1, part].wait_recv()
        swap[h].start()
    absorb(BESIDE)
    pass_on(2, 2, 3)
    for h, part in every:
        passed[h, 0, part].wait_recv()
    for dc in range(N_C):
        for h, part in every:
            strip[h, part, dc].wait_recv()
    adam_of_strips()
    absorb(AWAY)
    pass_on(3, 0, 1)
    for kind in (NEAR, NEAR_LONG, BESIDE):
        finish(kind)
    for h in range(2):
        swapped[h].wait_recv()
        swap[h].wait_send()
    absorb(AWAY_LONG)
    finish(AWAY_LONG)
    for h, part in every:
        ahead[h, 0, part, 1].wait_recv()
    absorb(BESIDE_CROSS, product=False)
    tiles_v[0] = jnp.broadcast_to(by_lane(adam_v[...]), (8, 128))

    def tell(dz):
        return pltpu.make_async_remote_copy(
            src_ref=tiles_v.at[0],
            dst_ref=tiles_v.at[dz],
            send_sem=zsend.at[dz],
            recv_sem=zrecv.at[dz],
            device_id=(me, lax.rem(z + dz, N_Z)),
            device_id_type=MESH,
        )

    for dz in range(1, N_Z):
        tell(dz).start()
    absorb(BESIDE_CROSS, adam=False)
    pass_on(3, 2)
    finish(AWAY)
    pass_on(3, 3)
    to_late.append(
        pltpu.make_async_copy(
            left_v.at[:, pl.ds(first_late, slots - first_late)], left_late, late_sems.at[slots - first_late]
        )
    )
    to_late[-1].start()
    finish(BESIDE_CROSS)
    sum_pre = by_lane(square_v[...])
    for dz in range(1, N_Z):
        tell(dz).wait()
    sum_adam = jnp.sum(tiles_v[...], axis=0)[:1]
    lane = lax.broadcasted_iota(jnp.int32, (1, 128), 1)
    dy = lax.rem(lane // (2 * N_X * N_C) - y + 2 * N_Y, N_Y)
    dx = lax.rem(lax.rem(lane // (2 * N_C), N_X) - x + N_X, N_X)
    odd = lax.rem(lane, 2) == 1
    later = (jnp.where(odd, dy, dx) == 2) & (lax.rem(jnp.where(odd, dx, dy), 2) == 1)
    norm = live_v[...] * jnp.sqrt(sum_adam / total)
    scale = jnp.where(later, norm, norm / jnp.sqrt(sum_pre / total + 1e-06))
    by_row = jnp.where(diagonal, jnp.broadcast_to(scale, (slots, 128)), 0.0)
    scale_out[...] = jnp.broadcast_to(jnp.sum(by_row, axis=1, keepdims=True), (slots, 128))
    for copy in to_late:
        copy.wait()
    for dc in range(N_C):
        for h, part in every:
            ahead[h, 1, part, dc].wait_recv()
    for group in (via, straight, onward, far, ahead, inside, passed, strip):
        for copy in group.values():
            copy.wait_send()
    for t in range(4):
        for chunk in range(RING):
            for part in range(2):
                if travels(part, t, chunk):
                    ring_out(part, t, chunk).wait_send()


def step(owner, grads, left, right, mone, mtwo):
    per_shard, order, _ = grads.shape
    slots, share, _ = mone.shape
    block = (order, order)
    late = slots - START[BESIDE_LONG]
    anywhere = pl.BlockSpec(memory_space=pl.ANY)
    vmem = pl.BlockSpec(memory_space=pltpu.VMEM)
    dma = pltpu.SemaphoreType.DMA
    return pl.pallas_call(
        step_kernel,
        out_shape=(
            pltpu.VMEM((slots, *block), jnp.bfloat16),
            pltpu.VMEM((N_Z, late, share, order), jnp.bfloat16),
            pltpu.VMEM((late, *block), jnp.bfloat16),
            pltpu.VMEM((slots, 128), jnp.float32),
        ),
        in_specs=[vmem] + [anywhere] * 5,
        out_specs=(vmem, vmem, vmem, vmem),
        scratch_shapes=[
            pltpu.VMEM((per_shard + 1, *block), jnp.bfloat16),
            pltpu.VMEM((2, 3, 8, *block), jnp.bfloat16),
            pltpu.VMEM((2, 4, 8, *block), jnp.bfloat16),
            pltpu.VMEM((2, 2, 4, *block), jnp.bfloat16),
            pltpu.VMEM((2, 2, 4, *block), jnp.bfloat16),
            pltpu.VMEM((N_Z, slots, share, order), jnp.bfloat16),
            pltpu.VMEM((slots, *block), jnp.bfloat16),
            pltpu.VMEM((slots, share, order), jnp.float32),
            pltpu.VMEM((slots, share, order), jnp.float32),
            pltpu.VMEM((slots, 8, 128), jnp.float32),
            pltpu.VMEM((slots, 8, 128), jnp.float32),
            pltpu.VMEM((N_Z, 8, 128), jnp.float32),
            pltpu.VMEM((8, share, order), jnp.bfloat16),
            pltpu.VMEM((1, 128), jnp.float32),
            pltpu.VMEM((1, 128), jnp.int32),
            pltpu.SMEM((1, 128), jnp.int32),
            dma((7,)),
            dma((RING,)),
            dma((2, 2)),
            dma((late + 1,)),
            dma,
            dma((74,)),
            dma((74,)),
            dma((2, 4, RING)),
            dma((2, 4, RING)),
            dma((N_Z,)),
            dma((N_Z,)),
        ],
        compiler_params=pltpu.CompilerParams(
            collective_id=0, has_side_effects=True, vmem_limit_bytes=LIMIT * 2**20
        ),
        cost_estimate=pl.CostEstimate(
            flops=4 * slots * order**3, bytes_accessed=4 * 10**8, transcendentals=10**6
        ),
    )(owner, grads, left, right, mone, mtwo)


def scale_kernel(x, left, right, scale, out, ready, sems):
    me = lax.axis_index("dp")
    order = x.shape[1]
    last = START[BESIDE_LONG]

    def copy(kind, pos):
        return pltpu.make_async_copy(ready.at[pos], out.at[slot_at(me, kind, pos)], sems.at[pos])

    def row(kind, pos):
        return scale[pl.ds(slot_at(me, kind, pos), 1), :]

    def in_fours(kind, some):
        def one(i, carry):
            places = [START[kind] + 4 * i + j for j in range(4)]
            some(places)
            for pos in places:
                copy(kind, pos).start()
            return carry

        lax.fori_loop(0, (START[kind + 1] - START[kind]) // 4, one, 0)

    def store(pos, values, factor):
        ready[pos] = (values * jnp.concatenate([factor, factor], axis=1)).astype(jnp.bfloat16)

    for kind in range(BESIDE_LONG):

        def scaled(places):
            for pos in places:
                store(pos, x[pos].astype(jnp.float32), row(kind, pos))

        in_fours(kind, scaled)

    def whole(places):
        halves = [
            jnp.dot(
                left[:, pos - last].reshape(order, order), x[pos], preferred_element_type=jnp.float32
            ).astype(jnp.bfloat16)
            for pos in places
        ]
        preconds = [
            jnp.dot(half, right[pos - last], preferred_element_type=jnp.float32)
            for pos, half in zip(places, halves)
        ]
        for pos, precond in zip(places, preconds):
            mean = jnp.sum(precond * precond, axis=(0, 1), keepdims=True) / float(order * order) + 1e-06
            store(pos, precond, row(BESIDE_LONG, pos) / jnp.sqrt(mean))

    in_fours(BESIDE_LONG, whole)
    for kind in range(BESIDE_LONG + 1):

        def settle(pos, carry):
            copy(kind, pos).wait()
            return carry

        lax.fori_loop(START[kind], START[kind + 1], settle, 0)


def apply_scale(x, left, right, scale):
    vmem, anywhere = pl.BlockSpec(memory_space=pltpu.VMEM), pl.BlockSpec(memory_space=pl.ANY)
    return pl.pallas_call(
        scale_kernel,
        out_shape=jax.ShapeDtypeStruct(x.shape, jnp.bfloat16),
        in_specs=[vmem] * 4,
        out_specs=anywhere,
        scratch_shapes=[
            pltpu.VMEM(x.shape, jnp.bfloat16),
            pltpu.SemaphoreType.DMA((x.shape[0],)),
        ],
        compiler_params=pltpu.CompilerParams(vmem_limit_bytes=24 * 2**20),
    )(x, left, right, scale)


def per_device(grads, owner, left_root, right_root, first_moment, second_moment):
    x, left, right, scale = step(
        owner.reshape(1, -1), grads, left_root[0], right_root[0], first_moment[0], second_moment[0]
    )
    return apply_scale(x, left, right, scale)[None]


def solution(mesh):
    placed = (
        P("dp", None, None),
        P(),
        P("dp", None, "replica", None),
        P("dp", None, None, None),
        P("dp", None, "replica", None),
        P("dp", None, "replica", None),
    )
    return jax.shard_map(
        per_device, mesh=mesh, in_specs=placed, out_specs=P("dp", None, None, None), check_vma=False
    )
```

```python
import functools

import jax
import jax.numpy as jnp
from jax import lax
from jax.experimental import pallas as pl
from jax.experimental.pallas import tpu as pltpu
from jax.sharding import PartitionSpec as P

MESH = pl.DeviceIdType.MESH
N_Y, N_X, N_C = 4, 4, 2
N_DP = N_Y * N_X * N_C
N_Z = 8
RING = 4
SIGNS = (1, -1)
LIMIT = 48

NEAR, NEAR_LONG, BESIDE, AWAY_LONG, AWAY, BESIDE_CROSS, BESIDE_LONG = range(7)
START = (0, 12, 16, 28, 32, 44, 56, 64)
PACKED = ((0, 0), (0, 1), (1, 0), (2, 0), (2, 1), (1, 1), (3, 0), (3, 1))
FULL = (pl.ds(0, 3), pl.ds(5, 3))


def decode(kind, q):
    long = kind in (NEAR_LONG, AWAY_LONG, BESIDE_LONG)
    d, g = (3, q) if long else (lax.rem(q, 3), q // 3)
    first, low = lax.rem(d + 3, 4), lax.rem(g, 2)
    if kind in (NEAR, NEAR_LONG):
        return g // 2, first, 0, low
    if kind in (AWAY, AWAY_LONG):
        return g // 2, first, 2, low
    return lax.rem(g // 2, 2), first, 3 - 2 * low, g // 4 if kind == BESIDE_LONG else int(kind == BESIDE_CROSS)


def slot_at(me, kind, pos):
    y, x, c = me // (N_X * N_C), (me // N_C) % N_X, me % N_C
    half, first, second, dc = decode(kind, pos - START[kind])
    dy, dx = second + half * (first - second), first + half * (second - first)
    source = lax.rem(y + dy, N_Y) * (N_X * N_C) + lax.rem(x + dx, N_X) * N_C + lax.rem(c + dc, N_C)
    return 2 * source + half


def step_kernel(
    owner, grads_hbm, left_hbm, right_hbm, mone_hbm, mtwo_hbm, recv_v, left_late, right_late, scale_out,
    grads_v, out_v, stage_v, pass_v, relay_v, left_v, right_v, mone_v, mtwo_v,
    adam_v, square_v, tiles_v, live_v, idx_v, idx,
    load_sems, left_sems, own_sems, late_sems, idx_sem, send_sems, recv_sems, ring_send, ring_recv, zsend, zrecv,
):
    me, z = lax.axis_index("dp"), lax.axis_index("replica")
    per_shard, order = grads_hbm.shape[0], grads_hbm.shape[1]
    slots, share = mone_hbm.shape[0], mone_hbm.shape[1]
    total = float(order * order)
    per_ring = slots // RING
    y, x, c = me // (N_X * N_C), (me // N_C) % N_X, me % N_C

    def at(dy, dx, dc):
        return (
            lax.rem(y + dy + N_Y, N_Y) * (N_X * N_C) + lax.rem(x + dx + N_X, N_X) * N_C + lax.rem(c + dc, N_C)
        )

    def along(half, first, second, dc):
        return at(second + half * (first - second), first + half * (second - first), dc)

    def slot_of(kind, pos):
        return slot_at(me, kind, pos)

    quarter = per_shard // 4
    grad_loads = [
        pltpu.make_async_copy(grads_hbm.at[some], grads_v.at[some], load_sems.at[i])
        for i, some in enumerate(pl.ds(quarter * i, quarter) for i in range(4))
    ]
    loads = [
        pltpu.make_async_copy(mone_hbm, mone_v, load_sems.at[4]),
        pltpu.make_async_copy(mtwo_hbm, mtwo_v, load_sems.at[5]),
        pltpu.make_async_copy(right_hbm, right_v, load_sems.at[6]),
    ]
    for load in grad_loads:
        load.start()

    barrier = pltpu.get_barrier_semaphore()
    near = [(0, 0, 1)] + [(dy, dx, dc) for dy, dx in ((0, 1), (0, -1), (1, 0), (-1, 0)) for dc in range(N_C)]
    for step in near:
        pl.semaphore_signal(barrier, inc=1, device_id=(at(*step), z), device_id_type=MESH)
    for dz in range(1, N_Z):
        pl.semaphore_signal(barrier, inc=1, device_id=(me, lax.rem(z + dz, N_Z)), device_id_type=MESH)

    row = lax.broadcasted_iota(jnp.int32, (per_shard, 128), 0)
    lane = lax.broadcasted_iota(jnp.int32, (per_shard, 128), 1)
    per_line = 128 // per_shard
    line = owner[:, pl.ds(pl.multiple_of(me // per_line * 128, 128), 128)]
    mine = pltpu.roll(
        jnp.broadcast_to(line, (per_shard, 128)), lax.rem(128 - lax.rem(me, per_line) * per_shard, 128), 1
    )
    names = jnp.sum(jnp.where(row == lane, mine, 0), axis=1, keepdims=True)
    ranks = jnp.sum(jnp.where((names == mine) & (lane < row), 1, 0), axis=1, keepdims=True)
    found = jnp.where(2 * names + ranks == lane, row - per_shard, 0)
    idx_v[...] = per_shard + jnp.sum(found, axis=0, keepdims=True)
    to_scalars = pltpu.make_async_copy(idx_v, idx, idx_sem)
    to_scalars.start()
    for kind in range(7):

        def load_left(pos, carry):
            pltpu.make_async_copy(
                left_hbm.at[slot_of(kind, pos)], left_v.at[z, pos], left_sems.at[pos // per_ring]
            ).start()
            return carry

        lax.fori_loop(START[kind], START[kind + 1], load_left, 0)
    grads_v[per_shard] = jnp.zeros((order, order), jnp.bfloat16)
    pl.semaphore_wait(barrier, len(near) + N_Z - 1)

    def pack(half, first, places, into):
        for i in places:
            p = along(half, first, *PACKED[i])
            into[i] = grads_v[idx[0, 2 * p + half]]

    count = [0]

    def message(src, dst, target, plane=z):
        n = count[0]
        count[0] += 1
        return pltpu.make_async_remote_copy(
            src_ref=src, dst_ref=dst, send_sem=send_sems.at[n], recv_sem=recv_sems.at[n],
            device_id=(target, plane), device_id_type=MESH,
        )

    def place(kind, g, some=slice(None)):
        n = 1 if kind in (NEAR_LONG, AWAY_LONG, BESIDE_LONG) else 3
        return recv_v.at[pl.ds(START[kind] + n * g, n), some]

    parity = lax.rem(z, 2)
    half_rows = pl.ds(pl.multiple_of(parity * (order // 2), order // 2), order // 2)
    other_rows = pl.ds(pl.multiple_of((1 - parity) * (order // 2), order // 2), order // 2)
    pieces = (pl.ds(0, 3), pl.ds(3, 1))
    via, straight, onward = {}, {}, {}
    far, ahead, inside, passed, own, swap, swapped, halves = {}, {}, {}, {}, {}, {}, {}, {}
    rows = pl.ds(pl.multiple_of(z * share, share), share)
    upper = z // (N_Z // 2) * (order // 2)
    in_order = [pl.ds(pl.multiple_of(r, order // 2), order // 2) for r in (upper, order // 2 - upper)]
    for h in range(2):
        for part, sign in enumerate(SIGNS):
            there = along(h, sign, 0, 0)
            for b, some in enumerate((*FULL, pl.ds(3, 2))):
                straight[h, b, part] = message(out_v.at[h, part, some], stage_v.at[h, 2 * part, some], there)
            via[h, 0, part] = message(out_v.at[h, 2, FULL[part]], pass_v.at[h, part, pl.ds(0, 3)], there)
            onward[h, 0, part] = message(pass_v.at[h, part, pl.ds(0, 3)], stage_v.at[h, 3, FULL[part]], there)
            via[h, 1, part] = message(
                out_v.at[h, 2, 3 + part, half_rows], pass_v.at[h, part, 3, half_rows], there
            )
            onward[h, 1, part] = message(
                pass_v.at[h, part, 3, half_rows], stage_v.at[h, 3, 3 + part, half_rows], there
            )
            there = along(h, 0, sign, 0)
            last = along(h, 0, sign, part)
            far[h, 0, part] = message(
                stage_v.at[h, pieces[0], 3 + part], relay_v.at[h, part, pieces[0]], there
            )
            for q, some in enumerate(in_order):
                halves[AWAY, q, h, part] = message(
                    relay_v.at[h, part, pieces[0], some], place(AWAY, h * 2 + part, some), last
                )
            far[h, 1, part] = message(
                stage_v.at[h, 3, 3 + part, half_rows], relay_v.at[h, part, 3, half_rows], there
            )
            passed[h, part] = message(
                relay_v.at[h, part, 3, half_rows], recv_v.at[START[AWAY_LONG] + h * 2 + part, half_rows], last
            )
            beside = [PACKED.index((sign % 4, dc)) for dc in range(N_C)]
            ahead[h, part] = message(
                stage_v.at[h, pieces[0], beside[0]], place(BESIDE, h * 2 + part), along(h, 0, sign, 0)
            )
            for q, some in enumerate(in_order):
                halves[BESIDE_CROSS, q, h, part] = message(
                    stage_v.at[h, pieces[0], beside[1], some],
                    place(BESIDE_CROSS, h * 2 + part, some),
                    along(h, 0, sign, 1),
                )
                for dc in range(N_C):
                    halves[BESIDE_LONG, q, h, part, dc] = message(
                        stage_v.at[h, pieces[1], beside[dc], some],
                        place(BESIDE_LONG, dc * 4 + h * 2 + part, some),
                        along(h, 0, sign, dc),
                    )
        for m, piece in enumerate(pieces):
            inside[h, m] = message(stage_v.at[h, piece, 1], place((NEAR, NEAR_LONG)[m], h * 2 + 1), at(0, 0, 1))
            own[h, m] = pltpu.make_async_copy(stage_v.at[h, piece, 0], place((NEAR, NEAR_LONG)[m], h * 2), own_sems.at[h, m])
        step = (1 - 2 * parity) * (1 - 2 * h)
        plane = lax.rem(z + step + N_Z, N_Z)
        both = pl.ds(START[AWAY_LONG] + h * 2, 2)
        swap[h] = message(recv_v.at[both, half_rows], recv_v.at[both, half_rows], me, plane)
        swapped[h] = pltpu.make_async_remote_copy(
            src_ref=recv_v.at[both, other_rows], dst_ref=recv_v.at[both, other_rows],
            send_sem=send_sems.at[count[0] - 1], recv_sem=recv_sems.at[count[0] - 1],
            device_id=(me, plane), device_id_type=MESH,
        )

    def ring(part, t, chunk, source):
        piece = left_v.at[source, pl.ds(chunk * per_ring, per_ring)]
        return pltpu.make_async_remote_copy(
            src_ref=piece, dst_ref=piece,
            send_sem=ring_send.at[part, t, chunk], recv_sem=ring_recv.at[part, t, chunk],
            device_id=(me, lax.rem(z + SIGNS[part] + N_Z, N_Z)), device_id_type=MESH,
        )

    def ring_out(part, t, chunk):
        return ring(part, t, chunk, lax.rem(z - SIGNS[part] * t + N_Z, N_Z))

    def ring_in(part, t, chunk):
        return ring(part, t, chunk, lax.rem(z - SIGNS[part] * (t + 1) + N_Z, N_Z))

    def travels(part, t, chunk):
        return t < 3 or chunk % 2 == part

    def pass_on(t, *chunks, forward=True):
        for chunk in chunks:
            for part in range(2):
                if travels(part, t, chunk):
                    ring_in(part, t, chunk).wait_recv()
                if forward and t < 3 and travels(part, t + 1, chunk):
                    ring_out(part, t + 1, chunk).start()

    def begin(chunk):
        for part in range(2):
            ring_out(part, 0, chunk).start()

    def fold(values):
        values = values[:, :128] + values[:, 128:]
        return jnp.sum(values.reshape(values.shape[0] // 8, 8, 128), axis=0)

    def in_fours(kind, some):
        def one(i, carry):
            places = [START[kind] + 4 * i + j for j in range(4)]
            some(places, [slot_of(kind, pos) for pos in places])
            return carry

        lax.fori_loop(0, (START[kind + 1] - START[kind]) // 4, one, 0)

    def square_ratio(grad, k):
        grad32 = grad.astype(jnp.float32)
        moment_one = 0.9 * mone_v[k] + 0.1 * grad32
        moment_two = 0.999 * mtwo_v[k] + 0.001 * grad32 * grad32
        ratio = moment_one / (jnp.sqrt(moment_two) + 1e-08)
        adam_v[k] = fold(ratio * ratio)

    def absorb(kind, adam=True, product=True):
        def some(places, ks):
            for pos, k in zip(places, ks) if adam else ():
                square_ratio(recv_v[pos, rows, :], k)
                if kind == BESIDE_LONG:
                    square_v[k] = jnp.zeros((8, 128), jnp.float32)
            for pos, k in zip(places, ks) if product else ():
                right = jnp.dot(recv_v[pos], right_v[k], preferred_element_type=jnp.float32)
                recv_v[pos] = right.astype(jnp.bfloat16)

        in_fours(kind, some)

    def finish(kind):
        def some(places, ks):
            for pos, k in zip(places, ks):
                precond = jnp.dot(
                    left_v[:, pos].reshape(order, order), recv_v[pos], preferred_element_type=jnp.float32
                )
                square_v[k] = fold(precond * precond)
                recv_v[pos] = precond.astype(jnp.bfloat16)

        in_fours(kind, some)

    def count_live():
        shard = lax.broadcasted_iota(jnp.int32, (owner.shape[1], 128), 0) // per_shard
        slot = lax.broadcasted_iota(jnp.int32, (owner.shape[1], 128), 1)
        ours = jnp.broadcast_to(jnp.where(owner[...] == me, 1.0, 0.0), (8, owner.shape[1]))
        counts = jnp.dot(
            ours.astype(jnp.bfloat16),
            jnp.where(shard == slot // 2, 1.0, 0.0).astype(jnp.bfloat16),
            preferred_element_type=jnp.float32,
        )[:1]
        rank = lax.rem(slot[:1], 2).astype(jnp.float32)
        live_v[...] = jnp.where(counts > rank, 1.0, 0.0)

    def by_lane(sums):
        by_slot = jnp.sum(jnp.sum(sums, axis=1), axis=1, keepdims=True)
        spread = jnp.broadcast_to(by_slot, (slots, 128))
        return jnp.sum(jnp.where(diagonal, spread, 0.0), axis=0, keepdims=True)

    diagonal = lax.broadcasted_iota(jnp.int32, (slots, 128), 0) == lax.broadcasted_iota(
        jnp.int32, (slots, 128), 1
    )

    every = [(h, part) for h in range(2) for part in range(2)]
    thirds = ((0, 1, 2), (5, 6, 7), (3, 4))

    def ready(chunk):
        first = pl.ds(chunk * per_ring, per_ring)
        pltpu.make_async_copy(left_hbm.at[first], left_v.at[z, first], left_sems.at[chunk]).wait()
        begin(chunk)

    for chunk in range(RING):
        ready(chunk)
    to_scalars.wait()
    for load in grad_loads:
        load.wait()
    for load in loads:
        load.start()
    for h, part in every:
        pack(h, 2, (3 + part,), out_v.at[h, 2])
        via[h, 1, part].start()
    for h, part in every:
        pack(h, 2, thirds[part], out_v.at[h, 2])
        via[h, 0, part].start()
    for h, part in every:
        pack(h, SIGNS[part], thirds[2], out_v.at[h, part])
        straight[h, 2, part].start()
    for h, part in every:
        via[h, 1, part].wait_recv()
        onward[h, 1, part].start()
    for h, part in every:
        for b in range(2):
            pack(h, SIGNS[part], thirds[b], out_v.at[h, part])
    for h in range(2):
        pack(h, 0, range(8), stage_v.at[h, 1])
    count_live()

    def halves_of(kind, q):
        return [copy for key, copy in halves.items() if key[:2] == (kind, q)]

    pass_on(0, 0)
    for h, part in every:
        onward[h, 1, part].wait_recv()
        far[h, 1, part].start()
    for b in range(2):
        for h, part in every:
            straight[h, b, part].start()
    for h, part in every:
        via[h, 0, part].wait_recv()
        onward[h, 0, part].start()
    pass_on(0, 1)
    for h, part in every:
        straight[h, 2, part].wait_recv()
    for h, part in every:
        far[h, 0, part].start()
    for h, part in every:
        far[h, 1, part].wait_recv()
        passed[h, part].start()
    pass_on(0, 2, 3)
    pass_on(1, 0)
    for h, part in every:
        for b in range(2):
            straight[h, b, part].wait_recv()
    for h, part in every:
        ahead[h, part].start()
    for h in range(2):
        inside[h, 0].start()
        own[h, 0].start()
    pass_on(1, 1, 2)
    for h, part in every:
        onward[h, 0, part].wait_recv()
    for h in range(2):
        inside[h, 1].start()
        own[h, 1].start()
    for h in range(2):
        for part in range(2):
            passed[h, part].wait_recv()
        swap[h].start()
    for load in loads:
        load.wait()
    first_late = START[BESIDE_LONG]
    to_late = [
        pltpu.make_async_copy(right_v.at[slot_of(BESIDE_LONG, first_late + i)], right_late.at[i], late_sems.at[i])
        for i in range(slots - first_late)
    ]
    for copy in to_late:
        copy.start()
    for m in range(2):
        for h in range(2):
            own[h, m].wait()
            inside[h, m].wait_recv()
    absorb(NEAR)
    absorb(NEAR_LONG)
    pass_on(1, 3)
    for h, part in every:
        far[h, 0, part].wait_recv()
    for q in range(2):
        for kind in (AWAY, BESIDE_CROSS, BESIDE_LONG):
            for copy in halves_of(kind, q):
                copy.start()
    pass_on(2, 0, 1)
    for h in range(2):
        swapped[h].wait_recv()
        swap[h].wait_send()
    absorb(AWAY_LONG)
    for h, part in every:
        ahead[h, part].wait_recv()
    absorb(BESIDE)
    pass_on(2, 2, forward=False)
    for kind in (AWAY, BESIDE_CROSS, BESIDE_LONG):
        for copy in halves_of(kind, 0):
            copy.wait_recv()
        absorb(kind, product=False)
    tiles_v[0] = jnp.broadcast_to(by_lane(adam_v[...]), (8, 128))

    def tell(dz):
        return pltpu.make_async_remote_copy(
            src_ref=tiles_v.at[0],
            dst_ref=tiles_v.at[dz],
            send_sem=zsend.at[dz],
            recv_sem=zrecv.at[dz],
            device_id=(me, lax.rem(z + dz, N_Z)),
            device_id_type=MESH,
        )

    for dz in range(1, N_Z):
        tell(dz).start()
    pass_on(2, 3, forward=False)
    for chunk in (2, 3):
        for part in range(2):
            if travels(part, 3, chunk):
                ring_out(part, 3, chunk).start()
    for copy in halves_of(AWAY, 1):
        copy.wait_recv()
    absorb(AWAY, adam=False)
    pass_on(3, 0, 1)
    for kind in (NEAR, NEAR_LONG, BESIDE, AWAY_LONG):
        finish(kind)
    for copy in halves_of(BESIDE_CROSS, 1):
        copy.wait_recv()
    absorb(BESIDE_CROSS, adam=False)
    pass_on(3, 2)
    finish(AWAY)
    pass_on(3, 3)
    to_late.append(
        pltpu.make_async_copy(
            left_v.at[:, pl.ds(first_late, slots - first_late)], left_late, late_sems.at[slots - first_late]
        )
    )
    to_late[-1].start()
    finish(BESIDE_CROSS)
    sum_pre = by_lane(square_v[...])
    for dz in range(1, N_Z):
        tell(dz).wait()
    sum_adam = jnp.sum(tiles_v[...], axis=0)[:1]
    lane = lax.broadcasted_iota(jnp.int32, (1, 128), 1)
    dy = lax.rem(lane // (2 * N_X * N_C) - y + 2 * N_Y, N_Y)
    dx = lax.rem(lax.rem(lane // (2 * N_C), N_X) - x + N_X, N_X)
    odd = lax.rem(lane, 2) == 1
    later = (jnp.where(odd, dy, dx) == 2) & (lax.rem(jnp.where(odd, dx, dy), 2) == 1)
    norm = live_v[...] * jnp.sqrt(sum_adam / total)
    scale = jnp.where(later, norm, norm / jnp.sqrt(sum_pre / total + 1e-06))
    by_row = jnp.where(diagonal, jnp.broadcast_to(scale, (slots, 128)), 0.0)
    scale_out[...] = jnp.broadcast_to(jnp.sum(by_row, axis=1, keepdims=True), (slots, 128))
    for copy in to_late:
        copy.wait()
    for copy in halves_of(BESIDE_LONG, 1):
        copy.wait_recv()
    for group in (via, straight, onward, far, ahead, inside, passed, halves):
        for copy in group.values():
            copy.wait_send()
    for t in range(4):
        for chunk in range(RING):
            for part in range(2):
                if travels(part, t, chunk):
                    ring_out(part, t, chunk).wait_send()


def step(owner, grads, left, right, mone, mtwo):
    per_shard, order, _ = grads.shape
    slots, share, _ = mone.shape
    block = (order, order)
    late = slots - START[BESIDE_LONG]
    anywhere = pl.BlockSpec(memory_space=pl.ANY)
    vmem = pl.BlockSpec(memory_space=pltpu.VMEM)
    dma = pltpu.SemaphoreType.DMA
    return pl.pallas_call(
        step_kernel,
        out_shape=(
            pltpu.VMEM((slots, *block), jnp.bfloat16),
            pltpu.VMEM((N_Z, late, share, order), jnp.bfloat16),
            pltpu.VMEM((late, *block), jnp.bfloat16),
            pltpu.VMEM((slots, 128), jnp.float32),
        ),
        in_specs=[vmem] + [anywhere] * 5,
        out_specs=(vmem, vmem, vmem, vmem),
        scratch_shapes=[
            pltpu.VMEM((per_shard + 1, *block), jnp.bfloat16),
            pltpu.VMEM((2, 3, 8, *block), jnp.bfloat16),
            pltpu.VMEM((2, 4, 8, *block), jnp.bfloat16),
            pltpu.VMEM((2, 2, 4, *block), jnp.bfloat16),
            pltpu.VMEM((2, 2, 4, *block), jnp.bfloat16),
            pltpu.VMEM((N_Z, slots, share, order), jnp.bfloat16),
            pltpu.VMEM((slots, *block), jnp.bfloat16),
            pltpu.VMEM((slots, share, order), jnp.float32),
            pltpu.VMEM((slots, share, order), jnp.float32),
            pltpu.VMEM((slots, 8, 128), jnp.float32),
            pltpu.VMEM((slots, 8, 128), jnp.float32),
            pltpu.VMEM((N_Z, 8, 128), jnp.float32),
            pltpu.VMEM((1, 128), jnp.float32),
            pltpu.VMEM((1, 128), jnp.int32),
            pltpu.SMEM((1, 128), jnp.int32),
            dma((7,)),
            dma((RING,)),
            dma((2, 2)),
            dma((late + 1,)),
            dma,
            dma((82,)),
            dma((82,)),
            dma((2, 4, RING)),
            dma((2, 4, RING)),
            dma((N_Z,)),
            dma((N_Z,)),
        ],
        compiler_params=pltpu.CompilerParams(
            collective_id=0, has_side_effects=True, vmem_limit_bytes=LIMIT * 2**20
        ),
        cost_estimate=pl.CostEstimate(
            flops=4 * slots * order**3, bytes_accessed=4 * 10**8, transcendentals=10**6
        ),
    )(owner, grads, left, right, mone, mtwo)


def scale_kernel(x, left, right, scale, out, ready, sems):
    me = lax.axis_index("dp")
    order = x.shape[1]
    last = START[BESIDE_LONG]

    def copy(kind, pos):
        return pltpu.make_async_copy(ready.at[pos], out.at[slot_at(me, kind, pos)], sems.at[pos])

    def row(kind, pos):
        return scale[pl.ds(slot_at(me, kind, pos), 1), :]

    def in_groups(kind, n, some):
        def one(i, carry):
            places = [START[kind] + n * i + j for j in range(n)]
            some(places)
            for pos in places:
                copy(kind, pos).start()
            return carry

        lax.fori_loop(0, (START[kind + 1] - START[kind]) // n, one, 0)

    def store(pos, values, factor):
        ready[pos] = (values * jnp.concatenate([factor, factor], axis=1)).astype(jnp.bfloat16)

    def scale_all(kind):
        def scaled(places):
            for pos in places:
                store(pos, x[pos].astype(jnp.float32), row(kind, pos))

        in_groups(kind, 4, scaled)

    def whole(places):
        halves = [
            jnp.dot(
                left[:, pos - last].reshape(order, order), x[pos], preferred_element_type=jnp.float32
            ).astype(jnp.bfloat16)
            for pos in places
        ]
        preconds = [
            jnp.dot(half, right[pos - last], preferred_element_type=jnp.float32)
            for pos, half in zip(places, halves)
        ]
        for pos, precond in zip(places, preconds):
            mean = jnp.sum(precond * precond, axis=(0, 1), keepdims=True) / float(order * order) + 1e-06
            store(pos, precond, row(BESIDE_LONG, pos) / jnp.sqrt(mean))

    for kind in (NEAR, NEAR_LONG, BESIDE, AWAY_LONG, AWAY):
        scale_all(kind)
    in_groups(BESIDE_LONG, 8, whole)
    scale_all(BESIDE_CROSS)
    for kind in range(BESIDE_LONG + 1):

        def settle(pos, carry):
            copy(kind, pos).wait()
            return carry

        lax.fori_loop(START[kind], START[kind + 1], settle, 0)


def apply_scale(x, left, right, scale):
    vmem, anywhere = pl.BlockSpec(memory_space=pltpu.VMEM), pl.BlockSpec(memory_space=pl.ANY)
    return pl.pallas_call(
        scale_kernel,
        out_shape=jax.ShapeDtypeStruct(x.shape, jnp.bfloat16),
        in_specs=[vmem] * 4,
        out_specs=anywhere,
        scratch_shapes=[
            pltpu.VMEM(x.shape, jnp.bfloat16),
            pltpu.SemaphoreType.DMA((x.shape[0],)),
        ],
        compiler_params=pltpu.CompilerParams(vmem_limit_bytes=24 * 2**20),
    )(x, left, right, scale)


def per_device(grads, owner, left_root, right_root, first_moment, second_moment):
    x, left, right, scale = step(
        owner.reshape(1, -1), grads, left_root[0], right_root[0], first_moment[0], second_moment[0]
    )
    return apply_scale(x, left, right, scale)[None]


def solution(mesh):
    placed = (
        P("dp", None, None),
        P(),
        P("dp", None, "replica", None),
        P("dp", None, None, None),
        P("dp", None, "replica", None),
        P("dp", None, "replica", None),
    )
    return jax.shard_map(
        per_device, mesh=mesh, in_specs=placed, out_specs=P("dp", None, None, None), check_vma=False
    )
```

```python
import functools

import jax
import jax.numpy as jnp
from jax import lax
from jax.experimental import pallas as pl
from jax.experimental.pallas import tpu as pltpu
from jax.sharding import PartitionSpec as P

MESH = pl.DeviceIdType.MESH
N_Y, N_X, N_C = 4, 4, 2
N_DP = N_Y * N_X * N_C
N_Z = 8
RING = 4
SIGNS = (1, -1)
LIMIT = 48

NEAR, NEAR_LONG, BESIDE, AWAY_LONG, AWAY, BESIDE_CROSS, BESIDE_LONG = range(7)
START = (0, 12, 16, 28, 32, 44, 56, 64)
PACKED = ((0, 0), (0, 1), (1, 0), (2, 0), (2, 1), (1, 1), (3, 0), (3, 1))
FULL = (pl.ds(0, 3), pl.ds(5, 3))


LONG = (NEAR_LONG, AWAY_LONG, BESIDE_LONG)


def slot_of_group(me, kind, d, g):
    y, x, c = me // (N_X * N_C), (me // N_C) % N_X, me % N_C
    first, low = (d + 3) % 4 if isinstance(d, int) else lax.rem(d + 3, 4), lax.rem(g, 2)
    if kind in (NEAR, NEAR_LONG):
        half, second, dc = g // 2, 0, low
    elif kind in (AWAY, AWAY_LONG):
        half, second, dc = g // 2, 2, low
    else:
        half, second = lax.rem(g // 2, 2), 3 - 2 * low
        dc = g // 4 if kind == BESIDE_LONG else int(kind == BESIDE_CROSS)
    dy, dx = second + half * (first - second), first + half * (second - first)
    source = lax.rem(y + dy, N_Y) * (N_X * N_C) + lax.rem(x + dx, N_X) * N_C + lax.rem(c + dc, N_C)
    return 2 * source + half


def slot_at(me, kind, pos):
    q = pos - START[kind]
    return slot_of_group(me, kind, 3, q) if kind in LONG else slot_of_group(me, kind, lax.rem(q, 3), q // 3)


def step_kernel(
    owner, grads_hbm, left_hbm, right_hbm, mone_hbm, mtwo_hbm, recv_v, left_late, right_late, scale_out,
    grads_v, out_v, stage_v, pass_v, relay_v, left_v, right_v, mone_v, mtwo_v,
    adam_v, square_v, tiles_v, strip_v, live_v, idx_v, idx,
    load_sems, left_sems, own_sems, late_sems, idx_sem, send_sems, recv_sems, ring_send, ring_recv, zsend, zrecv,
):
    me, z = lax.axis_index("dp"), lax.axis_index("replica")
    per_shard, order = grads_hbm.shape[0], grads_hbm.shape[1]
    slots, share = mone_hbm.shape[0], mone_hbm.shape[1]
    total = float(order * order)
    per_ring = slots // RING
    y, x, c = me // (N_X * N_C), (me // N_C) % N_X, me % N_C

    def at(dy, dx, dc):
        return (
            lax.rem(y + dy + N_Y, N_Y) * (N_X * N_C) + lax.rem(x + dx + N_X, N_X) * N_C + lax.rem(c + dc, N_C)
        )

    def along(half, first, second, dc):
        return at(second + half * (first - second), first + half * (second - first), dc)

    def slot_of(kind, pos):
        return slot_at(me, kind, pos)

    quarter = per_shard // 4
    grad_loads = [
        pltpu.make_async_copy(grads_hbm.at[some], grads_v.at[some], load_sems.at[i])
        for i, some in enumerate(pl.ds(quarter * i, quarter) for i in range(4))
    ]
    loads = [
        pltpu.make_async_copy(mone_hbm, mone_v, load_sems.at[4]),
        pltpu.make_async_copy(mtwo_hbm, mtwo_v, load_sems.at[5]),
        pltpu.make_async_copy(right_hbm, right_v, load_sems.at[6]),
    ]
    for load in grad_loads:
        load.start()

    barrier = pltpu.get_barrier_semaphore()
    near = [(0, 0, 1)] + [(dy, dx, dc) for dy, dx in ((0, 1), (0, -1), (1, 0), (-1, 0)) for dc in range(N_C)]
    for step in near:
        pl.semaphore_signal(barrier, inc=1, device_id=(at(*step), z), device_id_type=MESH)
    for dz in range(1, N_Z):
        pl.semaphore_signal(barrier, inc=1, device_id=(me, lax.rem(z + dz, N_Z)), device_id_type=MESH)

    row = lax.broadcasted_iota(jnp.int32, (per_shard, 128), 0)
    lane = lax.broadcasted_iota(jnp.int32, (per_shard, 128), 1)
    per_line = 128 // per_shard
    line = owner[:, pl.ds(pl.multiple_of(me // per_line * 128, 128), 128)]
    mine = pltpu.roll(
        jnp.broadcast_to(line, (per_shard, 128)), lax.rem(128 - lax.rem(me, per_line) * per_shard, 128), 1
    )
    names = jnp.sum(jnp.where(row == lane, mine, 0), axis=1, keepdims=True)
    ranks = jnp.sum(jnp.where((names == mine) & (lane < row), 1, 0), axis=1, keepdims=True)
    found = jnp.where(2 * names + ranks == lane, row - per_shard, 0)
    idx_v[...] = per_shard + jnp.sum(found, axis=0, keepdims=True)
    to_scalars = pltpu.make_async_copy(idx_v, idx, idx_sem)
    to_scalars.start()
    for kind in range(7):

        def load_left(pos, carry):
            pltpu.make_async_copy(
                left_hbm.at[slot_of(kind, pos)], left_v.at[z, pos], left_sems.at[pos // per_ring]
            ).start()
            return carry

        lax.fori_loop(START[kind], START[kind + 1], load_left, 0)
    grads_v[per_shard] = jnp.zeros((order, order), jnp.bfloat16)
    pl.semaphore_wait(barrier, len(near) + N_Z - 1)

    def pack(half, first, places, into):
        for i in places:
            p = along(half, first, *PACKED[i])
            into[i] = grads_v[idx[0, 2 * p + half]]

    count = [0]

    def message(src, dst, target, plane=z):
        n = count[0]
        count[0] += 1
        return pltpu.make_async_remote_copy(
            src_ref=src, dst_ref=dst, send_sem=send_sems.at[n], recv_sem=recv_sems.at[n],
            device_id=(target, plane), device_id_type=MESH,
        )

    def place(kind, g):
        n = 1 if kind in (NEAR_LONG, AWAY_LONG, BESIDE_LONG) else 3
        return recv_v.at[pl.ds(START[kind] + n * g, n)]

    parity = lax.rem(z, 2)
    half_rows = pl.ds(pl.multiple_of(parity * (order // 2), order // 2), order // 2)
    other_rows = pl.ds(pl.multiple_of((1 - parity) * (order // 2), order // 2), order // 2)
    pieces = (pl.ds(0, 3), pl.ds(3, 1))
    via, straight, onward = {}, {}, {}
    far, ahead, inside, passed, own, swap, swapped, strip = {}, {}, {}, {}, {}, {}, {}, {}
    rows = pl.ds(pl.multiple_of(z * share, share), share)
    for h in range(2):
        for part, sign in enumerate(SIGNS):
            there = along(h, sign, 0, 0)
            for b, some in enumerate((*FULL, pl.ds(3, 2))):
                straight[h, b, part] = message(out_v.at[h, part, some], stage_v.at[h, 2 * part, some], there)
            via[h, 0, part] = message(out_v.at[h, 2, FULL[part]], pass_v.at[h, part, pl.ds(0, 3)], there)
            onward[h, 0, part] = message(pass_v.at[h, part, pl.ds(0, 3)], stage_v.at[h, 3, FULL[part]], there)
            via[h, 1, part] = message(
                out_v.at[h, 2, 3 + part, half_rows], pass_v.at[h, part, 3, half_rows], there
            )
            onward[h, 1, part] = message(
                pass_v.at[h, part, 3, half_rows], stage_v.at[h, 3, 3 + part, half_rows], there
            )
            there = along(h, 0, sign, 0)
            last = along(h, 0, sign, part)
            far[h, 0, part] = message(
                stage_v.at[h, pieces[0], 3 + part], relay_v.at[h, part, pieces[0]], there
            )
            passed[h, 0, part] = message(relay_v.at[h, part, pieces[0]], place(AWAY, h * 2 + part), last)
            far[h, 1, part] = message(
                stage_v.at[h, 3, 3 + part, half_rows], relay_v.at[h, part, 3, half_rows], there
            )
            passed[h, 1, part] = message(
                relay_v.at[h, part, 3, half_rows], recv_v.at[START[AWAY_LONG] + h * 2 + part, half_rows], last
            )
            for dc in range(N_C):
                strip[h, part, dc] = message(
                    stage_v.at[h, 3, PACKED.index((sign % 4, dc)), rows],
                    strip_v.at[dc * 4 + h * 2 + part],
                    along(h, 0, sign, dc),
                )
            for m, piece in enumerate(pieces):
                for dc in range(N_C):
                    ahead[h, m, part, dc] = message(
                        stage_v.at[h, piece, PACKED.index((sign % 4, dc))],
                        place((BESIDE, BESIDE_CROSS)[dc], h * 2 + part) if m == 0 else place(BESIDE_LONG, dc * 4 + h * 2 + part),
                        along(h, 0, sign, dc),
                    )
        for m, piece in enumerate(pieces):
            inside[h, m] = message(stage_v.at[h, piece, 1], place((NEAR, NEAR_LONG)[m], h * 2 + 1), at(0, 0, 1))
            own[h, m] = pltpu.make_async_copy(stage_v.at[h, piece, 0], place((NEAR, NEAR_LONG)[m], h * 2), own_sems.at[h, m])
        step = (1 - 2 * parity) * (1 - 2 * h)
        plane = lax.rem(z + step + N_Z, N_Z)
        both = pl.ds(START[AWAY_LONG] + h * 2, 2)
        swap[h] = message(recv_v.at[both, half_rows], recv_v.at[both, half_rows], me, plane)
        swapped[h] = pltpu.make_async_remote_copy(
            src_ref=recv_v.at[both, other_rows], dst_ref=recv_v.at[both, other_rows],
            send_sem=send_sems.at[count[0] - 1], recv_sem=recv_sems.at[count[0] - 1],
            device_id=(me, plane), device_id_type=MESH,
        )

    def ring(part, t, chunk, source):
        piece = left_v.at[source, pl.ds(chunk * per_ring, per_ring)]
        return pltpu.make_async_remote_copy(
            src_ref=piece, dst_ref=piece,
            send_sem=ring_send.at[part, t, chunk], recv_sem=ring_recv.at[part, t, chunk],
            device_id=(me, lax.rem(z + SIGNS[part] + N_Z, N_Z)), device_id_type=MESH,
        )

    def ring_out(part, t, chunk):
        return ring(part, t, chunk, lax.rem(z - SIGNS[part] * t + N_Z, N_Z))

    def ring_in(part, t, chunk):
        return ring(part, t, chunk, lax.rem(z - SIGNS[part] * (t + 1) + N_Z, N_Z))

    def travels(part, t, chunk):
        return t < 3 or chunk % 2 == part

    def pass_on(t, *chunks):
        for chunk in chunks:
            for part in range(2):
                if travels(part, t, chunk):
                    ring_in(part, t, chunk).wait_recv()
                if t < 3 and travels(part, t + 1, chunk):
                    ring_out(part, t + 1, chunk).start()

    def begin(chunk):
        for part in range(2):
            ring_out(part, 0, chunk).start()

    def fold(values):
        values = values[:, :128] + values[:, 128:]
        return jnp.sum(values.reshape(values.shape[0] // 8, 8, 128), axis=0)

    def in_fours(kind, some):
        def one(i, carry):
            places = [START[kind] + 4 * i + j for j in range(4)]
            some(places, [slot_of(kind, pos) for pos in places])
            return carry

        lax.fori_loop(0, (START[kind + 1] - START[kind]) // 4, one, 0)

    def square_ratio(grad, k):
        grad32 = grad.astype(jnp.float32)
        moment_one = 0.9 * mone_v[k] + 0.1 * grad32
        moment_two = 0.999 * mtwo_v[k] + 0.001 * grad32 * grad32
        ratio = moment_one / (jnp.sqrt(moment_two) + 1e-08)
        adam_v[k] = fold(ratio * ratio)

    def absorb(kind, adam=True, product=True):
        def some(places, ks):
            for pos, k in zip(places, ks) if adam else ():
                square_ratio(recv_v[pos, rows, :], k)
            for pos, k in zip(places, ks) if product else ():
                right = jnp.dot(recv_v[pos], right_v[k], preferred_element_type=jnp.float32)
                recv_v[pos] = right.astype(jnp.bfloat16)

        in_fours(kind, some)

    def adam_of_strips():
        def some(places, ks):
            for pos, k in zip(places, ks):
                square_ratio(strip_v[pos - START[BESIDE_LONG]], k)
                square_v[k] = jnp.zeros((8, 128), jnp.float32)

        in_fours(BESIDE_LONG, some)

    def finish(kind):
        def some(places, ks):
            for pos, k in zip(places, ks):
                precond = jnp.dot(
                    left_v[:, pos].reshape(order, order), recv_v[pos], preferred_element_type=jnp.float32
                )
                square_v[k] = fold(precond * precond)
                recv_v[pos] = precond.astype(jnp.bfloat16)

        in_fours(kind, some)

    def count_live():
        shard = lax.broadcasted_iota(jnp.int32, (owner.shape[1], 128), 0) // per_shard
        slot = lax.broadcasted_iota(jnp.int32, (owner.shape[1], 128), 1)
        ours = jnp.broadcast_to(jnp.where(owner[...] == me, 1.0, 0.0), (8, owner.shape[1]))
        counts = jnp.dot(
            ours.astype(jnp.bfloat16),
            jnp.where(shard == slot // 2, 1.0, 0.0).astype(jnp.bfloat16),
            preferred_element_type=jnp.float32,
        )[:1]
        rank = lax.rem(slot[:1], 2).astype(jnp.float32)
        live_v[...] = jnp.where(counts > rank, 1.0, 0.0)

    def by_lane(sums):
        by_slot = jnp.sum(jnp.sum(sums, axis=1), axis=1, keepdims=True)
        spread = jnp.broadcast_to(by_slot, (slots, 128))
        return jnp.sum(jnp.where(diagonal, spread, 0.0), axis=0, keepdims=True)

    diagonal = lax.broadcasted_iota(jnp.int32, (slots, 128), 0) == lax.broadcasted_iota(
        jnp.int32, (slots, 128), 1
    )

    every = [(h, part) for h in range(2) for part in range(2)]
    thirds = ((0, 1, 2), (5, 6, 7), (3, 4))

    def ready(chunk):
        first = pl.ds(chunk * per_ring, per_ring)
        pltpu.make_async_copy(left_hbm.at[first], left_v.at[z, first], left_sems.at[chunk]).wait()
        begin(chunk)

    for chunk in range(RING):
        ready(chunk)
    to_scalars.wait()
    for load in grad_loads:
        load.wait()
    for load in loads:
        load.start()
    for h, part in every:
        pack(h, 2, (3 + part,), out_v.at[h, 2])
        via[h, 1, part].start()
    for h, part in every:
        pack(h, 2, thirds[part], out_v.at[h, 2])
        via[h, 0, part].start()
    for h, part in every:
        pack(h, SIGNS[part], thirds[2], out_v.at[h, part])
        straight[h, 2, part].start()
    for h, part in every:
        via[h, 1, part].wait_recv()
        onward[h, 1, part].start()
    for b in range(2):
        for h, part in every:
            pack(h, SIGNS[part], thirds[b], out_v.at[h, part])
            straight[h, b, part].start()
    for h in range(2):
        pack(h, 0, range(8), stage_v.at[h, 1])
    count_live()

    pass_on(0, 0)
    for h, part in every:
        via[h, 0, part].wait_recv()
        onward[h, 0, part].start()
    pass_on(0, 1)
    for h, part in every:
        onward[h, 1, part].wait_recv()
        far[h, 1, part].start()
    for h, part in every:
        straight[h, 2, part].wait_recv()
    for h, part in every:
        far[h, 0, part].start()
    pass_on(0, 2, 3)
    pass_on(1, 0)
    for h, part in every:
        for b in range(2):
            straight[h, b, part].wait_recv()
    for h, part in every:
        ahead[h, 0, part, 0].start()
    for h in range(2):
        inside[h, 0].start()
        own[h, 0].start()
    pass_on(1, 1, 2)
    for h, part in every:
        onward[h, 0, part].wait_recv()
    for dc in range(N_C):
        for h, part in every:
            strip[h, part, dc].start()
    for h in range(2):
        inside[h, 1].start()
        own[h, 1].start()
    for h, part in every:
        far[h, 1, part].wait_recv()
        passed[h, 1, part].start()
    for load in loads:
        load.wait()
    first_late = START[BESIDE_LONG]
    to_late = [
        pltpu.make_async_copy(right_v.at[slot_of(BESIDE_LONG, first_late + i)], right_late.at[i], late_sems.at[i])
        for i in range(slots - first_late)
    ]
    for copy in to_late:
        copy.start()
    for m in range(2):
        for h in range(2):
            own[h, m].wait()
            inside[h, m].wait_recv()
    absorb(NEAR)
    absorb(NEAR_LONG)
    pass_on(1, 3)
    for h, part in every:
        far[h, 0, part].wait_recv()
        passed[h, 0, part].start()
    for h, part in every:
        ahead[h, 0, part, 1].start()
    for dc in range(N_C):
        for h, part in every:
            ahead[h, 1, part, dc].start()
    pass_on(2, 0, 1)
    for h, part in every:
        ahead[h, 0, part, 0].wait_recv()
    for h in range(2):
        for part in range(2):
            passed[h, 1, part].wait_recv()
        swap[h].start()
    absorb(BESIDE)
    pass_on(2, 2, 3)
    done = [copy for group in (via, straight, onward, far, inside, strip) for copy in group.values()]
    done += [passed[h, 1, part] for h, part in every] + [ahead[h, 0, part, 0] for h, part in every]
    done += [ring_out(part, t, chunk) for t in range(2) for chunk in range(RING) for part in range(2)]
    for copy in done:
        copy.wait_send()
    for h, part in every:
        passed[h, 0, part].wait_recv()
    for dc in range(N_C):
        for h, part in every:
            strip[h, part, dc].wait_recv()
    adam_of_strips()
    absorb(AWAY)
    pass_on(3, 0, 1)
    for kind in (NEAR, NEAR_LONG, BESIDE):
        finish(kind)
    for h in range(2):
        swapped[h].wait_recv()
        swap[h].wait_send()
    absorb(AWAY_LONG)
    finish(AWAY_LONG)
    for h, part in every:
        ahead[h, 0, part, 1].wait_recv()
    absorb(BESIDE_CROSS, product=False)
    tiles_v[0] = jnp.broadcast_to(by_lane(adam_v[...]), (8, 128))

    def tell(dz):
        return pltpu.make_async_remote_copy(
            src_ref=tiles_v.at[0],
            dst_ref=tiles_v.at[dz],
            send_sem=zsend.at[dz],
            recv_sem=zrecv.at[dz],
            device_id=(me, lax.rem(z + dz, N_Z)),
            device_id_type=MESH,
        )

    for dz in range(1, N_Z):
        tell(dz).start()
    for chunk in range(RING):
        for part in range(2):
            ring_out(part, 2, chunk).wait_send()
    absorb(BESIDE_CROSS, adam=False)
    pass_on(3, 2)
    finish(AWAY)
    pass_on(3, 3)
    to_late.append(
        pltpu.make_async_copy(
            left_v.at[:, pl.ds(first_late, slots - first_late)], left_late, late_sems.at[slots - first_late]
        )
    )
    to_late[-1].start()
    finish(BESIDE_CROSS)
    sum_pre = by_lane(square_v[...])
    for dz in range(1, N_Z):
        tell(dz).wait()
    sum_adam = jnp.sum(tiles_v[...], axis=0)[:1]
    lane = lax.broadcasted_iota(jnp.int32, (1, 128), 1)
    dy = lax.rem(lane // (2 * N_X * N_C) - y + 2 * N_Y, N_Y)
    dx = lax.rem(lax.rem(lane // (2 * N_C), N_X) - x + N_X, N_X)
    odd = lax.rem(lane, 2) == 1
    later = (jnp.where(odd, dy, dx) == 2) & (lax.rem(jnp.where(odd, dx, dy), 2) == 1)
    norm = live_v[...] * jnp.sqrt(sum_adam / total)
    scale = jnp.where(later, norm, norm / jnp.sqrt(sum_pre / total + 1e-06))
    by_row = jnp.where(diagonal, jnp.broadcast_to(scale, (slots, 128)), 0.0)
    scale_out[...] = jnp.broadcast_to(jnp.sum(by_row, axis=1, keepdims=True), (slots, 128))
    for copy in to_late:
        copy.wait()
    for dc in range(N_C):
        for h, part in every:
            ahead[h, 1, part, dc].wait_recv()
    done = [passed[h, 0, part] for h, part in every] + [ahead[h, 0, part, 1] for h, part in every]
    done += [ahead[h, 1, part, dc] for dc in range(N_C) for h, part in every]
    done += [ring_out(part, 3, chunk) for chunk in range(RING) for part in range(2) if travels(part, 3, chunk)]
    for copy in done:
        copy.wait_send()


def step(owner, grads, left, right, mone, mtwo):
    per_shard, order, _ = grads.shape
    slots, share, _ = mone.shape
    block = (order, order)
    late = slots - START[BESIDE_LONG]
    anywhere = pl.BlockSpec(memory_space=pl.ANY)
    vmem = pl.BlockSpec(memory_space=pltpu.VMEM)
    dma = pltpu.SemaphoreType.DMA
    return pl.pallas_call(
        step_kernel,
        out_shape=(
            pltpu.VMEM((slots, *block), jnp.bfloat16),
            pltpu.VMEM((N_Z, late, share, order), jnp.bfloat16),
            pltpu.VMEM((late, *block), jnp.bfloat16),
            pltpu.VMEM((slots, 128), jnp.float32),
        ),
        in_specs=[vmem] + [anywhere] * 5,
        out_specs=(vmem, vmem, vmem, vmem),
        scratch_shapes=[
            pltpu.VMEM((per_shard + 1, *block), jnp.bfloat16),
            pltpu.VMEM((2, 3, 8, *block), jnp.bfloat16),
            pltpu.VMEM((2, 4, 8, *block), jnp.bfloat16),
            pltpu.VMEM((2, 2, 4, *block), jnp.bfloat16),
            pltpu.VMEM((2, 2, 4, *block), jnp.bfloat16),
            pltpu.VMEM((N_Z, slots, share, order), jnp.bfloat16),
            pltpu.VMEM((slots, *block), jnp.bfloat16),
            pltpu.VMEM((slots, share, order), jnp.float32),
            pltpu.VMEM((slots, share, order), jnp.float32),
            pltpu.VMEM((slots, 8, 128), jnp.float32),
            pltpu.VMEM((slots, 8, 128), jnp.float32),
            pltpu.VMEM((N_Z, 8, 128), jnp.float32),
            pltpu.VMEM((8, share, order), jnp.bfloat16),
            pltpu.VMEM((1, 128), jnp.float32),
            pltpu.VMEM((1, 128), jnp.int32),
            pltpu.SMEM((1, 128), jnp.int32),
            dma((7,)),
            dma((RING,)),
            dma((2, 2)),
            dma((late + 1,)),
            dma,
            dma((74,)),
            dma((74,)),
            dma((2, 4, RING)),
            dma((2, 4, RING)),
            dma((N_Z,)),
            dma((N_Z,)),
        ],
        compiler_params=pltpu.CompilerParams(
            collective_id=0, has_side_effects=True, vmem_limit_bytes=LIMIT * 2**20
        ),
        cost_estimate=pl.CostEstimate(
            flops=4 * slots * order**3, bytes_accessed=4 * 10**8, transcendentals=10**6
        ),
    )(owner, grads, left, right, mone, mtwo)


def scale_kernel(x, left, right, scale, out, ready, sem):
    me = lax.axis_index("dp")
    order = x.shape[1]
    last = START[BESIDE_LONG]

    def in_groups(kind, some):
        def one(i, carry):
            if kind in LONG:
                places = [START[kind] + j for j in range(START[kind + 1] - START[kind])]
                ks = [slot_of_group(me, kind, 3, j) for j in range(len(places))]
            else:
                places = [START[kind] + 6 * i + j for j in range(6)]
                ks = [slot_of_group(me, kind, j % 3, 2 * i + j // 3) for j in range(6)]
            some(places, [scale[pl.ds(k, 1), :] for k in ks])
            for pos, k in zip(places, ks):
                pltpu.make_async_copy(ready.at[pos], out.at[k], sem).start()
            return carry

        if kind in LONG:
            one(0, 0)
        else:
            lax.fori_loop(0, 2, one, 0)

    def store(pos, values, factor):
        ready[pos] = (values * jnp.concatenate([factor, factor], axis=1)).astype(jnp.bfloat16)

    def scaled(places, factors):
        for pos, factor in zip(places, factors):
            store(pos, x[pos].astype(jnp.float32), factor)

    def whole(places, factors):
        halves = [
            jnp.dot(
                left[:, pos - last].reshape(order, order), x[pos], preferred_element_type=jnp.float32
            ).astype(jnp.bfloat16)
            for pos in places
        ]
        preconds = [
            jnp.dot(half, right[pos - last], preferred_element_type=jnp.float32)
            for pos, half in zip(places, halves)
        ]
        for pos, precond, factor in zip(places, preconds, factors):
            mean = jnp.sum(precond * precond, axis=(0, 1), keepdims=True) / float(order * order) + 1e-06
            store(pos, precond, factor / jnp.sqrt(mean))

    for kind in (NEAR, NEAR_LONG, BESIDE, AWAY_LONG, AWAY):
        in_groups(kind, scaled)
    in_groups(BESIDE_LONG, whole)
    in_groups(BESIDE_CROSS, scaled)
    pltpu.make_async_copy(ready, out, sem).wait()


def apply_scale(x, left, right, scale):
    vmem, anywhere = pl.BlockSpec(memory_space=pltpu.VMEM), pl.BlockSpec(memory_space=pl.ANY)
    return pl.pallas_call(
        scale_kernel,
        out_shape=jax.ShapeDtypeStruct(x.shape, jnp.bfloat16),
        in_specs=[vmem] * 4,
        out_specs=anywhere,
        scratch_shapes=[
            pltpu.VMEM(x.shape, jnp.bfloat16),
            pltpu.SemaphoreType.DMA,
        ],
        compiler_params=pltpu.CompilerParams(vmem_limit_bytes=24 * 2**20),
    )(x, left, right, scale)


def per_device(grads, owner, left_root, right_root, first_moment, second_moment):
    x, left, right, scale = step(
        owner.reshape(1, -1), grads, left_root[0], right_root[0], first_moment[0], second_moment[0]
    )
    return apply_scale(x, left, right, scale)[None]


def solution(mesh):
    placed = (
        P("dp", None, None),
        P(),
        P("dp", None, "replica", None),
        P("dp", None, None, None),
        P("dp", None, "replica", None),
        P("dp", None, "replica", None),
    )
    return jax.shard_map(
        per_device, mesh=mesh, in_specs=placed, out_specs=P("dp", None, None, None), check_vma=False
    )
```

```python
import functools

import jax
import jax.numpy as jnp
from jax import lax
from jax.experimental import pallas as pl
from jax.experimental.pallas import tpu as pltpu
from jax.sharding import PartitionSpec as P

MESH = pl.DeviceIdType.MESH
N_Y, N_X, N_C = 4, 4, 2
N_DP = N_Y * N_X * N_C
N_Z = 8
RING = 4
SIGNS = (1, -1)
LIMIT = 48

NEAR, NEAR_LONG, BESIDE, AWAY_LONG, AWAY, BESIDE_CROSS, BESIDE_LONG = range(7)
START = (0, 12, 16, 28, 32, 44, 56, 64)
PACKED = ((0, 0), (0, 1), (1, 0), (2, 0), (2, 1), (1, 1), (3, 0), (3, 1))
FULL = (pl.ds(0, 3), pl.ds(5, 3))


LONG = (NEAR_LONG, AWAY_LONG, BESIDE_LONG)


def slot_of_group(me, kind, d, g):
    y, x, c = me // (N_X * N_C), (me // N_C) % N_X, me % N_C
    first, low = (d + 3) % 4 if isinstance(d, int) else lax.rem(d + 3, 4), lax.rem(g, 2)
    if kind in (NEAR, NEAR_LONG):
        half, second, dc = g // 2, 0, low
    elif kind in (AWAY, AWAY_LONG):
        half, second, dc = g // 2, 2, low
    else:
        half, second = lax.rem(g // 2, 2), 3 - 2 * low
        dc = g // 4 if kind == BESIDE_LONG else int(kind == BESIDE_CROSS)
    dy, dx = second + half * (first - second), first + half * (second - first)
    source = lax.rem(y + dy, N_Y) * (N_X * N_C) + lax.rem(x + dx, N_X) * N_C + lax.rem(c + dc, N_C)
    return 2 * source + half


def slot_at(me, kind, pos):
    q = pos - START[kind]
    return slot_of_group(me, kind, 3, q) if kind in LONG else slot_of_group(me, kind, lax.rem(q, 3), q // 3)


def step_kernel(
    owner, grads_hbm, left_hbm, right_hbm, mone_hbm, mtwo_hbm, recv_v, left_late, right_late, scale_out,
    grads_v, out_v, stage_v, pass_v, relay_v, left_v, right_v, mone_v, mtwo_v,
    adam_v, square_v, tiles_v, strip_v, live_v, idx_v, idx,
    load_sems, left_sems, own_sems, late_sems, idx_sem, send_sems, recv_sems, ring_send, ring_recv, zsend, zrecv,
):
    me, z = lax.axis_index("dp"), lax.axis_index("replica")
    per_shard, order = grads_hbm.shape[0], grads_hbm.shape[1]
    slots, share = mone_hbm.shape[0], mone_hbm.shape[1]
    total = float(order * order)
    per_ring = slots // RING
    y, x, c = me // (N_X * N_C), (me // N_C) % N_X, me % N_C

    def at(dy, dx, dc):
        return (
            lax.rem(y + dy + N_Y, N_Y) * (N_X * N_C) + lax.rem(x + dx + N_X, N_X) * N_C + lax.rem(c + dc, N_C)
        )

    def along(half, first, second, dc):
        return at(second + half * (first - second), first + half * (second - first), dc)

    def slot_of(kind, pos):
        return slot_at(me, kind, pos)

    quarter = per_shard // 4
    grad_loads = [
        pltpu.make_async_copy(grads_hbm.at[some], grads_v.at[some], load_sems.at[i])
        for i, some in enumerate(pl.ds(quarter * i, quarter) for i in range(4))
    ]
    loads = [
        pltpu.make_async_copy(mone_hbm, mone_v, load_sems.at[4]),
        pltpu.make_async_copy(mtwo_hbm, mtwo_v, load_sems.at[5]),
        pltpu.make_async_copy(right_hbm, right_v, load_sems.at[6]),
    ]
    for load in grad_loads:
        load.start()

    barrier = pltpu.get_barrier_semaphore()
    near = [(0, 0, 1)] + [(dy, dx, dc) for dy, dx in ((0, 1), (0, -1), (1, 0), (-1, 0)) for dc in range(N_C)]
    for step in near:
        pl.semaphore_signal(barrier, inc=1, device_id=(at(*step), z), device_id_type=MESH)
    for dz in range(1, N_Z):
        pl.semaphore_signal(barrier, inc=1, device_id=(me, lax.rem(z + dz, N_Z)), device_id_type=MESH)

    row = lax.broadcasted_iota(jnp.int32, (per_shard, 128), 0)
    lane = lax.broadcasted_iota(jnp.int32, (per_shard, 128), 1)
    per_line = 128 // per_shard
    line = owner[:, pl.ds(pl.multiple_of(me // per_line * 128, 128), 128)]
    mine = pltpu.roll(
        jnp.broadcast_to(line, (per_shard, 128)), lax.rem(128 - lax.rem(me, per_line) * per_shard, 128), 1
    )
    names = jnp.sum(jnp.where(row == lane, mine, 0), axis=1, keepdims=True)
    ranks = jnp.sum(jnp.where((names == mine) & (lane < row), 1, 0), axis=1, keepdims=True)
    found = jnp.where(2 * names + ranks == lane, row - per_shard, 0)
    idx_v[...] = per_shard + jnp.sum(found, axis=0, keepdims=True)
    to_scalars = pltpu.make_async_copy(idx_v, idx, idx_sem)
    to_scalars.start()
    for kind in range(7):

        def load_left(pos, carry):
            pltpu.make_async_copy(
                left_hbm.at[slot_of(kind, pos)], left_v.at[z, pos], left_sems.at[pos // per_ring]
            ).start()
            return carry

        lax.fori_loop(START[kind], START[kind + 1], load_left, 0)
    grads_v[per_shard] = jnp.zeros((order, order), jnp.bfloat16)
    pl.semaphore_wait(barrier, len(near) + N_Z - 1)

    def pack(half, first, places, into):
        for i in places:
            p = along(half, first, *PACKED[i])
            into[i] = grads_v[idx[0, 2 * p + half]]

    count = [0]

    def message(src, dst, target, plane=z):
        n = count[0]
        count[0] += 1
        return pltpu.make_async_remote_copy(
            src_ref=src, dst_ref=dst, send_sem=send_sems.at[n], recv_sem=recv_sems.at[n],
            device_id=(target, plane), device_id_type=MESH,
        )

    def place(kind, g):
        n = 1 if kind in (NEAR_LONG, AWAY_LONG, BESIDE_LONG) else 3
        return recv_v.at[pl.ds(START[kind] + n * g, n)]

    parity = lax.rem(z, 2)
    half_rows = pl.ds(pl.multiple_of(parity * (order // 2), order // 2), order // 2)
    other_rows = pl.ds(pl.multiple_of((1 - parity) * (order // 2), order // 2), order // 2)
    pieces = (pl.ds(0, 3), pl.ds(3, 1))
    via, straight, onward = {}, {}, {}
    far, ahead, inside, passed, own, swap, swapped, strip = {}, {}, {}, {}, {}, {}, {}, {}
    rows = pl.ds(pl.multiple_of(z * share, share), share)
    for h in range(2):
        for part, sign in enumerate(SIGNS):
            there = along(h, sign, 0, 0)
            for b, some in enumerate((*FULL, pl.ds(3, 2))):
                straight[h, b, part] = message(out_v.at[h, part, some], stage_v.at[h, 2 * part, some], there)
            via[h, 0, part] = message(out_v.at[h, 2, FULL[part]], pass_v.at[h, part, pl.ds(0, 3)], there)
            onward[h, 0, part] = message(pass_v.at[h, part, pl.ds(0, 3)], stage_v.at[h, 3, FULL[part]], there)
            via[h, 1, part] = message(
                out_v.at[h, 2, 3 + part, half_rows], pass_v.at[h, part, 3, half_rows], there
            )
            onward[h, 1, part] = message(
                pass_v.at[h, part, 3, half_rows], stage_v.at[h, 3, 3 + part, half_rows], there
            )
            there = along(h, 0, sign, 0)
            last = along(h, 0, sign, part)
            far[h, 0, part] = message(
                stage_v.at[h, pieces[0], 3 + part], relay_v.at[h, part, pieces[0]], there
            )
            passed[h, 0, part] = message(relay_v.at[h, part, pieces[0]], place(AWAY, h * 2 + part), last)
            far[h, 1, part] = message(
                stage_v.at[h, 3, 3 + part, half_rows], relay_v.at[h, part, 3, half_rows], there
            )
            passed[h, 1, part] = message(
                relay_v.at[h, part, 3, half_rows], recv_v.at[START[AWAY_LONG] + h * 2 + part, half_rows], last
            )
            for dc in range(N_C):
                strip[h, part, dc] = message(
                    stage_v.at[h, 3, PACKED.index((sign % 4, dc)), rows],
                    strip_v.at[dc * 4 + h * 2 + part],
                    along(h, 0, sign, dc),
                )
            for m, piece in enumerate(pieces):
                for dc in range(N_C):
                    ahead[h, m, part, dc] = message(
                        stage_v.at[h, piece, PACKED.index((sign % 4, dc))],
                        place((BESIDE, BESIDE_CROSS)[dc], h * 2 + part) if m == 0 else place(BESIDE_LONG, dc * 4 + h * 2 + part),
                        along(h, 0, sign, dc),
                    )
        for m, piece in enumerate(pieces):
            inside[h, m] = message(stage_v.at[h, piece, 1], place((NEAR, NEAR_LONG)[m], h * 2 + 1), at(0, 0, 1))
            own[h, m] = pltpu.make_async_copy(stage_v.at[h, piece, 0], place((NEAR, NEAR_LONG)[m], h * 2), own_sems.at[h, m])
        step = (1 - 2 * parity) * (1 - 2 * h)
        plane = lax.rem(z + step + N_Z, N_Z)
        both = pl.ds(START[AWAY_LONG] + h * 2, 2)
        swap[h] = message(recv_v.at[both, half_rows], recv_v.at[both, half_rows], me, plane)
        swapped[h] = pltpu.make_async_remote_copy(
            src_ref=recv_v.at[both, other_rows], dst_ref=recv_v.at[both, other_rows],
            send_sem=send_sems.at[count[0] - 1], recv_sem=recv_sems.at[count[0] - 1],
            device_id=(me, plane), device_id_type=MESH,
        )

    def ring(part, t, chunk, source):
        piece = left_v.at[source, pl.ds(chunk * per_ring, per_ring)]
        return pltpu.make_async_remote_copy(
            src_ref=piece, dst_ref=piece,
            send_sem=ring_send.at[part, t, chunk], recv_sem=ring_recv.at[part, t, chunk],
            device_id=(me, lax.rem(z + SIGNS[part] + N_Z, N_Z)), device_id_type=MESH,
        )

    def ring_out(part, t, chunk):
        return ring(part, t, chunk, lax.rem(z - SIGNS[part] * t + N_Z, N_Z))

    def ring_in(part, t, chunk):
        return ring(part, t, chunk, lax.rem(z - SIGNS[part] * (t + 1) + N_Z, N_Z))

    def travels(part, t, chunk):
        return t < 3 or chunk % 2 == part

    def pass_on(t, *chunks):
        for chunk in chunks:
            for part in range(2):
                if travels(part, t, chunk):
                    ring_in(part, t, chunk).wait_recv()
                if t < 3 and travels(part, t + 1, chunk):
                    ring_out(part, t + 1, chunk).start()

    def begin(chunk):
        for part in range(2):
            ring_out(part, 0, chunk).start()

    def fold(values):
        values = values[:, :128] + values[:, 128:]
        return jnp.sum(values.reshape(values.shape[0] // 8, 8, 128), axis=0)

    def in_fours(kind, some):
        def one(i, carry):
            places = [START[kind] + 4 * i + j for j in range(4)]
            some(places, [slot_of(kind, pos) for pos in places])
            return carry

        lax.fori_loop(0, (START[kind + 1] - START[kind]) // 4, one, 0)

    def square_ratio(grad, k):
        grad32 = grad.astype(jnp.float32)
        moment_one = 0.9 * mone_v[k] + 0.1 * grad32
        moment_two = 0.999 * mtwo_v[k] + 0.001 * grad32 * grad32
        ratio = moment_one / (jnp.sqrt(moment_two) + 1e-08)
        adam_v[k] = fold(ratio * ratio)

    def absorb(kind, adam=True, product=True):
        def some(places, ks):
            for pos, k in zip(places, ks) if adam else ():
                square_ratio(recv_v[pos, rows, :], k)
            for pos, k in zip(places, ks) if product else ():
                right = jnp.dot(recv_v[pos], right_v[k], preferred_element_type=jnp.float32)
                recv_v[pos] = right.astype(jnp.bfloat16)

        in_fours(kind, some)

    def adam_of_strips():
        def some(places, ks):
            for pos, k in zip(places, ks):
                square_ratio(strip_v[pos - START[BESIDE_LONG]], k)
                square_v[k] = jnp.zeros((8, 128), jnp.float32)

        in_fours(BESIDE_LONG, some)

    def finish(kind):
        def some(places, ks):
            for pos, k in zip(places, ks):
                precond = jnp.dot(
                    left_v[:, pos].reshape(order, order), recv_v[pos], preferred_element_type=jnp.float32
                )
                square_v[k] = fold(precond * precond)
                recv_v[pos] = precond.astype(jnp.bfloat16)

        in_fours(kind, some)

    def count_live():
        shard = lax.broadcasted_iota(jnp.int32, (owner.shape[1], 128), 0) // per_shard
        slot = lax.broadcasted_iota(jnp.int32, (owner.shape[1], 128), 1)
        ours = jnp.broadcast_to(jnp.where(owner[...] == me, 1.0, 0.0), (8, owner.shape[1]))
        counts = jnp.dot(
            ours.astype(jnp.bfloat16),
            jnp.where(shard == slot // 2, 1.0, 0.0).astype(jnp.bfloat16),
            preferred_element_type=jnp.float32,
        )[:1]
        rank = lax.rem(slot[:1], 2).astype(jnp.float32)
        live_v[...] = jnp.where(counts > rank, 1.0, 0.0)

    def by_lane(sums):
        by_slot = jnp.sum(jnp.sum(sums, axis=1), axis=1, keepdims=True)
        spread = jnp.broadcast_to(by_slot, (slots, 128))
        return jnp.sum(jnp.where(diagonal, spread, 0.0), axis=0, keepdims=True)

    diagonal = lax.broadcasted_iota(jnp.int32, (slots, 128), 0) == lax.broadcasted_iota(
        jnp.int32, (slots, 128), 1
    )

    every = [(h, part) for h in range(2) for part in range(2)]
    thirds = ((0, 1, 2), (5, 6, 7), (3, 4))

    def ready(chunk):
        first = pl.ds(chunk * per_ring, per_ring)
        pltpu.make_async_copy(left_hbm.at[first], left_v.at[z, first], left_sems.at[chunk]).wait()
        begin(chunk)

    for chunk in range(RING):
        ready(chunk)
    to_scalars.wait()
    for load in grad_loads:
        load.wait()
    for load in loads:
        load.start()
    for h, part in every:
        pack(h, 2, (3 + part,), out_v.at[h, 2])
        via[h, 1, part].start()
    for h, part in every:
        pack(h, 2, thirds[part], out_v.at[h, 2])
        via[h, 0, part].start()
    for h, part in every:
        pack(h, SIGNS[part], thirds[2], out_v.at[h, part])
        straight[h, 2, part].start()
    for h, part in every:
        via[h, 1, part].wait_recv()
        onward[h, 1, part].start()
    for b in range(2):
        for h, part in every:
            pack(h, SIGNS[part], thirds[b], out_v.at[h, part])
            straight[h, b, part].start()
    for h in range(2):
        pack(h, 0, range(8), stage_v.at[h, 1])
    count_live()

    pass_on(0, 0)
    for h, part in every:
        via[h, 0, part].wait_recv()
        onward[h, 0, part].start()
    pass_on(0, 1)
    for h, part in every:
        onward[h, 1, part].wait_recv()
        far[h, 1, part].start()
    for h, part in every:
        straight[h, 2, part].wait_recv()
    for h, part in every:
        far[h, 0, part].start()
    pass_on(0, 2, 3)
    pass_on(1, 0)
    for h, part in every:
        for b in range(2):
            straight[h, b, part].wait_recv()
    for h, part in every:
        ahead[h, 0, part, 0].start()
    for h in range(2):
        inside[h, 0].start()
        own[h, 0].start()
    pass_on(1, 1, 2)
    for h, part in every:
        onward[h, 0, part].wait_recv()
    for dc in range(N_C):
        for h, part in every:
            strip[h, part, dc].start()
    for h in range(2):
        inside[h, 1].start()
        own[h, 1].start()
    for h, part in every:
        far[h, 1, part].wait_recv()
        passed[h, 1, part].start()
    for load in loads:
        load.wait()
    first_late = START[BESIDE_LONG]
    to_late = [
        pltpu.make_async_copy(right_v.at[slot_of(BESIDE_LONG, first_late + i)], right_late.at[i], late_sems.at[i])
        for i in range(slots - first_late)
    ]
    for copy in to_late:
        copy.start()
    for m in range(2):
        for h in range(2):
            own[h, m].wait()
            inside[h, m].wait_recv()
    absorb(NEAR)
    absorb(NEAR_LONG)
    pass_on(1, 3)
    for h, part in every:
        far[h, 0, part].wait_recv()
        passed[h, 0, part].start()
    for h, part in every:
        ahead[h, 0, part, 1].start()
    for dc in range(N_C):
        for h, part in every:
            ahead[h, 1, part, dc].start()
    pass_on(2, 0, 1)
    for h, part in every:
        ahead[h, 0, part, 0].wait_recv()
    for h in range(2):
        for part in range(2):
            passed[h, 1, part].wait_recv()
        swap[h].start()
    absorb(BESIDE)
    pass_on(2, 2, 3)
    for h, part in every:
        passed[h, 0, part].wait_recv()
    for dc in range(N_C):
        for h, part in every:
            strip[h, part, dc].wait_recv()
    adam_of_strips()
    absorb(AWAY)
    pass_on(3, 0, 1)
    for kind in (NEAR, NEAR_LONG, BESIDE):
        finish(kind)
    for h in range(2):
        swapped[h].wait_recv()
        swap[h].wait_send()
    absorb(AWAY_LONG)
    finish(AWAY_LONG)
    for h, part in every:
        ahead[h, 0, part, 1].wait_recv()
    absorb(BESIDE_CROSS, product=False)
    tiles_v[0] = jnp.broadcast_to(by_lane(adam_v[...]), (8, 128))

    def tell(dz):
        return pltpu.make_async_remote_copy(
            src_ref=tiles_v.at[0],
            dst_ref=tiles_v.at[dz],
            send_sem=zsend.at[dz],
            recv_sem=zrecv.at[dz],
            device_id=(me, lax.rem(z + dz, N_Z)),
            device_id_type=MESH,
        )

    for dz in range(1, N_Z):
        tell(dz).start()
    absorb(BESIDE_CROSS, adam=False)
    pass_on(3, 2)
    finish(AWAY)
    pass_on(3, 3)
    to_late.append(
        pltpu.make_async_copy(
            left_v.at[:, pl.ds(first_late, slots - first_late)], left_late, late_sems.at[slots - first_late]
        )
    )
    to_late[-1].start()
    finish(BESIDE_CROSS)
    sum_pre = by_lane(square_v[...])
    for dz in range(1, N_Z):
        tell(dz).wait()
    sum_adam = jnp.sum(tiles_v[...], axis=0)[:1]
    lane = lax.broadcasted_iota(jnp.int32, (1, 128), 1)
    dy = lax.rem(lane // (2 * N_X * N_C) - y + 2 * N_Y, N_Y)
    dx = lax.rem(lax.rem(lane // (2 * N_C), N_X) - x + N_X, N_X)
    odd = lax.rem(lane, 2) == 1
    later = (jnp.where(odd, dy, dx) == 2) & (lax.rem(jnp.where(odd, dx, dy), 2) == 1)
    norm = live_v[...] * jnp.sqrt(sum_adam / total)
    scale = jnp.where(later, norm, norm / jnp.sqrt(sum_pre / total + 1e-06))
    by_row = jnp.where(diagonal, jnp.broadcast_to(scale, (slots, 128)), 0.0)
    scale_out[...] = jnp.broadcast_to(jnp.sum(by_row, axis=1, keepdims=True), (slots, 128))
    for copy in to_late:
        copy.wait()
    for dc in range(N_C):
        for h, part in every:
            ahead[h, 1, part, dc].wait_recv()
    for group in (via, straight, onward, far, ahead, inside, passed, strip):
        for copy in group.values():
            copy.wait_send()
    for t in range(4):
        for chunk in range(RING):
            for part in range(2):
                if travels(part, t, chunk):
                    ring_out(part, t, chunk).wait_send()


def step(owner, grads, left, right, mone, mtwo):
    per_shard, order, _ = grads.shape
    slots, share, _ = mone.shape
    block = (order, order)
    late = slots - START[BESIDE_LONG]
    anywhere = pl.BlockSpec(memory_space=pl.ANY)
    vmem = pl.BlockSpec(memory_space=pltpu.VMEM)
    dma = pltpu.SemaphoreType.DMA
    return pl.pallas_call(
        step_kernel,
        out_shape=(
            pltpu.VMEM((slots, *block), jnp.bfloat16),
            pltpu.VMEM((N_Z, late, share, order), jnp.bfloat16),
            pltpu.VMEM((late, *block), jnp.bfloat16),
            pltpu.VMEM((slots, 128), jnp.float32),
        ),
        in_specs=[vmem] + [anywhere] * 5,
        out_specs=(vmem, vmem, vmem, vmem),
        scratch_shapes=[
            pltpu.VMEM((per_shard + 1, *block), jnp.bfloat16),
            pltpu.VMEM((2, 3, 8, *block), jnp.bfloat16),
            pltpu.VMEM((2, 4, 8, *block), jnp.bfloat16),
            pltpu.VMEM((2, 2, 4, *block), jnp.bfloat16),
            pltpu.VMEM((2, 2, 4, *block), jnp.bfloat16),
            pltpu.VMEM((N_Z, slots, share, order), jnp.bfloat16),
            pltpu.VMEM((slots, *block), jnp.bfloat16),
            pltpu.VMEM((slots, share, order), jnp.float32),
            pltpu.VMEM((slots, share, order), jnp.float32),
            pltpu.VMEM((slots, 8, 128), jnp.float32),
            pltpu.VMEM((slots, 8, 128), jnp.float32),
            pltpu.VMEM((N_Z, 8, 128), jnp.float32),
            pltpu.VMEM((8, share, order), jnp.bfloat16),
            pltpu.VMEM((1, 128), jnp.float32),
            pltpu.VMEM((1, 128), jnp.int32),
            pltpu.SMEM((1, 128), jnp.int32),
            dma((7,)),
            dma((RING,)),
            dma((2, 2)),
            dma((late + 1,)),
            dma,
            dma((74,)),
            dma((74,)),
            dma((2, 4, RING)),
            dma((2, 4, RING)),
            dma((N_Z,)),
            dma((N_Z,)),
        ],
        compiler_params=pltpu.CompilerParams(
            collective_id=0, has_side_effects=True, vmem_limit_bytes=LIMIT * 2**20
        ),
        cost_estimate=pl.CostEstimate(
            flops=4 * slots * order**3, bytes_accessed=4 * 10**8, transcendentals=10**6
        ),
    )(owner, grads, left, right, mone, mtwo)


def scale_kernel(x, left, right, scale, out, ready, sem):
    me = lax.axis_index("dp")
    order = x.shape[1]
    last = START[BESIDE_LONG]

    def in_groups(kind, some):
        def one(i, carry):
            if kind in LONG:
                places = [START[kind] + j for j in range(START[kind + 1] - START[kind])]
                ks = [slot_of_group(me, kind, 3, j) for j in range(len(places))]
            else:
                places = [START[kind] + 6 * i + j for j in range(6)]
                ks = [slot_of_group(me, kind, j % 3, 2 * i + j // 3) for j in range(6)]
            some(places, [scale[pl.ds(k, 1), :] for k in ks])
            for pos, k in zip(places, ks):
                pltpu.make_async_copy(ready.at[pos], out.at[k], sem).start()
            return carry

        if kind in LONG:
            one(0, 0)
        else:
            lax.fori_loop(0, 2, one, 0)

    def store(pos, values, factor):
        ready[pos] = (values * jnp.concatenate([factor, factor], axis=1)).astype(jnp.bfloat16)

    def scaled(places, factors):
        for pos, factor in zip(places, factors):
            store(pos, x[pos].astype(jnp.float32), factor)

    def whole(places, factors):
        halves = [
            jnp.dot(
                left[:, pos - last].reshape(order, order), x[pos], preferred_element_type=jnp.float32
            ).astype(jnp.bfloat16)
            for pos in places
        ]
        preconds = [
            jnp.dot(half, right[pos - last], preferred_element_type=jnp.float32)
            for pos, half in zip(places, halves)
        ]
        for pos, precond, factor in zip(places, preconds, factors):
            mean = jnp.sum(precond * precond, axis=(0, 1), keepdims=True) / float(order * order) + 1e-06
            store(pos, precond, factor / jnp.sqrt(mean))

    for kind in (NEAR, NEAR_LONG, BESIDE, AWAY_LONG, AWAY):
        in_groups(kind, scaled)
    in_groups(BESIDE_LONG, whole)
    in_groups(BESIDE_CROSS, scaled)
    pltpu.make_async_copy(ready, out, sem).wait()


def apply_scale(x, left, right, scale):
    vmem, anywhere = pl.BlockSpec(memory_space=pltpu.VMEM), pl.BlockSpec(memory_space=pl.ANY)
    return pl.pallas_call(
        scale_kernel,
        out_shape=jax.ShapeDtypeStruct(x.shape, jnp.bfloat16),
        in_specs=[vmem] * 4,
        out_specs=anywhere,
        scratch_shapes=[
            pltpu.VMEM(x.shape, jnp.bfloat16),
            pltpu.SemaphoreType.DMA,
        ],
        compiler_params=pltpu.CompilerParams(vmem_limit_bytes=24 * 2**20),
    )(x, left, right, scale)


def per_device(grads, owner, left_root, right_root, first_moment, second_moment):
    x, left, right, scale = step(
        owner.reshape(1, -1), grads, left_root[0], right_root[0], first_moment[0], second_moment[0]
    )
    return apply_scale(x, left, right, scale)[None]


def solution(mesh):
    placed = (
        P("dp", None, None),
        P(),
        P("dp", None, "replica", None),
        P("dp", None, None, None),
        P("dp", None, "replica", None),
        P("dp", None, "replica", None),
    )
    return jax.shard_map(
        per_device, mesh=mesh, in_specs=placed, out_specs=P("dp", None, None, None), check_vma=False
    )
```
